32 devices in a mesh: dp: 8 (over z, x), seq: 2 (over y), mlp: 2 (over core).
Axes of the slice: x: 2, y: 2, z: 4, core: 2. Of those that a mesh axis runs over, the one named last changes fastest.
Arguments:
- patches: bfloat16 [1024, 48, 768], P('seq', 'dp'), may hold values from -6 to 6
- segments: int32 [1024, 48], P(None, 'dp'), may hold values from -1 to 992, as said below
- w_qkv: float32 [3, 768, 768], P(None, 'dp', 'mlp'), may hold values from -0.21875 to 0.21875
- w_out: float32 [768, 768], P('mlp', 'dp'), may hold values from -0.875 to 0.875
- w_up: float32 [768, 3072], P('dp', 'mlp'), may hold values from -0.21875 to 0.21875
- w_down: float32 [3072, 768], P('mlp', 'dp'), may hold values from -0.109375 to 0.109375
- ln_gain: float32 [2, 768], P(None, 'dp'), may hold values from 0.5 to 1.5
- ln_bias: float32 [2, 768], P(None, 'dp'), may hold values from -1.5 to 1.5
- head_gain: float32 [2, 12, 64], P(None, 'mlp', 'dp'), may hold values from 0.8 to 1.6
- cotangent: bfloat16 [1024, 48, 768], P('seq', 'dp', 'mlp'), may hold values from -6 to 6
Outputs:
- out: bfloat16 [1024, 48, 768], P('seq', 'dp', 'mlp')
- grad_patches: bfloat16 [1024, 48, 768], P('seq', 'dp')
- grad_w_qkv: float32 [3, 768, 768], P(None, 'dp', 'mlp')
- grad_w_out: float32 [768, 768], P('mlp', 'dp')
- grad_w_up: float32 [768, 3072], P('dp', 'mlp')
- grad_w_down: float32 [3072, 768], P('mlp', 'dp')
- grad_ln_gain: float32 [2, 768], P(None, 'dp')
- grad_ln_bias: float32 [2, 768], P(None, 'dp')
- grad_head_gain: float32 [2, 12, 64], P(None, 'mlp', 'dp')
The draws below stay inside these ranges and needn't reach their ends.
Inputs may be any that keep to these rules, and one draw needn't show every extreme that they name: `segments`: in each sequence (a column) every position carries the first position of its image; images are 16 to 1024 positions long, lengths multiples of 16, packed from position 0 and followed by -1 at the padding positions at the end. In each group of 6 consecutive sequences one sequence is a single image without padding.
All inputs are finite; a program needn't handle non-finite values.
Results may differ from the reference program's by a relative error of at most 0.02.
Values may be sent and summed in bfloat16 or wider, within the bound.
No kernel may reach another device: no remote copies, remote signals or barrier semaphores. Data moves between devices by JAX's collectives and lax.ppermute only.
A program may use at most 320 MiB of HBM per device.

```python
import math
import jax
import jax.numpy as jnp
from jax import lax

D = 768
HEADS = 12
HD = 64
FF = 3072
LEN = 1024
MIN_IMG = 16
SEQ_DEV = 6
SEQS = 48


def draw_segments(key, part):
    key = jax.random.fold_in(key, 7)
    key_starts, key_pads, key_whole = jax.random.split(key, 3)
    cell_count = LEN // MIN_IMG
    groups = SEQS // SEQ_DEV
    begins = jax.random.randint(key_starts, (SEQS, cell_count), 0, 4) == 0
    padding = jax.random.randint(key_pads, (SEQS,), 1, 4)
    whole_seq = jnp.arange(groups, dtype=jnp.int32) * SEQ_DEV + jax.random.randint(key_whole, (groups,), 0, SEQ_DEV)
    marked = (whole_seq[0] + 1) % SEQ_DEV
    cell_index = jnp.arange(cell_count, dtype=jnp.int32)
    is_whole = jnp.zeros((SEQS,), jnp.int32).at[whole_seq].set(1) == 1
    begins = jnp.where(is_whole[:, None], (cell_index == 0)[None, :], begins)
    padding = jnp.where(is_whole, 0, padding)
    is_marked = jnp.arange(SEQS, dtype=jnp.int32) == marked
    begins = jnp.where(is_marked[:, None], begins | (cell_index == cell_count - 2)[None, :], begins)
    padding = jnp.where(is_marked, 1, padding)
    begins = begins | (cell_index == 0)[None, :]
    first_cell = lax.cummax(jnp.where(begins, cell_index[None, :], 0), axis=1)
    labels = jnp.where(cell_index[None, :] < cell_count - padding[:, None], first_cell * MIN_IMG, -1)
    return jnp.transpose(jnp.repeat(labels, MIN_IMG, axis=1)).astype(jnp.int32)


def steps_of(rng, shape, cuts, least, high):
    loudness = 1.0
    for position, shards_of in cuts:
        heights = jax.random.uniform(jax.random.fold_in(jax.random.fold_in(rng, 6), position), (shards_of,), jnp.float32, least / len(cuts), high / len(cuts))
        loudness = loudness * jnp.repeat(jnp.exp(heights), shape[position] // shards_of).reshape((-1,) + (1,) * (len(shape) - 1 - position))
    return loudness


def bell_draw(own_key, dims, scale, most, pieces=(), kind=jnp.bfloat16):
    drawn = scale * jax.random.normal(own_key, dims, jnp.float32)
    if pieces:
        drawn = drawn * steps_of(own_key, dims, pieces, -0.22, 0.18)
    return jnp.clip(drawn, -most, most).astype(kind)


def setup_inputs(seed: int = 0) -> dict:
    splits = jax.random.split(jax.random.key(seed), 11)
    return {
        "patches": bell_draw(splits[0], (LEN, SEQS, D), 1.0, 6.0, ((0, 2), (1, 8))),
        "segments": draw_segments(jax.random.fold_in(splits[10], 71), 0),
        "w_qkv": bell_draw(splits[2], (3, D, D), D ** -0.5, 0.21875, ((1, 8), (2, 2)), jnp.float32),
        "w_out": bell_draw(splits[3], (D, D), (D // 16) ** -0.5, 0.875, ((0, 2), (1, 8)), jnp.float32),
        "w_up": bell_draw(splits[4], (D, FF), D ** -0.5, 0.21875, ((0, 8), (1, 2)), jnp.float32),
        "w_down": bell_draw(splits[5], (FF, D), FF ** -0.5, 0.109375, ((0, 2), (1, 8)), jnp.float32),
        "ln_gain": jnp.clip(0.5 + 1.0 * jax.random.uniform(splits[6], (2, D), jnp.float32) ** steps_of(splits[6], (2, D), ((1, 8),), -0.2, 0.2), 0.5, 1.5),
        "ln_bias": bell_draw(splits[7], (2, D), 0.3, 1.5, ((1, 8),), jnp.float32),
        "head_gain": jnp.clip(0.8 + 0.8 * jax.random.uniform(splits[8], (2, HEADS, HD), jnp.float32) ** steps_of(splits[8], (2, HEADS, HD), ((1, 2), (2, 8)), -0.2, 0.2), 0.8, 1.6),
        "cotangent": bell_draw(splits[9], (LEN, SEQS, D), 1.0, 6.0, ((0, 2), (1, 8), (2, 2))),
    }


norm_eps = 1e-06
masked_value = -1e+30
highest = lax.Precision.HIGHEST

@jax.custom_vjp
def low(v):
    return lax.optimization_barrier(v.astype(jnp.bfloat16)).astype(jnp.float32)

@jax.custom_vjp
def low_back(v):
    return v

def low_keep(v):
    return (low(v), None)

def low_pass(kept, grad):
    return (grad,)

def back_keep(v):
    return (v, None)

def back_low(kept, grad):
    return (low(grad),)
low.defvjp(low_keep, low_pass)
low_back.defvjp(back_keep, back_low)

def layer_norm(values, gain_row, bias_row):
    average = lax.optimization_barrier(jnp.mean(values, axis=-1, keepdims=True))
    centered = values - average
    variance = lax.optimization_barrier(jnp.mean(centered * centered, axis=-1, keepdims=True))
    return centered * lax.rsqrt(variance + norm_eps) * gain_row + bias_row

def head_norm(values, gain_rows):
    average = lax.optimization_barrier(jnp.mean(values, axis=-1, keepdims=True))
    centered = values - average
    variance = lax.optimization_barrier(jnp.mean(centered * centered, axis=-1, keepdims=True))
    return centered * lax.rsqrt(variance + norm_eps) * gain_rows

def forward(patch_group, w_qkv, w_out, w_up, w_down, ln_gain, ln_bias, head_gain, seg_group):
    w_qkv = low(w_qkv)
    w_out = low(w_out)
    w_up = low(w_up)
    w_down = low(w_down)
    ln_gain = low(ln_gain)
    ln_bias = low(ln_bias)
    head_gain = low(head_gain)
    group_size = patch_group.shape[1]
    normed = low(layer_norm(patch_group, ln_gain[0], ln_bias[0]))
    projected = low_back(jnp.einsum('lgd,cde->cgle', normed, w_qkv, precision=highest))
    shape_heads = (group_size, LEN, HEADS, HD)
    queries = low(head_norm(projected[0].reshape(shape_heads), head_gain[0]))
    key_heads = low(head_norm(projected[1].reshape(shape_heads), head_gain[1]))
    value_heads = low(projected[2].reshape(shape_heads))
    logits = low_back(jnp.einsum('gqhe,gkhe->ghqk', queries, key_heads, precision=highest) * HD ** (-0.5))
    seg_rows = jnp.transpose(seg_group)
    visible = (seg_rows[:, :, None] == seg_rows[:, None, :])[:, None]
    masked = jnp.where(visible, logits, masked_value)
    largest = lax.optimization_barrier(jnp.max(masked, axis=3, keepdims=True))
    powered = jnp.exp(masked - largest)
    attention = powered / lax.optimization_barrier(jnp.sum(powered, axis=3, keepdims=True))
    mixed = low(low_back(jnp.einsum('ghqk,gkhe->gqhe', low(attention), value_heads, precision=highest)))
    attended = low_back(jnp.einsum('gqf,fd->qgd', mixed.reshape(group_size, LEN, D), w_out, precision=highest))
    residual = patch_group + attended
    second_normalized = low(layer_norm(residual, ln_gain[1], ln_bias[1]))
    hidden_pre = low_back(jnp.einsum('lgd,df->lgf', second_normalized, w_up, precision=highest))
    mlp_activation = low(jax.nn.gelu(hidden_pre, approximate=True))
    branch = jnp.einsum('lgf,fd->lgd', mlp_activation, w_down, precision=highest)
    return jnp.where((seg_group >= 0)[:, :, None], residual + branch, 0.0)

def reference(patches, segments, w_qkv, w_out, w_up, w_down, ln_gain, ln_bias, head_gain, cotangent):
    group_size = 2
    group_count = SEQS // group_size
    patch_groups = jnp.transpose(patches.astype(jnp.float32).reshape(LEN, group_count, group_size, D), (1, 0, 2, 3))
    cot_groups = jnp.transpose(cotangent.astype(jnp.float32).reshape(LEN, group_count, group_size, D), (1, 0, 2, 3))
    seg_groups = jnp.transpose(segments.reshape(LEN, group_count, group_size), (1, 0, 2))
    params = (w_qkv.astype(jnp.float32), w_out.astype(jnp.float32), w_up.astype(jnp.float32), w_down.astype(jnp.float32), ln_gain.astype(jnp.float32), ln_bias.astype(jnp.float32), head_gain.astype(jnp.float32))

    def group_step(totals, inputs_group):
        patch_group, seg_group, cot_group = inputs_group

        def apply(patch_in, *weights):
            return forward(patch_in, *weights, seg_group)
        result, pullback = jax.vjp(apply, patch_group, *params)
        pulled = pullback(cot_group)
        totals = tuple((total + grad for total, grad in zip(totals, pulled[1:])))
        return (totals, (result.astype(jnp.bfloat16), pulled[0].astype(jnp.bfloat16)))
    zeros = tuple((jnp.zeros_like(param) for param in params))
    totals, (outs, grads_in) = lax.scan(group_step, zeros, (patch_groups, seg_groups, cot_groups))
    out = jnp.transpose(outs, (1, 0, 2, 3)).reshape(LEN, SEQS, D)
    grad_patches = jnp.transpose(grads_in, (1, 0, 2, 3)).reshape(LEN, SEQS, D)
    grad_scale = 1.0 / math.sqrt(SEQS * LEN)
    return (out, grad_patches, totals[0] * grad_scale, totals[1] * grad_scale, totals[2] * grad_scale, totals[3] * grad_scale, totals[4] * grad_scale, totals[5] * grad_scale, totals[6] * grad_scale)
```

```python
from functools import partial
import math

import jax
import jax.numpy as jnp
from jax import lax
from jax.experimental import pallas as pl
from jax.experimental.pallas import tpu as pltpu
from jax.sharding import PartitionSpec as P

norm_eps = 1e-06
masked_value = -1e30


def layer_norm(values, gain_row, bias_row):
    average = jnp.mean(values, axis=-1, keepdims=True)
    centered = values - average
    variance = jnp.mean(centered * centered, axis=-1, keepdims=True)
    return centered * lax.rsqrt(variance + norm_eps) * gain_row + bias_row


def head_norm(values, gain_rows):
    average = jnp.mean(values, axis=-1, keepdims=True)
    centered = values - average
    variance = jnp.mean(centered * centered, axis=-1, keepdims=True)
    return centered * lax.rsqrt(variance + norm_eps) * gain_rows


def on_device(
    patches, segments, w_qkv, w_out, w_up, w_down, ln_gain, ln_bias, head_gain, cotangent
):
    (
        query_weight,
        out_weight,
        up_projection_weight,
        down_projection_weight,
        norm_gains,
        norm_biases,
        head_gains,
    ) = (
        lax.all_gather(w_qkv.astype(jnp.bfloat16), "dp", axis=1, tiled=True),
        lax.all_gather(w_out.astype(jnp.bfloat16), "dp", axis=1, tiled=True),
        lax.all_gather(w_up.astype(jnp.bfloat16), "dp", axis=0, tiled=True),
        lax.all_gather(w_down.astype(jnp.bfloat16), "dp", axis=1, tiled=True),
        lax.all_gather(ln_gain.astype(jnp.bfloat16), "dp", axis=1, tiled=True),
        lax.all_gather(ln_bias.astype(jnp.bfloat16), "dp", axis=1, tiled=True),
        lax.all_gather(head_gain.astype(jnp.bfloat16), "dp", axis=2, tiled=True),
    )
    local_rows = patches.shape[0]
    seq_here = patches.shape[1]
    width = patches.shape[2]
    head_cols = query_weight.shape[2]
    heads_here = head_gains.shape[1]
    head_size = head_gains.shape[2]
    seq_len = local_rows * lax.axis_size("seq")
    feature_cols = width // lax.axis_size("mlp")
    score_scale = head_size ** (-0.5)
    gain_float = norm_gains.astype(jnp.float32)
    bias_float = norm_biases.astype(jnp.float32)
    head_float = head_gains.astype(jnp.float32)
    seg_here = lax.dynamic_slice_in_dim(segments, lax.axis_index("seq") * local_rows, local_rows, 0)
    valid_mask = (seg_here >= 0).astype(jnp.float32)[:, :, None]
    query_segs = jnp.transpose(seg_here)
    key_segs = jnp.transpose(segments)
    patch_float = patches.astype(jnp.float32)
    normed = layer_norm(patch_float, gain_float[0], bias_float[0]).astype(jnp.bfloat16)
    projected = jnp.einsum(
        "lsd,cde->csle", normed, query_weight, preferred_element_type=jnp.float32
    )
    shape_heads = (seq_here, local_rows, heads_here, head_size)
    query_raw = projected[0].reshape(shape_heads)
    key_raw = projected[1].reshape(shape_heads)
    query_low = head_norm(query_raw, head_float[0]).astype(jnp.bfloat16)
    key_low = head_norm(key_raw, head_float[1]).astype(jnp.bfloat16)
    value_low = projected[2].astype(jnp.bfloat16)
    key_pairs = jnp.concatenate(
        [key_low.reshape(seq_here, local_rows, head_cols), value_low], axis=2
    )

    def split_pairs(gathered):
        key_heads = gathered[:, :head_cols].reshape(gathered.shape[0], heads_here, head_size)
        value_heads = gathered[:, head_cols:].reshape(gathered.shape[0], heads_here, head_size)
        return (key_heads, value_heads)

    def attend_forward(unused, inputs_seq):
        query_seq, pairs_seq, query_rows, key_rows = inputs_seq
        gathered = lax.all_gather(pairs_seq, "seq", axis=0, tiled=True)
        key_heads, value_heads = split_pairs(gathered)
        logits = (
            jnp.einsum("qhe,khe->hqk", query_seq, key_heads, preferred_element_type=jnp.float32)
            * score_scale
        )
        visible = (query_rows[:, None] == key_rows[None, :])[None]
        masked = jnp.where(visible, logits, masked_value)
        largest = jnp.max(masked, axis=2, keepdims=True)
        powered = jnp.exp(masked - largest)
        totals = jnp.sum(powered, axis=2, keepdims=True)
        attention = (powered / totals).astype(jnp.bfloat16)
        mixed = jnp.einsum(
            "hqk,khe->qhe", attention, value_heads, preferred_element_type=jnp.float32
        )
        log_total = (largest + jnp.log(totals))[:, :, 0]
        return (unused, (mixed.astype(jnp.bfloat16).reshape(local_rows, head_cols), log_total))

    _, (attn_heads, log_totals) = lax.scan(
        attend_forward, 0, (query_low, key_pairs, query_segs, key_segs)
    )
    attn_part = jnp.einsum(
        "slf,fd->lsd", attn_heads, out_weight, preferred_element_type=jnp.float32
    )
    attn_mine = lax.psum_scatter(
        attn_part.astype(jnp.bfloat16), "mlp", scatter_dimension=2, tiled=True
    ).astype(jnp.float32)
    patch_mine = lax.dynamic_slice_in_dim(
        patch_float, lax.axis_index("mlp") * feature_cols, feature_cols, 2
    )
    resid_mine = patch_mine + attn_mine
    residual = lax.all_gather(resid_mine.astype(jnp.bfloat16), "mlp", axis=2, tiled=True).astype(
        resid_mine.dtype
    )
    second_normalized = layer_norm(residual, gain_float[1], bias_float[1]).astype(jnp.bfloat16)
    hidden_pre = jnp.einsum(
        "own,nr->owr", second_normalized, up_projection_weight, preferred_element_type=jnp.float32
    )
    mlp_activation = jax.nn.gelu(hidden_pre, approximate=True).astype(jnp.bfloat16)
    branch_part = jnp.einsum(
        "ruo,oe->rue", mlp_activation, down_projection_weight, preferred_element_type=jnp.float32
    )
    branch_mine = lax.psum_scatter(
        branch_part.astype(jnp.bfloat16), "mlp", scatter_dimension=2, tiled=True
    ).astype(jnp.float32)
    out = (valid_mask * (resid_mine + branch_mine)).astype(jnp.bfloat16)
    cot_full = lax.all_gather(cotangent, "mlp", axis=2, tiled=True)
    grad_out = valid_mask * cot_full.astype(jnp.float32)
    output_gradient_reduced = grad_out.astype(jnp.bfloat16)
    grad_down = jnp.einsum(
        "xgr,xge->re", mlp_activation, output_gradient_reduced, preferred_element_type=jnp.float32
    )
    grad_act = jnp.einsum(
        "mit,nt->min",
        output_gradient_reduced,
        down_projection_weight,
        preferred_element_type=jnp.float32,
    )
    _, gelu_pull = jax.vjp(partial(jax.nn.gelu, approximate=True), hidden_pre)
    hidden_gradient = gelu_pull(grad_act)[0].astype(jnp.bfloat16)
    up_projection_gradient = jnp.einsum(
        "gih,giv->hv", second_normalized, hidden_gradient, preferred_element_type=jnp.float32
    )
    grad_normed_two = lax.psum(
        jnp.einsum(
            "vwb,kb->vwk", hidden_gradient, up_projection_weight, preferred_element_type=jnp.float32
        ).astype(jnp.bfloat16),
        "mlp",
    ).astype(jnp.float32)
    _, second_pull = jax.vjp(layer_norm, residual, gain_float[1], bias_float[1])
    grad_resid_norm, grad_gain_two, grad_bias_two = second_pull(grad_normed_two)
    grad_resid = grad_out + grad_resid_norm
    grad_resid_low = grad_resid.astype(jnp.bfloat16)
    grad_out_weight = jnp.einsum(
        "slf,lsd->fd", attn_heads, grad_resid_low, preferred_element_type=jnp.float32
    )
    grad_mixed = jnp.einsum(
        "lsd,fd->slf", grad_resid_low, out_weight, preferred_element_type=jnp.float32
    ).astype(jnp.bfloat16)

    def attend_backward(unused, inputs_seq):
        query_seq, pairs_seq, query_rows, key_rows, log_total, grad_seq = inputs_seq
        gathered = lax.all_gather(pairs_seq, "seq", axis=0, tiled=True)
        key_heads, value_heads = split_pairs(gathered)
        logits = (
            jnp.einsum("qhe,khe->hqk", query_seq, key_heads, preferred_element_type=jnp.float32)
            * score_scale
        )
        visible = (query_rows[:, None] == key_rows[None, :])[None]
        attention = jnp.exp(jnp.where(visible, logits - log_total[:, :, None], masked_value))
        attention_low = attention.astype(jnp.bfloat16)
        grad_heads = grad_seq.reshape(local_rows, heads_here, head_size)
        grad_attention = jnp.einsum(
            "qhe,khe->hqk", grad_heads, value_heads, preferred_element_type=jnp.float32
        )
        inner = jnp.sum(grad_attention * attention, axis=2, keepdims=True)
        grad_logits = (attention * (grad_attention - inner)).astype(jnp.bfloat16)
        grad_query = (
            jnp.einsum("hqk,khe->qhe", grad_logits, key_heads, preferred_element_type=jnp.float32)
            * score_scale
        )
        grad_key = (
            jnp.einsum("hqk,qhe->khe", grad_logits, query_seq, preferred_element_type=jnp.float32)
            * score_scale
        )
        grad_value = jnp.einsum(
            "hqk,qhe->khe", attention_low, grad_heads, preferred_element_type=jnp.float32
        )
        grad_pairs = lax.psum_scatter(
            jnp.concatenate(
                [
                    grad_key.reshape(lax.axis_size("seq") * local_rows, head_cols),
                    grad_value.reshape(lax.axis_size("seq") * local_rows, head_cols),
                ],
                axis=1,
            ).astype(jnp.bfloat16),
            "seq",
            scatter_dimension=0,
            tiled=True,
        ).astype(jnp.float32)
        return (unused, (grad_query.reshape(local_rows, head_cols), grad_pairs))

    _, (grad_queries, grad_pairs_all) = lax.scan(
        attend_backward, 0, (query_low, key_pairs, query_segs, key_segs, log_totals, grad_mixed)
    )
    _, query_pull = jax.vjp(head_norm, query_raw, head_float[0])
    grad_query_raw, grad_query_gain = query_pull(grad_queries.reshape(shape_heads))
    _, key_pull = jax.vjp(head_norm, key_raw, head_float[1])
    grad_key_raw, grad_key_gain = key_pull(grad_pairs_all[:, :, :head_cols].reshape(shape_heads))
    grad_projected = jnp.stack(
        [
            grad_query_raw.reshape(seq_here, local_rows, head_cols),
            grad_key_raw.reshape(seq_here, local_rows, head_cols),
            grad_pairs_all[:, :, head_cols:],
        ],
        axis=0,
    ).astype(jnp.bfloat16)
    grad_query_weight = jnp.einsum(
        "lsd,csle->cde", normed, grad_projected, preferred_element_type=jnp.float32
    )
    grad_normed = lax.psum(
        jnp.einsum(
            "csle,cde->lsd", grad_projected, query_weight, preferred_element_type=jnp.float32
        ).astype(jnp.bfloat16),
        "mlp",
    ).astype(jnp.float32)
    _, first_pull = jax.vjp(layer_norm, patch_float, gain_float[0], bias_float[0])
    grad_patch_norm, grad_gain_one, grad_bias_one = first_pull(grad_normed)
    grad_patches = (grad_resid + grad_patch_norm).astype(jnp.bfloat16)
    grad_scale = 1.0 / math.sqrt(lax.axis_size("dp") * seq_here * seq_len)
    term_qkv = grad_query_weight * grad_scale
    term_out = grad_out_weight * grad_scale
    term_up = up_projection_gradient * grad_scale
    term_down = grad_down * grad_scale
    term_gain = jnp.stack([grad_gain_one, grad_gain_two]) * grad_scale
    term_bias = jnp.stack([grad_bias_one, grad_bias_two]) * grad_scale
    term_head = jnp.stack([grad_query_gain, grad_key_gain]) * grad_scale
    summed = (
        lax.psum(term_qkv.astype(jnp.bfloat16), "seq").astype(jnp.float32),
        lax.psum(term_out.astype(jnp.bfloat16), "seq").astype(jnp.float32),
        lax.psum(term_up.astype(jnp.bfloat16), "seq").astype(jnp.float32),
        lax.psum(term_down.astype(jnp.bfloat16), "seq").astype(jnp.float32),
        lax.psum(term_gain.astype(jnp.bfloat16), "seq").astype(jnp.float32),
        lax.psum(term_bias.astype(jnp.bfloat16), "seq").astype(jnp.float32),
        lax.psum(term_head.astype(jnp.bfloat16), "seq").astype(jnp.float32),
    )
    shards = (
        lax.psum_scatter(
            summed[0].astype(jnp.bfloat16), "dp", scatter_dimension=1, tiled=True
        ).astype(jnp.float32),
        lax.psum_scatter(
            summed[1].astype(jnp.bfloat16), "dp", scatter_dimension=1, tiled=True
        ).astype(jnp.float32),
        lax.psum_scatter(
            summed[2].astype(jnp.bfloat16), "dp", scatter_dimension=0, tiled=True
        ).astype(jnp.float32),
        lax.psum_scatter(
            summed[3].astype(jnp.bfloat16), "dp", scatter_dimension=1, tiled=True
        ).astype(jnp.float32),
        lax.psum_scatter(
            summed[4].astype(jnp.bfloat16), "dp", scatter_dimension=1, tiled=True
        ).astype(jnp.float32),
        lax.psum_scatter(
            summed[5].astype(jnp.bfloat16), "dp", scatter_dimension=1, tiled=True
        ).astype(jnp.float32),
        lax.psum_scatter(
            summed[6].astype(jnp.bfloat16), "dp", scatter_dimension=2, tiled=True
        ).astype(jnp.float32),
    )
    return (
        out,
        grad_patches,
        shards[0],
        shards[1],
        shards[2],
        shards[3],
        shards[4],
        shards[5],
        shards[6],
    )


low = jnp.bfloat16
wide = jnp.float32
log2e = math.log2(math.e)
mask_weight = 128.0
query_block = 256
windows = (384, 512, 1024)
vmem_bytes = 56 * 1024 * 1024


def dot(left, right, left_dim=1, right_dim=0):
    return lax.dot_general(
        left, right, (((left_dim,), (right_dim,)), ((), ())), preferred_element_type=wide
    )


def params(count):
    return pltpu.CompilerParams(
        dimension_semantics=("arbitrary",) * count, vmem_limit_bytes=vmem_bytes
    )


def split_dot(values, ones_matrix):
    top = values.astype(low)
    rest = (values - top.astype(wide)).astype(low)
    return dot(top, ones_matrix) + dot(rest, ones_matrix)


def qkv_kernel(
    x_ref, gain_ref, bias_ref, w_ref, hg_ref, mean_ref, q_ref, k_ref, v_ref, rq_ref, rk_ref, h_ref
):
    x = x_ref[0].astype(wide)
    centered = x - jnp.mean(x, axis=1, keepdims=True)
    variance = jnp.mean(centered * centered, axis=1, keepdims=True)
    h = (centered * lax.rsqrt(variance + norm_eps) * gain_ref[...] + bias_ref[...]).astype(low)
    h_ref[0] = h
    cols = q_ref.shape[2]
    means = mean_ref[...]
    for index, out_ref, rate_ref in ((0, q_ref, rq_ref), (1, k_ref, rk_ref)):
        raw = dot(h, w_ref[:, cols * index : cols * (index + 1)])
        inner = raw - split_dot(raw, means)
        rate = lax.rsqrt(dot((inner * inner).astype(low), means) + norm_eps)
        rate_ref[0] = rate
        out_ref[0] = (inner * rate * hg_ref[index : index + 1, :]).astype(low)
    v_ref[0] = dot(h, w_ref[:, 2 * cols :]).astype(low)


def attn_fwd_kernel(start_ref, kind_ref, q_ref, k_ref, v_ref, aug_ref, side_ref, o_ref, inv_ref):
    seq = pl.program_id(0)
    blocks = q_ref.shape[1] // query_block
    lane = lax.broadcasted_iota(jnp.int32, (query_block, 128), 1)

    def step(block, carry):
        row = pl.multiple_of(block * query_block, query_block)
        which = seq * blocks + block

        def body(size):
            begin = pl.multiple_of(start_ref[which], 16)
            q_pair = q_ref[0, pl.ds(row, query_block), :]
            q_side = aug_ref[0, pl.ds(row, query_block), :] * side_ref[...]
            keys = jnp.concatenate(
                [k_ref[0, pl.ds(begin, size), :], aug_ref[0, pl.ds(begin, size), :]], axis=1
            )
            values = jnp.concatenate(
                [v_ref[0, pl.ds(begin, size), :], jnp.ones((size, 128), low)], axis=1
            )
            mixed = []
            for head in range(2):
                mine = jnp.where(lane // 64 == head, q_pair, jnp.zeros_like(q_pair))
                scores = dot(jnp.concatenate([mine, q_side], axis=1), keys, 1, 1)
                mixed.append(dot(jnp.exp2(scores).astype(low), values))
            inverse = 1.0 / jnp.where(lane < 64, mixed[0][:, 128:], mixed[1][:, 128:])
            outcome = jnp.where(lane < 64, mixed[0][:, :128], mixed[1][:, :128]) * inverse
            o_ref[0, pl.ds(row, query_block), :] = outcome.astype(low)
            inv_ref[0, pl.ds(row, query_block), :] = inverse

        for index, size in enumerate(windows):
            pl.when(kind_ref[which] == index)(partial(body, size))
        return carry

    lax.fori_loop(0, blocks, step, 0)


def attn_bwd_kernel(
    start_ref,
    kind_ref,
    q_ref,
    k_ref,
    v_ref,
    go_ref,
    o_ref,
    inv_ref,
    rq_ref,
    rk_ref,
    aug_ref,
    side_ref,
    hg_ref,
    mean_ref,
    gq_ref,
    gk_ref,
    gv_ref,
    gain_ref,
    gq_acc,
    gk_acc,
    gv_acc,
):
    seq = pl.program_id(1)
    blocks = q_ref.shape[1] // query_block
    lane = lax.broadcasted_iota(jnp.int32, (query_block, 128), 1)
    gk_acc[...] = jnp.zeros_like(gk_acc)
    gv_acc[...] = jnp.zeros_like(gv_acc)

    def step(block, carry):
        row = pl.multiple_of(block * query_block, query_block)
        which = seq * blocks + block

        def body(size):
            begin = pl.multiple_of(start_ref[which], 16)
            rows = pl.ds(row, query_block)
            span = pl.ds(begin, size)
            q_pair = q_ref[0, rows, :]
            q_side = aug_ref[0, rows, :] * side_ref[...]
            k_pair = k_ref[0, span, :]
            k_side = aug_ref[0, span, :]
            keys = jnp.concatenate([k_pair, k_side], axis=1)
            values = jnp.concatenate([v_ref[0, span, :], k_side], axis=1)
            scaled = go_ref[0, rows, :].astype(wide) * inv_ref[0, rows, :]
            scaled_low = scaled.astype(low)
            product = scaled_low.astype(wide) * o_ref[0, rows, :].astype(wide)
            powers, grads, queries, pulls = [], [], [], []
            for head in range(2):
                mine = lane // 64 == head
                inner = jnp.sum(jnp.where(mine, product, 0.0), axis=1, keepdims=True)
                one = inner.astype(low)
                two = (inner - one.astype(wide)).astype(low)
                three = (inner - one.astype(wide) - two.astype(wide)).astype(low)
                go_side = jnp.where(
                    lane == 6,
                    -one,
                    jnp.where(lane == 7, -two, jnp.where(lane == 8, -three, jnp.zeros_like(q_pair))),
                )
                q_mine = jnp.where(mine, q_pair, jnp.zeros_like(q_pair))
                go_mine = jnp.where(mine, scaled_low, jnp.zeros_like(q_pair))
                power = jnp.exp2(dot(keys, jnp.concatenate([q_mine, q_side], axis=1), 1, 1))
                slope = dot(values, jnp.concatenate([go_mine, go_side], axis=1), 1, 1)
                grad = (power * slope).astype(low)
                powers.append(power.astype(low))
                grads.append(grad)
                queries.append(q_mine)
                pulls.append(go_mine)
            gv_acc[span, :] += dot(
                jnp.concatenate(powers, axis=1), jnp.concatenate(pulls, axis=0)
            )
            gk_acc[span, :] += dot(
                jnp.concatenate(grads, axis=1), jnp.concatenate(queries, axis=0)
            )
            gq_acc[rows, :] = jnp.where(
                lane < 64, dot(grads[0], k_pair, 0, 0), dot(grads[1], k_pair, 0, 0)
            )

        for index, size in enumerate(windows):
            pl.when(kind_ref[which] == index)(partial(body, size))
        return carry

    lax.fori_loop(0, blocks, step, 0)
    gv_ref[0] = gv_acc[...].astype(low)
    means = mean_ref[...]

    @pl.when(seq == 0)
    def _():
        gain_ref[...] = jnp.zeros_like(gain_ref)

    for index, acc, raw_ref, rate_ref, out_ref, scale, unscale in (
        (0, gq_acc, q_ref, rq_ref, gq_ref, 0.125, 8.0 / log2e),
        (1, gk_acc, k_ref, rk_ref, gk_ref, 1.0 / log2e, 1.0),
    ):
        gain = hg_ref[index : index + 1, :]
        grad = acc[...] * scale
        normed = raw_ref[0].astype(wide) * unscale
        weighted = grad * gain
        cross = grad * normed
        first = split_dot(weighted, means)
        second = split_dot(cross, means)
        out_ref[0] = (rate_ref[0] * (weighted - first - normed / gain * second)).astype(low)
        gain_ref[0, index : index + 1, :] += jnp.sum(cross, axis=0, keepdims=True) / gain


def attn_out_kernel(
    o_mine_ref, o_other_ref, w_mine_ref, w_other_ref, x_ref, gy_ref, gain_ref, bias_ref,
    x2_ref, h_ref, ht_ref, gyt_ref,
):
    x2 = (
        x_ref[...].astype(wide)
        + dot(o_mine_ref[...], w_mine_ref[...], 1, 1)
        + dot(o_other_ref[...], w_other_ref[...], 1, 1)
    )
    x2_ref[...] = x2
    centered = x2 - jnp.mean(x2, axis=1, keepdims=True)
    variance = jnp.mean(centered * centered, axis=1, keepdims=True)
    h = centered * lax.rsqrt(variance + norm_eps) * gain_ref[...] + bias_ref[...]
    h_ref[...] = h.astype(low)
    ht_ref[...] = jnp.transpose(h).astype(low)
    gyt_ref[...] = jnp.transpose(gy_ref[...].astype(wide)).astype(low)


def mlp_kernel(
    first, scale, h_ref, ht_ref, gy_ref, gyt_ref, up_mine_ref, up_other_ref, down_mine_ref,
    down_other_ref, *refs,
):
    if first:
        out_in_ref, *refs = refs
    else:
        out_in_ref, gh_in_ref, *refs = refs
    out_ref, gh_ref, *refs = refs
    grad_refs, accs = refs[:4], refs[4:]
    step = pl.program_id(0)
    h = h_ref[...]
    gy = gy_ref[...]
    out_sum = out_in_ref[...]
    gh_sum = None if first else gh_in_ref[...]
    root = math.sqrt(2.0 / math.pi)
    for up_ref, down_ref, up_acc, down_acc in (
        (up_mine_ref, down_mine_ref, accs[0], accs[1]),
        (up_other_ref, down_other_ref, accs[2], accs[3]),
    ):
        up = up_ref[...]
        down = down_ref[...]
        t = dot(h, up)
        square = t * t
        gate = 0.5 + 0.5 * jnp.tanh(t * (root + (root * 0.044715) * square))
        act = t * gate
        slope = gate + 2.0 * act * (1.0 - gate) * (root + (3.0 * root * 0.044715) * square)
        act_low = act.astype(low)
        grad = (dot(gy, down) * slope).astype(low)
        out_sum = out_sum + dot(act_low, down, 1, 1)
        back = dot(grad, up, 1, 1)
        gh_sum = back if gh_sum is None else gh_sum + back
        up_grad = dot(ht_ref[...], grad)
        down_grad = dot(gyt_ref[...], act_low)

        @pl.when(step == 0)
        def _():
            up_acc[...] = up_grad
            down_acc[...] = down_grad

        @pl.when(step > 0)
        def _():
            up_acc[...] += up_grad
            down_acc[...] += down_grad

    out_ref[...] = out_sum
    gh_ref[...] = gh_sum

    @pl.when(step == pl.num_programs(0) - 1)
    def _():
        for ref, acc in zip(grad_refs, accs):
            ref[...] = (acc[...] * scale).astype(low)


def second_norm_kernel(
    scale, x2_ref, gh_ref, gy_ref, y_ref, valid_ref, o_mine_ref, o_other_ref, w_mine_ref,
    w_other_ref, gain_ref, out_ref, gx_ref, go_mine_ref, go_other_ref, gw_mine_ref, gw_other_ref,
    sums_ref, acc_mine, acc_other,
):
    step = pl.program_id(0)
    x2 = x2_ref[...]
    gh = gh_ref[...]
    out_ref[...] = (y_ref[...] * valid_ref[...][:, :1]).astype(low)
    centered = x2 - jnp.mean(x2, axis=1, keepdims=True)
    rate = lax.rsqrt(jnp.mean(centered * centered, axis=1, keepdims=True) + norm_eps)
    normed = centered * rate
    weighted = gh * gain_ref[...]
    gx = gy_ref[...].astype(wide) + rate * (
        weighted
        - jnp.mean(weighted, axis=1, keepdims=True)
        - normed * jnp.mean(weighted * normed, axis=1, keepdims=True)
    )
    gx_ref[...] = gx
    gx_low = gx.astype(low)
    go_mine_ref[...] = dot(gx_low, w_mine_ref[...]).astype(low)
    go_other_ref[...] = dot(gx_low, w_other_ref[...]).astype(low)
    gx_turned = jnp.transpose(gx).astype(low)

    @pl.when(step == 0)
    def _():
        sums_ref[...] = jnp.zeros_like(sums_ref)
        acc_mine[...] = jnp.zeros_like(acc_mine)
        acc_other[...] = jnp.zeros_like(acc_other)

    sums_ref[0:1, :] += jnp.sum(gh * normed, axis=0, keepdims=True)
    sums_ref[1:2, :] += jnp.sum(gh, axis=0, keepdims=True)
    acc_mine[...] += dot(gx_turned, o_mine_ref[...])
    acc_other[...] += dot(gx_turned, o_other_ref[...])

    @pl.when(step == pl.num_programs(0) - 1)
    def _():
        gw_mine_ref[...] = (acc_mine[...] * scale).astype(low)
        gw_other_ref[...] = (acc_other[...] * scale).astype(low)


def first_norm_kernel(x_ref, a_ref, b_ref, gx2_ref, gain_ref, out_ref, sums_ref):
    x = x_ref[...].astype(wide)
    gh = a_ref[...].astype(wide) + b_ref[...].astype(wide)
    centered = x - jnp.mean(x, axis=1, keepdims=True)
    rate = lax.rsqrt(jnp.mean(centered * centered, axis=1, keepdims=True) + norm_eps)
    normed = centered * rate
    weighted = gh * gain_ref[...]
    out_ref[...] = (
        gx2_ref[...]
        + rate
        * (
            weighted
            - jnp.mean(weighted, axis=1, keepdims=True)
            - normed * jnp.mean(weighted * normed, axis=1, keepdims=True)
        )
    ).astype(low)

    @pl.when(pl.program_id(0) == 0)
    def _():
        sums_ref[...] = jnp.zeros_like(sums_ref)

    sums_ref[0:1, :] += jnp.sum(gh * normed, axis=0, keepdims=True)
    sums_ref[1:2, :] += jnp.sum(gh, axis=0, keepdims=True)


def shape_of(dims, kind=low):
    return jax.ShapeDtypeStruct(dims, kind)


def window_table(segs, blocks):
    length = segs.shape[1]
    pad_begin = jnp.sum((segs >= 0).astype(jnp.int32), axis=1, keepdims=True)
    begins = jnp.where(segs >= 0, segs, pad_begin)
    size = length // blocks
    firsts = begins[:, ::size]
    lasts = begins[:, size - 1 :: size]
    ends = jnp.sum((begins[:, None, :] <= lasts[:, :, None]).astype(jnp.int32), axis=2)
    reach = ends - firsts
    kinds = jnp.zeros_like(reach)
    spans = jnp.full_like(reach, windows[0])
    for index in range(1, len(windows)):
        larger = reach > windows[index - 1]
        kinds = jnp.where(larger, index, kinds)
        spans = jnp.where(larger, windows[index], spans)
    starts = jnp.minimum(firsts, length - spans)
    return starts.reshape(-1), kinds.reshape(-1)


def mask_columns(segs):
    codes = (segs + 16) // 16
    lane = jnp.arange(128, dtype=jnp.int32)
    bits = (codes[:, :, None] >> jnp.minimum(lane, 5)) & 1
    signs = (2 * bits - 1).astype(wide)
    return jnp.where(lane < 6, signs, jnp.where(lane < 9, 1.0, 0.0)).astype(low)


def swap(values, axis):
    return lax.ppermute(values, axis, [(0, 1), (1, 0)])


def in_order(index, mine, other, axis):
    return jnp.where(
        index == 0,
        jnp.concatenate([mine, other], axis=axis),
        jnp.concatenate([other, mine], axis=axis),
    )


def pick(values, index, axis):
    return lax.dynamic_index_in_dim(values, index, axis, keepdims=False)


def on_device_small(
    patches, segments, w_qkv, w_out, w_up, w_down, ln_gain, ln_bias, head_gain, cotangent
):
    half, seqs_all, width = patches.shape
    length = 2 * half
    seqs = seqs_all // 2
    cols = w_qkv.shape[2]
    part = half // 2
    y = lax.axis_index("seq")
    c = lax.axis_index("mlp")
    dp_size = lax.axis_size("dp")
    scale = 1.0 / math.sqrt(dp_size * seqs_all * length)
    own_rows = seqs * 2 * part
    hidden = w_up.shape[1]

    gather = partial(lax.all_gather, axis_name="dp", axis=0, tiled=True)
    w_in = gather(jnp.transpose(w_qkv.astype(low), (1, 0, 2)).reshape(-1, 3 * cols))
    w_o = gather(jnp.transpose(w_out.astype(low)))
    w_u = gather(w_up.astype(low))
    w_d = gather(jnp.transpose(w_down.astype(low)))
    small = gather(
        jnp.concatenate(
            [jnp.transpose(ln_gain), jnp.transpose(ln_bias)], axis=1
        ).astype(low)
    )
    gains = jnp.transpose(small[:, :2]).astype(wide)
    biases = jnp.transpose(small[:, 2:]).astype(wide)
    head_gains = lax.all_gather(head_gain.astype(low), "dp", axis=2, tiled=True)
    head_gains = head_gains.reshape(2, cols).astype(wide)
    w_o_other = swap(w_o, "mlp")
    w_u_other = swap(w_u, "mlp")
    w_d_other = swap(w_d, "mlp")

    turned = jnp.transpose(patches, (1, 0, 2)).reshape(2, seqs, 2, part, width)
    mine = pick(turned, y, 0)
    sent = pick(pick(turned, 1 - y, 0), c, 1)
    got = swap(sent, "seq")
    got_other = swap(got, "mlp")
    other = in_order(c, got[:, None], got_other[:, None], 1)
    x = in_order(y, mine[:, None], other[:, None], 1)
    segs = lax.dynamic_slice_in_dim(jnp.transpose(segments), y * seqs, seqs, 0)

    cot = cotangent.reshape(2, part, seqs_all, cols)
    cot_other = swap(pick(cot, 1 - c, 0), "mlp")
    cot = jnp.transpose(in_order(c, pick(cot, c, 0), cot_other, 2), (1, 0, 2))
    cot = cot.reshape(2, seqs, part, width)
    cot_got = swap(pick(cot, 1 - y, 0), "seq")
    cot = in_order(y, pick(cot, y, 0)[:, None], cot_got[:, None], 1)
    valid = pick((segs >= 0).reshape(seqs, 2, 2, part), c, 2)
    gy = jnp.where(valid[..., None], cot, jnp.zeros_like(cot)).reshape(own_rows, width)
    valid = jnp.broadcast_to(valid.reshape(own_rows, 1).astype(wide), (own_rows, 128))
    x_own = pick(x, c, 2).reshape(own_rows, width)
    x = x.reshape(seqs, length, width)

    starts, kinds = window_table(segs, length // query_block)
    aug = mask_columns(segs)
    lanes = jnp.arange(128)
    side = jnp.where(lanes < 6, mask_weight, jnp.where(lanes == 6, -6.0 * mask_weight, 0.0))
    side = side.astype(low)[None]
    index = jnp.arange(cols)
    means = jnp.where(index[:, None] // 64 == index[None] // 64, 1.0 / 64, 0.0).astype(low)
    block = 512
    row_spec = pl.BlockSpec((1, block, width), lambda i, j: (i, j, 0))
    col_spec = pl.BlockSpec((1, block, cols), lambda i, j: (i, j, 0))

    def whole(dims):
        return pl.BlockSpec(dims, lambda *ids: (0,) * len(dims))

    q, k, v, rate_q, rate_k, h1 = pl.pallas_call(
        qkv_kernel,
        grid=(seqs, length // block),
        in_specs=[
            row_spec,
            whole((1, width)),
            whole((1, width)),
            whole((width, 3 * cols)),
            whole((2, cols)),
            whole((cols, cols)),
        ],
        out_specs=[col_spec] * 5 + [row_spec],
        out_shape=[shape_of((seqs, length, cols))] * 3
        + [shape_of((seqs, length, cols), wide)] * 2
        + [shape_of((seqs, length, width))],
        compiler_params=params(2),
        name="qkv",
    )(
        x,
        gains[:1],
        biases[:1],
        w_in,
        head_gains * jnp.array([[log2e / 8.0], [1.0]], wide),
        means,
    )
    pairs = cols // 128

    def pair_spec(order):
        return pl.BlockSpec((1, length, 128), lambda *ids: order(*ids))

    by_seq = pair_spec(lambda s, p, *_: (s, 0, p))
    aug_seq = pair_spec(lambda s, p, *_: (s, 0, 0))
    o, inverse = pl.pallas_call(
        attn_fwd_kernel,
        grid_spec=pltpu.PrefetchScalarGridSpec(
            num_scalar_prefetch=2,
            grid=(seqs, pairs),
            in_specs=[by_seq, by_seq, by_seq, aug_seq, whole((1, 128))],
            out_specs=[by_seq, by_seq],
        ),
        out_shape=[shape_of((seqs, length, cols)), shape_of((seqs, length, cols), wide)],
        compiler_params=params(2),
        name="attn_fwd",
    )(starts, kinds, q, k, v, aug, side)

    o_parts = o.reshape(seqs, 2, 2, part, cols)
    o_mine = pick(o_parts, c, 2).reshape(own_rows, cols)
    o_other = swap(pick(o_parts, 1 - c, 2), "mlp").reshape(own_rows, cols)
    steps = own_rows // block
    rows_spec = pl.BlockSpec((block, width), lambda i: (i, 0))
    turned_spec = pl.BlockSpec((width, block), lambda i: (0, i))
    part_spec = pl.BlockSpec((block, cols), lambda i: (i, 0))
    x2, h2, h2t, gyt = pl.pallas_call(
        attn_out_kernel,
        grid=(steps,),
        in_specs=[
            part_spec,
            part_spec,
            whole((width, cols)),
            whole((width, cols)),
            rows_spec,
            rows_spec,
            whole((1, width)),
            whole((1, width)),
        ],
        out_specs=[rows_spec, rows_spec, turned_spec, turned_spec],
        out_shape=[
            shape_of((own_rows, width), wide),
            shape_of((own_rows, width)),
            shape_of((width, own_rows)),
            shape_of((width, own_rows)),
        ],
        compiler_params=params(1),
        name="attn_out",
    )(o_mine, o_other, w_o, w_o_other, x_own, gy, gains[1:], biases[1:])

    chunk = 512
    chunks = hidden // chunk
    total, gh = x2, None
    up_grads, down_grads = [], []
    for f in range(chunks):
        weight_spec = pl.BlockSpec((width, chunk), lambda i, f=f: (0, f))
        grad_spec = whole((width, chunk))
        first = f == 0
        carried = [total] if first else [total, gh]
        total, gh, *grads = pl.pallas_call(
            partial(mlp_kernel, first, scale),
            grid=(steps,),
            in_specs=[rows_spec, turned_spec, rows_spec, turned_spec]
            + [weight_spec] * 4
            + [rows_spec] * len(carried),
            out_specs=[rows_spec] * 2 + [grad_spec] * 4,
            out_shape=[shape_of((own_rows, width), wide)] * 2 + [shape_of((width, chunk))] * 4,
            scratch_shapes=[pltpu.VMEM((width, chunk), wide)] * 4,
            compiler_params=params(1),
            name="mlp",
        )(h2, h2t, gy, gyt, w_u, w_u_other, w_d, w_d_other, *carried)
        up_grads.append((grads[0], grads[2]))
        down_grads.append((grads[1], grads[3]))

    out_rows, gx2, go_mine, go_other, gwo_mine, gwo_other, second_sums = pl.pallas_call(
        partial(second_norm_kernel, scale),
        grid=(steps,),
        in_specs=[
            rows_spec,
            rows_spec,
            rows_spec,
            rows_spec,
            pl.BlockSpec((block, 128), lambda i: (i, 0)),
            part_spec,
            part_spec,
            whole((width, cols)),
            whole((width, cols)),
            whole((1, width)),
        ],
        out_specs=[
            rows_spec,
            rows_spec,
            part_spec,
            part_spec,
            whole((width, cols)),
            whole((width, cols)),
            whole((8, width)),
        ],
        out_shape=[
            shape_of((own_rows, width)),
            shape_of((own_rows, width), wide),
            shape_of((own_rows, cols)),
            shape_of((own_rows, cols)),
            shape_of((width, cols)),
            shape_of((width, cols)),
            shape_of((8, width), wide),
        ],
        scratch_shapes=[pltpu.VMEM((width, cols), wide)] * 2,
        compiler_params=params(1),
        name="second_norm",
    )(x2, gh, gy, total, valid, o_mine, o_other, w_o, w_o_other, gains[1:])

    go_shape = (seqs, 2, 1, part, cols)
    go = in_order(c, go_mine.reshape(go_shape), swap(go_other, "mlp").reshape(go_shape), 2)
    go = go.reshape(seqs, length, cols)
    by_pair = pair_spec(lambda p, s, *_: (s, 0, p))
    gain_spec = pl.BlockSpec((2, 128), lambda p, s, *_: (0, p))
    gq, gk, gv, gain_sums = pl.pallas_call(
        attn_bwd_kernel,
        grid_spec=pltpu.PrefetchScalarGridSpec(
            num_scalar_prefetch=2,
            grid=(pairs, seqs),
            in_specs=[by_pair] * 8
            + [
                pair_spec(lambda p, s, *_: (s, 0, 0)),
                whole((1, 128)),
                gain_spec,
                whole((128, 128)),
            ],
            out_specs=[by_pair] * 3 + [pl.BlockSpec((1, 8, 128), lambda p, s, *_: (p, 0, 0))],
            scratch_shapes=[pltpu.VMEM((length, 128), wide)] * 3,
        ),
        out_shape=[shape_of((seqs, length, cols))] * 3 + [shape_of((pairs, 8, 128), wide)],
        compiler_params=params(2),
        name="attn_bwd",
    )(starts, kinds, q, k, v, go, o, inverse, rate_q, rate_k, aug, side, head_gains, means[:128, :128])

    gw_in = jnp.concatenate(
        [
            jnp.einsum("sld,slf->df", h1, grad, preferred_element_type=wide)
            for grad in (gq, gk, gv)
        ],
        axis=1,
    )
    gw_in = (gw_in * scale).astype(low)
    gh1 = sum(
        jnp.einsum(
            "slf,df->sld",
            grad,
            w_in[:, cols * i : cols * (i + 1)],
            preferred_element_type=wide,
        )
        for i, grad in enumerate((gq, gk, gv))
    ).astype(low)
    gh1 = gh1.reshape(seqs, 2, 2, part, width)
    gh1_got = swap(pick(gh1, 1 - c, 2), "mlp").reshape(own_rows, width)
    gh1_own = pick(gh1, c, 2).reshape(own_rows, width)
    grad_rows, first_sums = pl.pallas_call(
        first_norm_kernel,
        grid=(steps,),
        in_specs=[rows_spec] * 4 + [whole((1, width))],
        out_specs=[rows_spec, whole((8, width))],
        out_shape=[shape_of((own_rows, width)), shape_of((8, width), wide)],
        compiler_params=params(1),
        name="first_norm",
    )(x_own, gh1_own, gh1_got, gx2, gains[:1])

    def all_seqs(rows):
        rows = rows.reshape(seqs, 2, part, width)
        return in_order(y, pick(rows, y, 1), swap(pick(rows, 1 - y, 1), "seq"), 0)

    out_six = all_seqs(out_rows).reshape(seqs_all, part, 2, cols)
    out_got = swap(pick(out_six, 1 - c, 2), "mlp")
    out = in_order(c, pick(out_six, c, 2), out_got, 1)
    out = jnp.transpose(out, (1, 0, 2))
    grad_six = all_seqs(grad_rows)
    grad_patches = jnp.transpose(in_order(c, grad_six, swap(grad_six, "mlp"), 1), (1, 0, 2))

    def over_cores(mine, other):
        return (mine.astype(wide) + swap(other, "mlp").astype(wide)).astype(low)

    gw_up = jnp.concatenate([over_cores(*pair) for pair in up_grads], axis=1)
    gw_down = jnp.concatenate([over_cores(*pair) for pair in down_grads], axis=1)
    gw_out = over_cores(gwo_mine, gwo_other)

    def shard(grad):
        mine = lax.psum_scatter(grad, "dp", scatter_dimension=0, tiled=True)
        return mine.astype(wide) + swap(mine, "seq").astype(wide)

    gw_in, gw_out, gw_up, gw_down = (shard(g) for g in (gw_in, gw_out, gw_up, gw_down))
    d = lax.axis_index("dp")
    norm_sums = lax.psum(
        jnp.concatenate([first_sums[:2], second_sums[:2]]) * scale, ("dp", "seq", "mlp")
    )
    norm_sums = lax.dynamic_slice_in_dim(norm_sums, d * (width // dp_size), width // dp_size, 1)
    head_sums = lax.psum(jnp.transpose(gain_sums[:, :2], (1, 0, 2)) * scale, ("dp", "seq"))
    head_sums = head_sums.reshape(2, cols // 64, 64)
    head_sums = lax.dynamic_slice_in_dim(head_sums, d * (64 // dp_size), 64 // dp_size, 2)
    return (
        out,
        grad_patches,
        jnp.transpose(gw_in.reshape(-1, 3, cols), (1, 0, 2)),
        jnp.transpose(gw_out),
        gw_up,
        jnp.transpose(gw_down),
        norm_sums[0::2],
        norm_sums[1::2],
        head_sums,
    )


def solution(mesh):
    shape = dict(mesh.shape)
    small = shape["seq"] == 2 and shape["mlp"] == 2 and shape["dp"] == 8
    return jax.shard_map(
        on_device_small if small else on_device,
        mesh=mesh,
        in_specs=(
            P("seq", "dp", None),
            P(None, "dp"),
            P(None, "dp", "mlp"),
            P("mlp", "dp"),
            P("dp", "mlp"),
            P("mlp", "dp"),
            P(None, "dp"),
            P(None, "dp"),
            P(None, "mlp", "dp"),
            P("seq", "dp", "mlp"),
        ),
        out_specs=(
            P("seq", "dp", "mlp"),
            P("seq", "dp", None),
            P(None, "dp", "mlp"),
            P("mlp", "dp"),
            P("dp", "mlp"),
            P("mlp", "dp"),
            P(None, "dp"),
            P(None, "dp"),
            P(None, "mlp", "dp"),
        ),
        check_vma=False,
    )
```

```python
from functools import partial
import math

import jax
import jax.numpy as jnp
from jax import lax
from jax.experimental import pallas as pl
from jax.experimental.pallas import tpu as pltpu
from jax.sharding import PartitionSpec as P

norm_eps = 1e-06
masked_value = -1e30


def layer_norm(values, gain_row, bias_row):
    average = jnp.mean(values, axis=-1, keepdims=True)
    centered = values - average
    variance = jnp.mean(centered * centered, axis=-1, keepdims=True)
    return centered * lax.rsqrt(variance + norm_eps) * gain_row + bias_row


def head_norm(values, gain_rows):
    average = jnp.mean(values, axis=-1, keepdims=True)
    centered = values - average
    variance = jnp.mean(centered * centered, axis=-1, keepdims=True)
    return centered * lax.rsqrt(variance + norm_eps) * gain_rows


def on_device(
    patches, segments, w_qkv, w_out, w_up, w_down, ln_gain, ln_bias, head_gain, cotangent
):
    (
        query_weight,
        out_weight,
        up_projection_weight,
        down_projection_weight,
        norm_gains,
        norm_biases,
        head_gains,
    ) = (
        lax.all_gather(w_qkv.astype(jnp.bfloat16), "dp", axis=1, tiled=True),
        lax.all_gather(w_out.astype(jnp.bfloat16), "dp", axis=1, tiled=True),
        lax.all_gather(w_up.astype(jnp.bfloat16), "dp", axis=0, tiled=True),
        lax.all_gather(w_down.astype(jnp.bfloat16), "dp", axis=1, tiled=True),
        lax.all_gather(ln_gain.astype(jnp.bfloat16), "dp", axis=1, tiled=True),
        lax.all_gather(ln_bias.astype(jnp.bfloat16), "dp", axis=1, tiled=True),
        lax.all_gather(head_gain.astype(jnp.bfloat16), "dp", axis=2, tiled=True),
    )
    local_rows = patches.shape[0]
    seq_here = patches.shape[1]
    width = patches.shape[2]
    head_cols = query_weight.shape[2]
    heads_here = head_gains.shape[1]
    head_size = head_gains.shape[2]
    seq_len = local_rows * lax.axis_size("seq")
    feature_cols = width // lax.axis_size("mlp")
    score_scale = head_size ** (-0.5)
    gain_float = norm_gains.astype(jnp.float32)
    bias_float = norm_biases.astype(jnp.float32)
    head_float = head_gains.astype(jnp.float32)
    seg_here = lax.dynamic_slice_in_dim(segments, lax.axis_index("seq") * local_rows, local_rows, 0)
    valid_mask = (seg_here >= 0).astype(jnp.float32)[:, :, None]
    query_segs = jnp.transpose(seg_here)
    key_segs = jnp.transpose(segments)
    patch_float = patches.astype(jnp.float32)
    normed = layer_norm(patch_float, gain_float[0], bias_float[0]).astype(jnp.bfloat16)
    projected = jnp.einsum(
        "lsd,cde->csle", normed, query_weight, preferred_element_type=jnp.float32
    )
    shape_heads = (seq_here, local_rows, heads_here, head_size)
    query_raw = projected[0].reshape(shape_heads)
    key_raw = projected[1].reshape(shape_heads)
    query_low = head_norm(query_raw, head_float[0]).astype(jnp.bfloat16)
    key_low = head_norm(key_raw, head_float[1]).astype(jnp.bfloat16)
    value_low = projected[2].astype(jnp.bfloat16)
    key_pairs = jnp.concatenate(
        [key_low.reshape(seq_here, local_rows, head_cols), value_low], axis=2
    )

    def split_pairs(gathered):
        key_heads = gathered[:, :head_cols].reshape(gathered.shape[0], heads_here, head_size)
        value_heads = gathered[:, head_cols:].reshape(gathered.shape[0], heads_here, head_size)
        return (key_heads, value_heads)

    def attend_forward(unused, inputs_seq):
        query_seq, pairs_seq, query_rows, key_rows = inputs_seq
        gathered = lax.all_gather(pairs_seq, "seq", axis=0, tiled=True)
        key_heads, value_heads = split_pairs(gathered)
        logits = (
            jnp.einsum("qhe,khe->hqk", query_seq, key_heads, preferred_element_type=jnp.float32)
            * score_scale
        )
        visible = (query_rows[:, None] == key_rows[None, :])[None]
        masked = jnp.where(visible, logits, masked_value)
        largest = jnp.max(masked, axis=2, keepdims=True)
        powered = jnp.exp(masked - largest)
        totals = jnp.sum(powered, axis=2, keepdims=True)
        attention = (powered / totals).astype(jnp.bfloat16)
        mixed = jnp.einsum(
            "hqk,khe->qhe", attention, value_heads, preferred_element_type=jnp.float32
        )
        log_total = (largest + jnp.log(totals))[:, :, 0]
        return (unused, (mixed.astype(jnp.bfloat16).reshape(local_rows, head_cols), log_total))

    _, (attn_heads, log_totals) = lax.scan(
        attend_forward, 0, (query_low, key_pairs, query_segs, key_segs)
    )
    attn_part = jnp.einsum(
        "slf,fd->lsd", attn_heads, out_weight, preferred_element_type=jnp.float32
    )
    attn_mine = lax.psum_scatter(
        attn_part.astype(jnp.bfloat16), "mlp", scatter_dimension=2, tiled=True
    ).astype(jnp.float32)
    patch_mine = lax.dynamic_slice_in_dim(
        patch_float, lax.axis_index("mlp") * feature_cols, feature_cols, 2
    )
    resid_mine = patch_mine + attn_mine
    residual = lax.all_gather(resid_mine.astype(jnp.bfloat16), "mlp", axis=2, tiled=True).astype(
        resid_mine.dtype
    )
    second_normalized = layer_norm(residual, gain_float[1], bias_float[1]).astype(jnp.bfloat16)
    hidden_pre = jnp.einsum(
        "own,nr->owr", second_normalized, up_projection_weight, preferred_element_type=jnp.float32
    )
    mlp_activation = jax.nn.gelu(hidden_pre, approximate=True).astype(jnp.bfloat16)
    branch_part = jnp.einsum(
        "ruo,oe->rue", mlp_activation, down_projection_weight, preferred_element_type=jnp.float32
    )
    branch_mine = lax.psum_scatter(
        branch_part.astype(jnp.bfloat16), "mlp", scatter_dimension=2, tiled=True
    ).astype(jnp.float32)
    out = (valid_mask * (resid_mine + branch_mine)).astype(jnp.bfloat16)
    cot_full = lax.all_gather(cotangent, "mlp", axis=2, tiled=True)
    grad_out = valid_mask * cot_full.astype(jnp.float32)
    output_gradient_reduced = grad_out.astype(jnp.bfloat16)
    grad_down = jnp.einsum(
        "xgr,xge->re", mlp_activation, output_gradient_reduced, preferred_element_type=jnp.float32
    )
    grad_act = jnp.einsum(
        "mit,nt->min",
        output_gradient_reduced,
        down_projection_weight,
        preferred_element_type=jnp.float32,
    )
    _, gelu_pull = jax.vjp(partial(jax.nn.gelu, approximate=True), hidden_pre)
    hidden_gradient = gelu_pull(grad_act)[0].astype(jnp.bfloat16)
    up_projection_gradient = jnp.einsum(
        "gih,giv->hv", second_normalized, hidden_gradient, preferred_element_type=jnp.float32
    )
    grad_normed_two = lax.psum(
        jnp.einsum(
            "vwb,kb->vwk", hidden_gradient, up_projection_weight, preferred_element_type=jnp.float32
        ).astype(jnp.bfloat16),
        "mlp",
    ).astype(jnp.float32)
    _, second_pull = jax.vjp(layer_norm, residual, gain_float[1], bias_float[1])
    grad_resid_norm, grad_gain_two, grad_bias_two = second_pull(grad_normed_two)
    grad_resid = grad_out + grad_resid_norm
    grad_resid_low = grad_resid.astype(jnp.bfloat16)
    grad_out_weight = jnp.einsum(
        "slf,lsd->fd", attn_heads, grad_resid_low, preferred_element_type=jnp.float32
    )
    grad_mixed = jnp.einsum(
        "lsd,fd->slf", grad_resid_low, out_weight, preferred_element_type=jnp.float32
    ).astype(jnp.bfloat16)

    def attend_backward(unused, inputs_seq):
        query_seq, pairs_seq, query_rows, key_rows, log_total, grad_seq = inputs_seq
        gathered = lax.all_gather(pairs_seq, "seq", axis=0, tiled=True)
        key_heads, value_heads = split_pairs(gathered)
        logits = (
            jnp.einsum("qhe,khe->hqk", query_seq, key_heads, preferred_element_type=jnp.float32)
            * score_scale
        )
        visible = (query_rows[:, None] == key_rows[None, :])[None]
        attention = jnp.exp(jnp.where(visible, logits - log_total[:, :, None], masked_value))
        attention_low = attention.astype(jnp.bfloat16)
        grad_heads = grad_seq.reshape(local_rows, heads_here, head_size)
        grad_attention = jnp.einsum(
            "qhe,khe->hqk", grad_heads, value_heads, preferred_element_type=jnp.float32
        )
        inner = jnp.sum(grad_attention * attention, axis=2, keepdims=True)
        grad_logits = (attention * (grad_attention - inner)).astype(jnp.bfloat16)
        grad_query = (
            jnp.einsum("hqk,khe->qhe", grad_logits, key_heads, preferred_element_type=jnp.float32)
            * score_scale
        )
        grad_key = (
            jnp.einsum("hqk,qhe->khe", grad_logits, query_seq, preferred_element_type=jnp.float32)
            * score_scale
        )
        grad_value = jnp.einsum(
            "hqk,qhe->khe", attention_low, grad_heads, preferred_element_type=jnp.float32
        )
        grad_pairs = lax.psum_scatter(
            jnp.concatenate(
                [
                    grad_key.reshape(lax.axis_size("seq") * local_rows, head_cols),
                    grad_value.reshape(lax.axis_size("seq") * local_rows, head_cols),
                ],
                axis=1,
            ).astype(jnp.bfloat16),
            "seq",
            scatter_dimension=0,
            tiled=True,
        ).astype(jnp.float32)
        return (unused, (grad_query.reshape(local_rows, head_cols), grad_pairs))

    _, (grad_queries, grad_pairs_all) = lax.scan(
        attend_backward, 0, (query_low, key_pairs, query_segs, key_segs, log_totals, grad_mixed)
    )
    _, query_pull = jax.vjp(head_norm, query_raw, head_float[0])
    grad_query_raw, grad_query_gain = query_pull(grad_queries.reshape(shape_heads))
    _, key_pull = jax.vjp(head_norm, key_raw, head_float[1])
    grad_key_raw, grad_key_gain = key_pull(grad_pairs_all[:, :, :head_cols].reshape(shape_heads))
    grad_projected = jnp.stack(
        [
            grad_query_raw.reshape(seq_here, local_rows, head_cols),
            grad_key_raw.reshape(seq_here, local_rows, head_cols),
            grad_pairs_all[:, :, head_cols:],
        ],
        axis=0,
    ).astype(jnp.bfloat16)
    grad_query_weight = jnp.einsum(
        "lsd,csle->cde", normed, grad_projected, preferred_element_type=jnp.float32
    )
    grad_normed = lax.psum(
        jnp.einsum(
            "csle,cde->lsd", grad_projected, query_weight, preferred_element_type=jnp.float32
        ).astype(jnp.bfloat16),
        "mlp",
    ).astype(jnp.float32)
    _, first_pull = jax.vjp(layer_norm, patch_float, gain_float[0], bias_float[0])
    grad_patch_norm, grad_gain_one, grad_bias_one = first_pull(grad_normed)
    grad_patches = (grad_resid + grad_patch_norm).astype(jnp.bfloat16)
    grad_scale = 1.0 / math.sqrt(lax.axis_size("dp") * seq_here * seq_len)
    term_qkv = grad_query_weight * grad_scale
    term_out = grad_out_weight * grad_scale
    term_up = up_projection_gradient * grad_scale
    term_down = grad_down * grad_scale
    term_gain = jnp.stack([grad_gain_one, grad_gain_two]) * grad_scale
    term_bias = jnp.stack([grad_bias_one, grad_bias_two]) * grad_scale
    term_head = jnp.stack([grad_query_gain, grad_key_gain]) * grad_scale
    summed = (
        lax.psum(term_qkv.astype(jnp.bfloat16), "seq").astype(jnp.float32),
        lax.psum(term_out.astype(jnp.bfloat16), "seq").astype(jnp.float32),
        lax.psum(term_up.astype(jnp.bfloat16), "seq").astype(jnp.float32),
        lax.psum(term_down.astype(jnp.bfloat16), "seq").astype(jnp.float32),
        lax.psum(term_gain.astype(jnp.bfloat16), "seq").astype(jnp.float32),
        lax.psum(term_bias.astype(jnp.bfloat16), "seq").astype(jnp.float32),
        lax.psum(term_head.astype(jnp.bfloat16), "seq").astype(jnp.float32),
    )
    shards = (
        lax.psum_scatter(
            summed[0].astype(jnp.bfloat16), "dp", scatter_dimension=1, tiled=True
        ).astype(jnp.float32),
        lax.psum_scatter(
            summed[1].astype(jnp.bfloat16), "dp", scatter_dimension=1, tiled=True
        ).astype(jnp.float32),
        lax.psum_scatter(
            summed[2].astype(jnp.bfloat16), "dp", scatter_dimension=0, tiled=True
        ).astype(jnp.float32),
        lax.psum_scatter(
            summed[3].astype(jnp.bfloat16), "dp", scatter_dimension=1, tiled=True
        ).astype(jnp.float32),
        lax.psum_scatter(
            summed[4].astype(jnp.bfloat16), "dp", scatter_dimension=1, tiled=True
        ).astype(jnp.float32),
        lax.psum_scatter(
            summed[5].astype(jnp.bfloat16), "dp", scatter_dimension=1, tiled=True
        ).astype(jnp.float32),
        lax.psum_scatter(
            summed[6].astype(jnp.bfloat16), "dp", scatter_dimension=2, tiled=True
        ).astype(jnp.float32),
    )
    return (
        out,
        grad_patches,
        shards[0],
        shards[1],
        shards[2],
        shards[3],
        shards[4],
        shards[5],
        shards[6],
    )


low = jnp.bfloat16
wide = jnp.float32
log2e = math.log2(math.e)
mask_weight = 128.0
query_block = 256
windows = (384, 512, 1024)
vmem_bytes = 56 * 1024 * 1024
micros = {
    "qkv": 23,
    "attn_fwd": 29,
    "attn_out": 13,
    "mlp": 26,
    "second_norm": 18,
    "attn_bwd": 53,
    "gw_in": 11,
    "gh1": 12,
    "first_norm": 10,
}


def dot(left, right, left_dim=1, right_dim=0):
    return lax.dot_general(
        left, right, (((left_dim,), (right_dim,)), ((), ())), preferred_element_type=wide
    )


def params(count):
    return pltpu.CompilerParams(
        dimension_semantics=("arbitrary",) * count, vmem_limit_bytes=vmem_bytes
    )


def split_dot(values, ones_matrix):
    top = values.astype(low)
    rest = (values - top.astype(wide)).astype(low)
    return dot(top, ones_matrix) + dot(rest, ones_matrix)


def load_pieces(info_ref, sets, scratch, sems):
    copies = []
    rows = scratch.shape[0] // 8
    for number, (pieces, first, count, target) in enumerate(sets):
        for index in range(8):
            if len(pieces) == 8:
                piece = pieces[index]
            else:
                piece = pieces[index % 2].at[index // 2]
            place = pl.multiple_of(info_ref[2 + index] * rows, rows)
            copies.append(
                pltpu.make_async_copy(
                    piece.at[pl.ds(0, rows), pl.ds(first, count)],
                    scratch.at[pl.ds(place, rows), pl.ds(target, count)],
                    sems.at[number, index],
                )
            )
    return copies


def load_shards(pairs_of, scratch, sems):
    copies = []
    rows = scratch.shape[0] // 8
    for number, (source, owner, first, count, target) in enumerate(pairs_of):
        for index in range(8):
            copies.append(
                pltpu.make_async_copy(
                    source.at[2 * index + owner, :, pl.ds(first, count)],
                    scratch.at[pl.ds(index * rows, rows), pl.ds(target, count)],
                    sems.at[number, index],
                )
            )
    return copies


def run_all(copies):
    for copy in copies:
        copy.start()
    for copy in copies:
        copy.wait()


def qkv_kernel(info_ref, mine_ref, got_ref, far_ref, gain_ref, bias_ref, hg_ref, mean_ref, *refs):
    pieces, refs = refs[:8], refs[8:]
    p_ref, rate_ref, ht_ref, w_ref, sems = refs
    sub = pl.program_id(1)

    @pl.when((pl.program_id(0) == 0) & (sub == 0))
    def _():
        run_all(load_pieces(info_ref, [(pieces, 0, w_ref.shape[1], 0)], w_ref, sems))

    x = jnp.where(
        sub // 2 == info_ref[0],
        mine_ref[0],
        jnp.where(sub % 2 == info_ref[1], got_ref[0], far_ref[0]),
    ).astype(wide)
    centered = x - jnp.mean(x, axis=1, keepdims=True)
    variance = jnp.mean(centered * centered, axis=1, keepdims=True)
    h_wide = centered * lax.rsqrt(variance + norm_eps) * gain_ref[...] + bias_ref[...]
    h = h_wide.astype(low)
    ht_ref[...] = jnp.transpose(h_wide).astype(low)
    means = mean_ref[...]
    projected = dot(h, w_ref[...])
    for at in range(0, projected.shape[1], 128):
        raw = projected[:, at : at + 128]
        if at % 384 == 256:
            p_ref[0, :, at : at + 128] = raw.astype(low)
            continue
        inner = raw - split_dot(raw, means)
        rate = lax.rsqrt(dot((inner * inner).astype(low), means) + norm_eps)
        to = at // 384 * 256 + at % 384
        rate_ref[0, :, to : to + 128] = rate
        p_ref[0, :, at : at + 128] = (inner * rate * hg_ref[:, to : to + 128]).astype(low)


def attn_fwd_kernel(
    info_ref, start_ref, kind_ref, p_ref, aug_ref, side_ref, mine_ref, send_ref, inv_ref
):
    seq = pl.program_id(0)
    blocks = p_ref.shape[1] // query_block
    lane = lax.broadcasted_iota(jnp.int32, (query_block, 128), 1)

    def step(block, carry):
        row = pl.multiple_of(block * query_block, query_block)
        which = seq * blocks + block

        def body(size):
            begin = pl.multiple_of(start_ref[which], 16)
            q_pair = p_ref[0, pl.ds(row, query_block), 0:128]
            q_side = aug_ref[0, pl.ds(row, query_block), :] * side_ref[...]
            keys = jnp.concatenate(
                [p_ref[0, pl.ds(begin, size), 128:256], aug_ref[0, pl.ds(begin, size), :]], axis=1
            )
            values = jnp.concatenate(
                [p_ref[0, pl.ds(begin, size), 256:384], jnp.ones((size, 128), low)], axis=1
            )
            mixed = []
            for head in range(2):
                mine = jnp.where(lane // 64 == head, q_pair, jnp.zeros_like(q_pair))
                scores = dot(jnp.concatenate([mine, q_side], axis=1), keys, 1, 1)
                mixed.append(dot(jnp.exp2(scores).astype(low), values))
            inverse = 1.0 / jnp.where(lane < 64, mixed[0][:, 128:], mixed[1][:, 128:])
            outcome = jnp.where(lane < 64, mixed[0][:, :128], mixed[1][:, :128]) * inverse

            @pl.when(block % 2 == info_ref[1])
            def _():
                mine_ref[0, block // 2] = outcome.astype(low)

            @pl.when(block % 2 != info_ref[1])
            def _():
                send_ref[0, block // 2] = outcome.astype(low)

            inv_ref[0, pl.ds(row, query_block), :] = inverse

        for index, size in enumerate(windows):
            pl.when(kind_ref[which] == index)(partial(body, size))
        return carry

    lax.fori_loop(0, blocks, step, 0)


def attn_bwd_kernel(
    base,
    info_ref,
    start_ref,
    kind_ref,
    p_ref,
    go_mine_ref,
    go_got_ref,
    o_mine_ref,
    o_send_ref,
    inv_ref,
    rate_ref,
    aug_ref,
    side_ref,
    hg_ref,
    mean_ref,
    g_ref,
    gain_ref,
    gq_acc,
    gk_acc,
    gv_acc,
):
    seq = pl.program_id(0) + base
    blocks = p_ref.shape[1] // query_block
    lane = lax.broadcasted_iota(jnp.int32, (query_block, 128), 1)
    gk_acc[...] = jnp.zeros_like(gk_acc)
    gv_acc[...] = jnp.zeros_like(gv_acc)

    def step(block, carry):
        row = pl.multiple_of(block * query_block, query_block)
        which = seq * blocks + block

        def body(size):
            begin = pl.multiple_of(start_ref[which], 16)
            rows = pl.ds(row, query_block)
            span = pl.ds(begin, size)
            q_pair = p_ref[0, rows, 0:128]
            q_side = aug_ref[0, rows, :] * side_ref[...]
            k_pair = p_ref[0, span, 128:256]
            k_side = aug_ref[0, span, :]
            keys = jnp.concatenate([k_pair, k_side], axis=1)
            values = jnp.concatenate([p_ref[0, span, 256:384], k_side], axis=1)
            near = block % 2 == info_ref[1]
            go = jnp.where(near, go_mine_ref[0, block // 2], go_got_ref[0, block // 2])
            o = jnp.where(near, o_mine_ref[0, block // 2], o_send_ref[0, block // 2])
            scaled = go.astype(wide) * inv_ref[0, rows, :]
            scaled_low = scaled.astype(low)
            product = scaled_low.astype(wide) * o.astype(wide)
            powers, grads, queries, pulls = [], [], [], []
            for head in range(2):
                mine = lane // 64 == head
                inner = jnp.sum(jnp.where(mine, product, 0.0), axis=1, keepdims=True)
                one = inner.astype(low)
                two = (inner - one.astype(wide)).astype(low)
                three = (inner - one.astype(wide) - two.astype(wide)).astype(low)
                go_side = jnp.where(
                    lane == 6,
                    -one,
                    jnp.where(lane == 7, -two, jnp.where(lane == 8, -three, jnp.zeros_like(q_pair))),
                )
                q_mine = jnp.where(mine, q_pair, jnp.zeros_like(q_pair))
                go_mine = jnp.where(mine, scaled_low, jnp.zeros_like(q_pair))
                power = jnp.exp2(dot(keys, jnp.concatenate([q_mine, q_side], axis=1), 1, 1))
                slope = dot(values, jnp.concatenate([go_mine, go_side], axis=1), 1, 1)
                grad = (power * slope).astype(low)
                powers.append(power.astype(low))
                grads.append(grad)
                queries.append(q_mine)
                pulls.append(go_mine)
            gv_acc[span, :] += dot(
                jnp.concatenate(powers, axis=1), jnp.concatenate(pulls, axis=0)
            )
            gk_acc[span, :] += dot(
                jnp.concatenate(grads, axis=1), jnp.concatenate(queries, axis=0)
            )
            gq_acc[rows, :] = jnp.where(
                lane < 64, dot(grads[0], k_pair, 0, 0), dot(grads[1], k_pair, 0, 0)
            )

        for index, size in enumerate(windows):
            pl.when(kind_ref[which] == index)(partial(body, size))
        return carry

    lax.fori_loop(0, blocks, step, 0)
    g_ref[0, :, 256:384] = gv_acc[...].astype(low)
    means = mean_ref[...]

    @pl.when(pl.program_id(0) == 0)
    def _():
        gain_ref[...] = jnp.zeros_like(gain_ref)

    for index, acc, scale, unscale in (
        (0, gq_acc, 0.125, 8.0 / log2e),
        (1, gk_acc, 1.0 / log2e, 1.0),
    ):
        at = slice(128 * index, 128 * index + 128)
        gain = hg_ref[:, at]
        grad = acc[...] * scale
        normed = p_ref[0, :, at].astype(wide) * unscale
        weighted = grad * gain
        cross = grad * normed
        first = split_dot(weighted, means)
        second = split_dot(cross, means)
        g_ref[0, :, at] = (
            rate_ref[0, :, at] * (weighted - first - normed / gain * second)
        ).astype(low)
        gain_ref[index : index + 1, :] += jnp.sum(cross, axis=0, keepdims=True) / gain


def attn_out_kernel(info_ref, o_mine_ref, o_got_ref, mine_ref, got_ref, gy_ref, gain_ref, bias_ref, shards, *refs):
    x2_ref, h_ref, ht_ref, gyt_ref, w_ref, sems = refs
    cols = o_mine_ref.shape[3]
    c = info_ref[1]

    @pl.when((pl.program_id(0) == 0) & (pl.program_id(1) == 0))
    def _():
        run_all(
            load_shards([(shards, c, 0, cols, 0), (shards, 1 - c, 0, cols, cols)], w_ref, sems)
        )

    x = jnp.where(pl.program_id(1) == info_ref[0], mine_ref[0], got_ref[0]).astype(wide)
    x2 = x + dot(jnp.concatenate([o_mine_ref[0, 0], o_got_ref[0, 0]], axis=1), w_ref[...], 1, 1)
    x2_ref[...] = x2
    centered = x2 - jnp.mean(x2, axis=1, keepdims=True)
    variance = jnp.mean(centered * centered, axis=1, keepdims=True)
    h = centered * lax.rsqrt(variance + norm_eps) * gain_ref[...] + bias_ref[...]
    h_ref[...] = h.astype(low)
    ht_ref[...] = jnp.transpose(h).astype(low)
    gyt_ref[...] = jnp.transpose(gy_ref[...].astype(wide)).astype(low)


def spread(info_ref, acc, scale, mine_ref, other_ref, from_col, to_col, count):
    rows = mine_ref.shape[2]
    for side, ref in enumerate((mine_ref, other_ref)):
        if ref is None:
            continue
        for index in range(8):
            place = pl.multiple_of(info_ref[2 + index] * rows, rows)
            ref[index % 2, index // 2, :, to_col : to_col + count] = (
                acc[pl.ds(place, rows), from_col + side * count : from_col + (side + 1) * count]
                * scale
            ).astype(low)


def blocks(grad_ref, acc, scale, owners, to_col, count):
    rows = grad_ref.shape[1]
    for number, owner in enumerate(owners):
        for index in range(8):
            grad_ref[2 * index + owner, :, to_col : to_col + count] = (
                acc[index * rows : (index + 1) * rows, number * count : (number + 1) * count]
                * scale
            ).astype(low)


def mlp_kernel(first, begin, scale, info_ref, h_ref, ht_ref, gy_ref, gyt_ref, out_in_ref, *refs):
    if not first:
        gh_in_ref, *refs = refs
    shards, *refs = refs if first else [refs[0], *refs[2:]]
    out_ref, gh_ref, grad_ref, up_ref, down_ref, up_acc, down_acc, sems = refs
    step = pl.program_id(0)
    chunk = up_ref.shape[1] // 2

    @pl.when(step == 0)
    def _():
        run_all(
            load_shards([(shards, m, begin, chunk, m * chunk) for m in range(2)], up_ref, sems)
            + load_shards(
                [(shards, m, begin + chunk, chunk, m * chunk) for m in range(2)],
                down_ref,
                sems.at[pl.ds(2, 2)],
            )
        )

    root = math.sqrt(2.0 / math.pi)
    t = dot(h_ref[...], up_ref[...])
    square = t * t
    gate = 0.5 + 0.5 * jnp.tanh(t * (root + (root * 0.044715) * square))
    act = t * gate
    slope = gate + 2.0 * act * (1.0 - gate) * (root + (3.0 * root * 0.044715) * square)
    act = act.astype(low)
    grad = (dot(gy_ref[...], down_ref[...]) * slope).astype(low)
    out_ref[...] = out_in_ref[...] + dot(act, down_ref[...], 1, 1)
    back = dot(grad, up_ref[...], 1, 1)
    gh_ref[...] = back if first else gh_in_ref[...] + back

    @pl.when(step == 0)
    def _():
        up_acc[...] = dot(ht_ref[...], grad)
        down_acc[...] = dot(gyt_ref[...], act)

    @pl.when(step > 0)
    def _():
        up_acc[...] += dot(ht_ref[...], grad)
        down_acc[...] += dot(gyt_ref[...], act)

    @pl.when(step == pl.num_programs(0) - 1)
    def _():
        blocks(grad_ref, up_acc, scale, (0, 1), 0, chunk)
        blocks(grad_ref, down_acc, scale, (0, 1), chunk, chunk)


def norm_back(values, grad, gain):
    centered = values - jnp.mean(values, axis=1, keepdims=True)
    rate = lax.rsqrt(jnp.mean(centered * centered, axis=1, keepdims=True) + norm_eps)
    normed = centered * rate
    weighted = grad * gain
    result = rate * (
        weighted
        - jnp.mean(weighted, axis=1, keepdims=True)
        - normed * jnp.mean(weighted * normed, axis=1, keepdims=True)
    )
    return result, normed


def second_norm_kernel(
    scale, info_ref, x2_ref, gh_ref, gy_ref, y_ref, valid_ref, o_mine_ref, o_got_ref, gain_ref, *refs
):
    shards, refs = refs[0], refs[2:]
    keep_ref, send_ref, gx_ref, go_mine_ref, go_send_ref, grad_ref, sums_ref = refs[:7]
    w_ref, acc, sems = refs[7:]
    c = info_ref[1]
    cols = o_mine_ref.shape[3]
    half = pl.program_id(1)
    start = (pl.program_id(0) == 0) & (half == 0)
    end = (pl.program_id(0) == pl.num_programs(0) - 1) & (half == 1)

    @pl.when(start)
    def _():
        run_all(
            load_shards([(shards, c, 0, cols, 0), (shards, 1 - c, 0, cols, cols)], w_ref, sems)
        )
        sums_ref[...] = jnp.zeros_like(sums_ref)
        acc[...] = jnp.zeros_like(acc)

    out = (y_ref[...] * valid_ref[...][:, :1]).astype(low)

    @pl.when(half == info_ref[0])
    def _():
        keep_ref[0] = out

    @pl.when(half != info_ref[0])
    def _():
        send_ref[0] = out

    gh = gh_ref[...]
    back, normed = norm_back(x2_ref[...], gh, gain_ref[...])
    gx = gy_ref[...].astype(wide) + back
    gx_ref[...] = gx
    go = dot(gx.astype(low), w_ref[...]).astype(low)
    go_mine_ref[0, 0] = go[:, :cols]
    go_send_ref[0, 0] = go[:, cols:]
    turned = jnp.transpose(gx).astype(low)
    sums_ref[0:1, :] += jnp.sum(gh * normed, axis=0, keepdims=True)
    sums_ref[1:2, :] += jnp.sum(gh, axis=0, keepdims=True)
    acc[...] += dot(turned, jnp.concatenate([o_mine_ref[0, 0], o_got_ref[0, 0]], axis=1))

    @pl.when(end)
    def _():
        blocks(grad_ref, acc, scale, (c, 1 - c), 0, cols)


def gw_in_kernel(scale, info_ref, ht_ref, *refs):
    grads, (out_ref, acc) = refs[:-2], refs[-2:]
    step = pl.program_id(0)

    def add(grad_ref):
        @pl.when(step == 0)
        def _():
            acc[...] = dot(ht_ref[...], grad_ref[0])

        @pl.when(step > 0)
        def _():
            acc[...] += dot(ht_ref[...], grad_ref[0])

    if len(grads) == 1:
        add(grads[0])
    else:
        for index, grad_ref in enumerate(grads):
            pl.when(step == index)(partial(add, grad_ref))

    @pl.when(step == pl.num_programs(0) - 1)
    def _():
        spread(info_ref, acc, scale, out_ref, None, 0, 0, out_ref.shape[3])


def gh1_kernel(info_ref, *refs):
    grads, pieces = refs[:3], refs[3:11]
    mine_ref, send_ref, w_ref, sems = refs[11:]

    @pl.when(pl.program_id(0) == 0)
    def _():
        run_all(load_pieces(info_ref, [(pieces, 0, w_ref.shape[1], 0)], w_ref, sems))

    both = dot(jnp.concatenate([ref[0] for ref in grads], axis=1), w_ref[...], 1, 1).astype(low)
    part = mine_ref.shape[1]
    near = info_ref[1] == 0
    mine_ref[0] = jnp.where(near, both[:part], both[part:])
    send_ref[0] = jnp.where(near, both[part:], both[:part])


def first_norm_kernel(
    info_ref, mine_ref, got_ref, a_ref, b_ref, gx2_ref, gain_ref, keep_ref, send_ref, sums_ref
):
    half = pl.program_id(0)
    x = jnp.where(half == info_ref[0], mine_ref[0], got_ref[0]).astype(wide)
    gh = a_ref[0].astype(wide) + b_ref[0].astype(wide)
    back, normed = norm_back(x, gh, gain_ref[...])
    out = (gx2_ref[...] + back).astype(low)

    @pl.when(half == info_ref[0])
    def _():
        keep_ref[...] = out

    @pl.when(half != info_ref[0])
    def _():
        send_ref[...] = out

    @pl.when(half == 0)
    def _():
        sums_ref[...] = jnp.zeros_like(sums_ref)

    sums_ref[0:1, :] += jnp.sum(gh * normed, axis=0, keepdims=True)
    sums_ref[1:2, :] += jnp.sum(gh, axis=0, keepdims=True)


def shape_of(dims, kind=low):
    return jax.ShapeDtypeStruct(dims, kind)


def window_table(segs, blocks):
    length = segs.shape[1]
    pad_begin = jnp.sum((segs >= 0).astype(jnp.int32), axis=1, keepdims=True)
    begins = jnp.where(segs >= 0, segs, pad_begin)
    size = length // blocks
    firsts = begins[:, ::size]
    lasts = begins[:, size - 1 :: size]
    ends = jnp.sum((begins[:, None, :] <= lasts[:, :, None]).astype(jnp.int32), axis=2)
    reach = ends - firsts
    kinds = jnp.zeros_like(reach)
    spans = jnp.full_like(reach, windows[0])
    for index in range(1, len(windows)):
        larger = reach > windows[index - 1]
        kinds = jnp.where(larger, index, kinds)
        spans = jnp.where(larger, windows[index], spans)
    starts = jnp.minimum(firsts, length - spans)
    return starts.reshape(-1), kinds.reshape(-1)


def mask_columns(segs):
    codes = (segs + 16) // 16
    lane = jnp.arange(128, dtype=jnp.int32)
    bits = (codes[:, :, None] >> jnp.minimum(lane, 5)) & 1
    signs = (2 * bits - 1).astype(wide)
    return jnp.where(lane < 6, signs, jnp.where(lane < 9, 1.0, 0.0)).astype(low)


def swap(values, axis):
    return lax.ppermute(values, axis, [(0, 1), (1, 0)])


def in_order(index, mine, other, axis):
    return jnp.where(
        index == 0,
        jnp.concatenate([mine, other], axis=axis),
        jnp.concatenate([other, mine], axis=axis),
    )


def pick(values, index, axis):
    return lax.dynamic_index_in_dim(values, index, axis, keepdims=False)


def shift_far(values, step):
    return lax.ppermute(
        values,
        "dp",
        [(2 * ((z + step) % 4) + x, 2 * z + x) for z in range(4) for x in range(2)],
    )


def swap_x(values):
    return lax.ppermute(values, "dp", [(d, d ^ 1) for d in range(8)])


def gather_pieces(shard):
    pieces = []
    for step in range(4):
        piece = shard if step == 0 else shift_far(shard, step)
        pieces += [piece, swap_x(piece)]
    return pieces


class Reduce:
    def __init__(self, mine, other=None):
        self.mine = mine
        self.other = other
        self.got = None
        self.state = None
        self.phase = "core" if other is not None else "x"

    def advance(self):
        if self.phase == "core":
            self.state = self.got = swap(self.other, "mlp")
            self.phase = "x"
        elif self.phase == "x":
            far = self.mine[1]
            if self.got is not None:
                far = (far.astype(wide) + self.got[1].astype(wide)).astype(low)
            self.state = swap_x(far)
            self.phase = "z"
        elif self.phase == "z":
            total = self.mine[0].astype(wide) + self.state.astype(wide)
            if self.got is not None:
                total = total + self.got[0].astype(wide)
            low_total = total.astype(low)
            self.mine = total[0]
            self.state = [shift_far(low_total[step], 4 - step) for step in range(1, 4)]
            self.phase = "y"
        elif self.phase == "y":
            self.mine = self.mine + sum(part.astype(wide) for part in self.state)
            self.state = swap(self.mine.astype(low), "seq")
            self.phase = "end"
        elif self.phase == "end":
            self.mine = self.mine + self.state.astype(wide)
            self.state = None
            self.phase = "done"

    def result(self):
        while self.phase != "done":
            self.advance()
        return self.mine


def on_device_small(
    patches, segments, w_qkv, w_out, w_up, w_down, ln_gain, ln_bias, head_gain, cotangent
):
    half, seqs_all, width = patches.shape
    length = 2 * half
    seqs = seqs_all // 2
    cols = w_qkv.shape[2]
    part = half // 2
    y = lax.axis_index("seq")
    c = lax.axis_index("mlp")
    d = lax.axis_index("dp")
    dp_size = lax.axis_size("dp")
    scale = 1.0 / math.sqrt(dp_size * seqs_all * length)
    own_rows = seqs * half
    hidden = w_up.shape[1]
    shard_rows = width // dp_size
    places = jnp.stack(
        [2 * ((d // 2 + index // 2) % 4) + ((d % 2) ^ (index % 2)) for index in range(8)]
    )
    info = jnp.concatenate([jnp.stack([y, c]), places]).astype(jnp.int32)

    turned = jnp.transpose(patches, (1, 0, 2)).reshape(2, seqs, 2, part, width)
    got = swap(pick(pick(turned, 1 - y, 0), c, 1), "seq")
    far = swap(got, "mlp")
    turned = turned.reshape(seqs_all, half, width)
    small = jnp.concatenate(
        [
            ln_gain.astype(low),
            ln_bias.astype(low),
            head_gain.astype(low).reshape(1, -1),
            jnp.zeros((3, shard_rows), low),
        ]
    )
    small = jnp.pad(small, ((0, 8), (0, 3 * cols - shard_rows)))
    pairs = cols // 128
    w_in = jnp.transpose(w_qkv.astype(low).reshape(3, shard_rows, pairs, 128), (1, 2, 0, 3))
    w_in = w_in.reshape(shard_rows, 3 * cols)
    in_pieces = gather_pieces(
        jnp.concatenate(
            [w_in, small]
        )
    )
    small = [piece[shard_rows : shard_rows + 8, :shard_rows] for piece in in_pieces]
    chunk = 512
    chunks = hidden // chunk
    up_low = w_up.astype(low)
    down_low = jnp.transpose(w_down.astype(low))
    parts = [jnp.transpose(w_out.astype(low))]
    for f in range(chunks):
        at = slice(f * chunk, (f + 1) * chunk)
        parts += [up_low[:, at], down_low[:, at]]

    def gather_shards(parts):
        return lax.all_gather(jnp.concatenate(parts, axis=1), ("dp", "mlp"), axis=0)

    split = 5
    shards_a = gather_shards(parts[:split])
    shards_b = gather_shards(parts[split:])

    order = (places[None, :] == jnp.arange(8)[:, None]).astype(low)
    small = jnp.einsum("nr,rkw->knw", order, jnp.stack(small), preferred_element_type=wide)
    gains = small[0:2].reshape(2, width)
    biases = small[2:4].reshape(2, width)
    head_gains = jnp.transpose(small[4].reshape(dp_size, 2, cols // 64, 64 // dp_size), (1, 2, 0, 3))
    head_gains = jnp.transpose(head_gains.reshape(2, pairs, 128), (1, 0, 2))
    key_scale = jnp.array([[[log2e / 8.0], [1.0]]], wide)
    head_scaled = (head_gains * key_scale).reshape(1, 2 * cols)
    head_gains = head_gains.reshape(1, 2 * cols)

    segs = lax.dynamic_slice_in_dim(jnp.transpose(segments), y * seqs, seqs, 0)
    cot = cotangent.reshape(2, part, seqs_all, cols)
    cot_other = swap(pick(cot, 1 - c, 0), "mlp")
    cot = jnp.transpose(in_order(c, pick(cot, c, 0), cot_other, 2), (1, 0, 2))
    cot = cot.reshape(2, seqs, part, width)
    cot_got = swap(pick(cot, 1 - y, 0), "seq")
    cot = in_order(y, pick(cot, y, 0)[:, None], cot_got[:, None], 1)
    valid = pick((segs >= 0).reshape(seqs, 2, 2, part), c, 2)
    gy = jnp.where(valid[..., None], cot, jnp.zeros_like(cot)).reshape(own_rows, width)
    valid = jnp.broadcast_to(valid.reshape(own_rows, 1).astype(wide), (own_rows, 128))

    starts, kinds = window_table(segs, length // query_block)
    aug = mask_columns(segs)
    lanes = jnp.arange(128)
    side = jnp.where(lanes < 6, mask_weight, jnp.where(lanes == 6, -6.0 * mask_weight, 0.0))
    side = side.astype(low)[None]
    means = jnp.where(lanes[:, None] // 64 == lanes[None] // 64, 1.0 / 64, 0.0).astype(low)
    anywhere = pl.BlockSpec(memory_space=pl.ANY)

    def whole(dims):
        return pl.BlockSpec(dims, lambda *ids: (0,) * len(dims))

    def call(kernel, grid, in_specs, out_specs, out_shape, scratch, name, scalars, pins=(), share=1, alias=None):
        work = micros[name] * 1150000000 // share
        ends = scalars + len(in_specs)

        def unpinned(*refs):
            kernel(*refs[:ends], *refs[ends + len(pins) :])

        run = pl.pallas_call(
            unpinned,
            grid_spec=pltpu.PrefetchScalarGridSpec(
                num_scalar_prefetch=scalars,
                grid=grid,
                in_specs=in_specs + [anywhere] * len(pins),
                out_specs=out_specs,
                scratch_shapes=scratch,
            ),
            out_shape=out_shape,
            compiler_params=params(len(grid)),
            input_output_aliases=alias or {},
            cost_estimate=pl.CostEstimate(flops=work, bytes_accessed=1000000, transcendentals=0),
            name=name,
        )
        return lambda *operands: run(*operands, *pins)

    piece_sems = pltpu.SemaphoreType.DMA((4, 8))
    one_seq = pl.BlockSpec((1, part, width), lambda s, j, *_: (s, 0, 0))
    projected, rates, h1t = call(
        qkv_kernel,
        (seqs, 4),
        [
            pl.BlockSpec((1, part, width), lambda s, j, info: (seqs * info[0] + s, j % 2, 0)),
            one_seq,
            one_seq,
            whole((1, width)),
            whole((1, width)),
            whole((1, 2 * cols)),
            whole((128, 128)),
        ]
        + [anywhere] * 8,
        [
            pl.BlockSpec((1, part, 3 * cols), lambda s, j, *_: (s, j, 0)),
            pl.BlockSpec((1, part, 2 * cols), lambda s, j, *_: (s, j, 0)),
            pl.BlockSpec((width, part), lambda s, j, *_: (0, 4 * s + j)),
        ],
        [
            shape_of((seqs, length, 3 * cols)),
            shape_of((seqs, length, 2 * cols), wide),
            shape_of((width, seqs * length)),
        ],
        [pltpu.VMEM((width, 3 * cols), low), piece_sems],
        "qkv",
        1,
    )(info, turned, got, far, gains[:1], biases[:1], head_scaled, means, *in_pieces)
    split_seq = pl.BlockSpec((1, 2, part, 128), lambda s, p, *_: (s, 0, 0, p))
    o_mine, o_send, inverse = call(
        attn_fwd_kernel,
        (seqs, pairs),
        [
            pl.BlockSpec((1, length, 384), lambda s, p, *_: (s, 0, p)),
            pl.BlockSpec((1, length, 128), lambda s, p, *_: (s, 0, 0)),
            whole((1, 128)),
        ],
        [split_seq, split_seq, pl.BlockSpec((1, length, 128), lambda s, p, *_: (s, 0, p))],
        [shape_of((seqs, 2, part, cols))] * 2 + [shape_of((seqs, length, cols), wide)],
        [],
        "attn_fwd",
        3,
    )(info, starts, kinds, projected, aug, side)

    o_got = swap(o_send, "mlp")
    mine_spec = pl.BlockSpec((1, part, width), lambda s, h, info: (seqs * info[0] + s, info[1], 0))
    got_spec = pl.BlockSpec((1, part, width), lambda s, h, *_: (s, 0, 0))
    rows_spec = pl.BlockSpec((part, width), lambda s, h, *_: (2 * s + h, 0))
    turned_spec = pl.BlockSpec((width, part), lambda s, h, *_: (0, 2 * s + h))
    part_spec = pl.BlockSpec((1, 1, part, cols), lambda s, h, *_: (s, h, 0, 0))
    x2, h2, h2t, gyt = call(
        attn_out_kernel,
        (seqs, 2),
        [part_spec, part_spec, mine_spec, got_spec, rows_spec, whole((1, width)), whole((1, width))]
        + [anywhere],
        [rows_spec, rows_spec, turned_spec, turned_spec],
        [
            shape_of((own_rows, width), wide),
            shape_of((own_rows, width)),
            shape_of((width, own_rows)),
            shape_of((width, own_rows)),
        ],
        [pltpu.VMEM((width, width), low), piece_sems],
        "attn_out",
        1,
    )(info, o_mine, o_got, turned, got, gy, gains[1:], biases[1:], shards_a)

    block = half
    block_spec = pl.BlockSpec((block, width), lambda i, *_: (i, 0))
    block_turned = pl.BlockSpec((width, block), lambda i, *_: (0, i))
    total, gh = x2, None
    sums = []

    def advance():
        pins = []
        for one in sums:
            pins += jax.tree.leaves(one.state)
            one.advance()
        return pins

    grads = None
    grad_shape = shape_of((16, shard_rows, cols + 2 * hidden))
    for f in range(chunks):
        first = f == 0
        carried = [total] if first else [total, gh]
        begin = cols + f * 2 * chunk
        source = shards_a
        if begin >= shards_a.shape[2]:
            source, begin = shards_b, begin - shards_a.shape[2]
        extra = [] if first else [grads]
        total, gh, grads = call(
            partial(mlp_kernel, first, begin, scale),
            (seqs,),
            [block_spec, block_turned, block_spec, block_turned]
            + [block_spec] * len(carried)
            + [anywhere] * (1 + len(extra)),
            [block_spec] * 2
            + [pl.BlockSpec((16, shard_rows, 2 * chunk), lambda *_, f=f: (0, 0, f))],
            [shape_of((own_rows, width), wide)] * 2 + [grad_shape],
            [pltpu.VMEM((width, 2 * chunk), low)] * 2
            + [pltpu.VMEM((width, 2 * chunk), wide)] * 2
            + [piece_sems],
            "mlp",
            1,
            alias={} if first else {8: 2},
        )(info, h2, h2t, gy, gyt, *carried, source, *extra)

    last_block = 2 * hidden // cols
    out_keep, out_send, gx2, go_mine, go_send, grads, second_sums = call(
        partial(second_norm_kernel, scale),
        (seqs, 2),
        [
            rows_spec,
            rows_spec,
            rows_spec,
            rows_spec,
            pl.BlockSpec((part, 128), lambda s, h, *_: (2 * s + h, 0)),
            part_spec,
            part_spec,
            whole((1, width)),
        ]
        + [anywhere] * 2,
        [got_spec, got_spec, rows_spec, part_spec, part_spec]
        + [pl.BlockSpec((16, shard_rows, cols), lambda *_: (0, 0, last_block))]
        + [whole((8, width))],
        [shape_of((seqs, part, width))] * 2
        + [shape_of((own_rows, width), wide)]
        + [shape_of((seqs, 2, part, cols))] * 2
        + [grad_shape]
        + [shape_of((8, width), wide)],
        [pltpu.VMEM((width, width), low), pltpu.VMEM((width, width), wide), piece_sems],
        "second_norm",
        1,
        alias={10: 5},
    )(info, x2, gh, gy, total, valid, o_mine, o_got, gains[1:], shards_a, grads)
    go_got = swap(go_send, "mlp")
    out_swapped = swap(out_send, "seq")
    scattered = lax.psum_scatter(grads, ("dp", "mlp"), scatter_dimension=0, tiled=True)[0]

    def attention_back(pair, base, count, pins):
        split_pair = pl.BlockSpec((1, 2, part, 128), lambda s, *_: (s + base, 0, 0, pair))
        columns = pl.BlockSpec((1, length, 128), lambda s, *_: (s + base, 0, pair))
        return call(
            partial(attn_bwd_kernel, base),
            (count,),
            [pl.BlockSpec((1, length, 384), lambda s, *_: (s + base, 0, pair))]
            + [split_pair] * 4
            + [
                columns,
                pl.BlockSpec((1, length, 256), lambda s, *_: (s + base, 0, pair)),
                pl.BlockSpec((1, length, 128), lambda s, *_: (s + base, 0, 0)),
                whole((1, 128)),
                pl.BlockSpec((1, 256), lambda s, *_: (0, pair)),
                whole((128, 128)),
            ],
            [pl.BlockSpec((1, length, 384), lambda s, *_: (s, 0, 0)), whole((8, 128))],
            [shape_of((count, length, 384)), shape_of((8, 128), wide)],
            [pltpu.VMEM((length, 128), wide)] * 3,
            "attn_bwd",
            3,
            pins,
            3 * seqs // count,
        )(
            info, starts, kinds, projected, go_mine, go_got, o_mine, o_send, inverse, rates,
            aug, side, head_gains, means,
        )

    def input_weights(grads):
        if len(grads) == 1:
            specs = [pl.BlockSpec((1, length, 384), lambda s, *_: (s, 0, 0))]
        else:
            specs = [whole((1, length, 384))] * len(grads)
        shares = (2, 4, shard_rows, 384)
        return call(
            partial(gw_in_kernel, scale),
            (seqs,),
            [pl.BlockSpec((width, length), lambda s, *_: (0, s))] + specs,
            whole(shares),
            shape_of(shares),
            [pltpu.VMEM((width, 384), wide)],
            "gw_in",
            1,
            (),
            3,
        )(info, h1t, *grads)

    def first_grads(seq, grads, pins):
        return call(
            gh1_kernel,
            (2,),
            [
                pl.BlockSpec((1, half, 384), lambda h, *_, at=seq % grad.shape[0]: (at, h, 0))
                for grad in grads
            ]
            + [anywhere] * 8,
            [pl.BlockSpec((1, part, width), lambda h, *_: (h, 0, 0))] * 2,
            [shape_of((2, part, width))] * 2,
            [pltpu.VMEM((width, 3 * cols), low), piece_sems],
            "gh1",
            1,
            pins,
            3,
        )(info, *grads, *in_pieces)

    def first_back(seq, mine, got_part, pins):
        halves = pl.BlockSpec((1, part, width), lambda h, *_: (h, 0, 0))
        return call(
            first_norm_kernel,
            (2,),
            [
                pl.BlockSpec((1, part, width), lambda h, info: (seqs * info[0] + seq, info[1], 0)),
                pl.BlockSpec((1, part, width), lambda h, *_: (seq, 0, 0)),
                halves,
                halves,
                pl.BlockSpec((part, width), lambda h, *_: (2 * seq + h, 0)),
                whole((1, width)),
            ],
            [whole((part, width))] * 2 + [whole((8, width))],
            [shape_of((part, width))] * 2 + [shape_of((8, width), wide)],
            [],
            "first_norm",
            1,
            pins,
            3,
        )(info, turned, got, mine, got_part, gx2, gains[:1])

    def finish_out():
        out_six = in_order(y, out_keep, out_swapped, 0).reshape(seqs_all, part, 2, cols)
        out_got = swap(pick(out_six, 1 - c, 2), "mlp")
        return jnp.transpose(in_order(c, pick(out_six, c, 2), out_got, 1), (1, 0, 2))

    full_grads, gain_sums, in_sums = [], [], []
    out = None
    for pair in range(pairs):
        pins = advance()
        if pair == 1:
            pins.append(out_swapped)
            out = finish_out()
        if pair == 2:
            pins.append(out)
        grads, gain_sum = attention_back(pair, 0, seqs, pins)
        full_grads.append(grads)
        gain_sums.append(gain_sum)
        if pair < pairs - 1:
            in_sums.append(Reduce(input_weights([grads])))
            sums.append(in_sums[-1])
    halves_sent, backs = [], []
    for seq in range(seqs):
        mine, send = first_grads(seq, full_grads, ())
        halves_sent.append((mine, swap(send, "mlp")))
        if seq:
            backs.append(first_back(seq - 1, *halves_sent[seq - 1], ()))
    in_sums.append(Reduce(input_weights([grads])))
    sums.append(in_sums[-1])
    advance()
    backs.append(first_back(seqs - 1, *halves_sent[seqs - 1], ()))
    first_sums = sum(back[2] for back in backs)

    mine_parts, other_parts = [], []
    for keep, send, _ in backs:
        got_rows = swap(send, "seq")
        mine_parts.append(in_order(c, keep, swap(keep, "mlp"), 0))
        other_parts.append(in_order(c, got_rows, swap(got_rows, "mlp"), 0))
    grad_patches = in_order(y, jnp.stack(mine_parts), jnp.stack(other_parts), 0)
    grad_patches = jnp.transpose(grad_patches, (1, 0, 2))

    scattered = scattered.astype(wide) + swap(scattered, "seq").astype(wide)
    gw_up = jnp.concatenate(
        [scattered[:, 2 * f * chunk : (2 * f + 1) * chunk] for f in range(chunks)], axis=1
    )
    gw_down = jnp.concatenate(
        [scattered[:, (2 * f + 1) * chunk : (2 * f + 2) * chunk] for f in range(chunks)], axis=1
    )
    gw_out = scattered[:, 2 * hidden :]
    gw_in = jnp.stack([one.result() for one in in_sums], axis=1)
    gw_in = gw_in.reshape(shard_rows, pairs, 3, 128)
    gw_in = jnp.transpose(gw_in, (2, 0, 1, 3)).reshape(3, shard_rows, cols)
    norms = jnp.concatenate([first_sums[:2], second_sums[:2]]) * scale
    norms = norms + swap(norms, "mlp")
    heads = jnp.stack([part[:2] for part in gain_sums], axis=1).reshape(2, cols) * scale
    small = jnp.concatenate([norms, heads.reshape(1, width)])
    small = small + swap(small, "seq")
    for bit in (1, 2, 4):
        small = small + lax.ppermute(small, "dp", [(i, i ^ bit) for i in range(8)])
    norms = lax.dynamic_slice_in_dim(small[:4], d * shard_rows, shard_rows, 1)
    heads = small[4].reshape(2, cols // 64, 64)
    heads = lax.dynamic_slice_in_dim(heads, d * (64 // dp_size), 64 // dp_size, 2)
    return (
        out,
        grad_patches,
        gw_in,
        jnp.transpose(gw_out),
        gw_up,
        jnp.transpose(gw_down),
        norms[0::2],
        norms[1::2],
        heads,
    )


def solution(mesh):
    shape = dict(mesh.shape)
    small = shape["seq"] == 2 and shape["mlp"] == 2 and shape["dp"] == 8
    return jax.shard_map(
        on_device_small if small else on_device,
        mesh=mesh,
        in_specs=(
            P("seq", "dp", None),
            P(None, "dp"),
            P(None, "dp", "mlp"),
            P("mlp", "dp"),
            P("dp", "mlp"),
            P("mlp", "dp"),
            P(None, "dp"),
            P(None, "dp"),
            P(None, "mlp", "dp"),
            P("seq", "dp", "mlp"),
        ),
        out_specs=(
            P("seq", "dp", "mlp"),
            P("seq", "dp", None),
            P(None, "dp", "mlp"),
            P("mlp", "dp"),
            P("dp", "mlp"),
            P("mlp", "dp"),
            P(None, "dp"),
            P(None, "dp"),
            P(None, "mlp", "dp"),
        ),
        check_vma=False,
    )
```

```python
from functools import partial
import math

import jax
import jax.numpy as jnp
from jax import lax
from jax.experimental import pallas as pl
from jax.experimental.pallas import tpu as pltpu
from jax.sharding import PartitionSpec as P

norm_eps = 1e-06
masked_value = -1e30


def layer_norm(values, gain_row, bias_row):
    average = jnp.mean(values, axis=-1, keepdims=True)
    centered = values - average
    variance = jnp.mean(centered * centered, axis=-1, keepdims=True)
    return centered * lax.rsqrt(variance + norm_eps) * gain_row + bias_row


def head_norm(values, gain_rows):
    average = jnp.mean(values, axis=-1, keepdims=True)
    centered = values - average
    variance = jnp.mean(centered * centered, axis=-1, keepdims=True)
    return centered * lax.rsqrt(variance + norm_eps) * gain_rows


def on_device(
    patches, segments, w_qkv, w_out, w_up, w_down, ln_gain, ln_bias, head_gain, cotangent
):
    (
        query_weight,
        out_weight,
        up_projection_weight,
        down_projection_weight,
        norm_gains,
        norm_biases,
        head_gains,
    ) = (
        lax.all_gather(w_qkv.astype(jnp.bfloat16), "dp", axis=1, tiled=True),
        lax.all_gather(w_out.astype(jnp.bfloat16), "dp", axis=1, tiled=True),
        lax.all_gather(w_up.astype(jnp.bfloat16), "dp", axis=0, tiled=True),
        lax.all_gather(w_down.astype(jnp.bfloat16), "dp", axis=1, tiled=True),
        lax.all_gather(ln_gain.astype(jnp.bfloat16), "dp", axis=1, tiled=True),
        lax.all_gather(ln_bias.astype(jnp.bfloat16), "dp", axis=1, tiled=True),
        lax.all_gather(head_gain.astype(jnp.bfloat16), "dp", axis=2, tiled=True),
    )
    local_rows = patches.shape[0]
    seq_here = patches.shape[1]
    width = patches.shape[2]
    head_cols = query_weight.shape[2]
    heads_here = head_gains.shape[1]
    head_size = head_gains.shape[2]
    seq_len = local_rows * lax.axis_size("seq")
    feature_cols = width // lax.axis_size("mlp")
    score_scale = head_size ** (-0.5)
    gain_float = norm_gains.astype(jnp.float32)
    bias_float = norm_biases.astype(jnp.float32)
    head_float = head_gains.astype(jnp.float32)
    seg_here = lax.dynamic_slice_in_dim(segments, lax.axis_index("seq") * local_rows, local_rows, 0)
    valid_mask = (seg_here >= 0).astype(jnp.float32)[:, :, None]
    query_segs = jnp.transpose(seg_here)
    key_segs = jnp.transpose(segments)
    patch_float = patches.astype(jnp.float32)
    normed = layer_norm(patch_float, gain_float[0], bias_float[0]).astype(jnp.bfloat16)
    projected = jnp.einsum(
        "lsd,cde->csle", normed, query_weight, preferred_element_type=jnp.float32
    )
    shape_heads = (seq_here, local_rows, heads_here, head_size)
    query_raw = projected[0].reshape(shape_heads)
    key_raw = projected[1].reshape(shape_heads)
    query_low = head_norm(query_raw, head_float[0]).astype(jnp.bfloat16)
    key_low = head_norm(key_raw, head_float[1]).astype(jnp.bfloat16)
    value_low = projected[2].astype(jnp.bfloat16)
    key_pairs = jnp.concatenate(
        [key_low.reshape(seq_here, local_rows, head_cols), value_low], axis=2
    )

    def split_pairs(gathered):
        key_heads = gathered[:, :head_cols].reshape(gathered.shape[0], heads_here, head_size)
        value_heads = gathered[:, head_cols:].reshape(gathered.shape[0], heads_here, head_size)
        return (key_heads, value_heads)

    def attend_forward(unused, inputs_seq):
        query_seq, pairs_seq, query_rows, key_rows = inputs_seq
        gathered = lax.all_gather(pairs_seq, "seq", axis=0, tiled=True)
        key_heads, value_heads = split_pairs(gathered)
        logits = (
            jnp.einsum("qhe,khe->hqk", query_seq, key_heads, preferred_element_type=jnp.float32)
            * score_scale
        )
        visible = (query_rows[:, None] == key_rows[None, :])[None]
        masked = jnp.where(visible, logits, masked_value)
        largest = jnp.max(masked, axis=2, keepdims=True)
        powered = jnp.exp(masked - largest)
        totals = jnp.sum(powered, axis=2, keepdims=True)
        attention = (powered / totals).astype(jnp.bfloat16)
        mixed = jnp.einsum(
            "hqk,khe->qhe", attention, value_heads, preferred_element_type=jnp.float32
        )
        log_total = (largest + jnp.log(totals))[:, :, 0]
        return (unused, (mixed.astype(jnp.bfloat16).reshape(local_rows, head_cols), log_total))

    _, (attn_heads, log_totals) = lax.scan(
        attend_forward, 0, (query_low, key_pairs, query_segs, key_segs)
    )
    attn_part = jnp.einsum(
        "slf,fd->lsd", attn_heads, out_weight, preferred_element_type=jnp.float32
    )
    attn_mine = lax.psum_scatter(
        attn_part.astype(jnp.bfloat16), "mlp", scatter_dimension=2, tiled=True
    ).astype(jnp.float32)
    patch_mine = lax.dynamic_slice_in_dim(
        patch_float, lax.axis_index("mlp") * feature_cols, feature_cols, 2
    )
    resid_mine = patch_mine + attn_mine
    residual = lax.all_gather(resid_mine.astype(jnp.bfloat16), "mlp", axis=2, tiled=True).astype(
        resid_mine.dtype
    )
    second_normalized = layer_norm(residual, gain_float[1], bias_float[1]).astype(jnp.bfloat16)
    hidden_pre = jnp.einsum(
        "own,nr->owr", second_normalized, up_projection_weight, preferred_element_type=jnp.float32
    )
    mlp_activation = jax.nn.gelu(hidden_pre, approximate=True).astype(jnp.bfloat16)
    branch_part = jnp.einsum(
        "ruo,oe->rue", mlp_activation, down_projection_weight, preferred_element_type=jnp.float32
    )
    branch_mine = lax.psum_scatter(
        branch_part.astype(jnp.bfloat16), "mlp", scatter_dimension=2, tiled=True
    ).astype(jnp.float32)
    out = (valid_mask * (resid_mine + branch_mine)).astype(jnp.bfloat16)
    cot_full = lax.all_gather(cotangent, "mlp", axis=2, tiled=True)
    grad_out = valid_mask * cot_full.astype(jnp.float32)
    output_gradient_reduced = grad_out.astype(jnp.bfloat16)
    grad_down = jnp.einsum(
        "xgr,xge->re", mlp_activation, output_gradient_reduced, preferred_element_type=jnp.float32
    )
    grad_act = jnp.einsum(
        "mit,nt->min",
        output_gradient_reduced,
        down_projection_weight,
        preferred_element_type=jnp.float32,
    )
    _, gelu_pull = jax.vjp(partial(jax.nn.gelu, approximate=True), hidden_pre)
    hidden_gradient = gelu_pull(grad_act)[0].astype(jnp.bfloat16)
    up_projection_gradient = jnp.einsum(
        "gih,giv->hv", second_normalized, hidden_gradient, preferred_element_type=jnp.float32
    )
    grad_normed_two = lax.psum(
        jnp.einsum(
            "vwb,kb->vwk", hidden_gradient, up_projection_weight, preferred_element_type=jnp.float32
        ).astype(jnp.bfloat16),
        "mlp",
    ).astype(jnp.float32)
    _, second_pull = jax.vjp(layer_norm, residual, gain_float[1], bias_float[1])
    grad_resid_norm, grad_gain_two, grad_bias_two = second_pull(grad_normed_two)
    grad_resid = grad_out + grad_resid_norm
    grad_resid_low = grad_resid.astype(jnp.bfloat16)
    grad_out_weight = jnp.einsum(
        "slf,lsd->fd", attn_heads, grad_resid_low, preferred_element_type=jnp.float32
    )
    grad_mixed = jnp.einsum(
        "lsd,fd->slf", grad_resid_low, out_weight, preferred_element_type=jnp.float32
    ).astype(jnp.bfloat16)

    def attend_backward(unused, inputs_seq):
        query_seq, pairs_seq, query_rows, key_rows, log_total, grad_seq = inputs_seq
        gathered = lax.all_gather(pairs_seq, "seq", axis=0, tiled=True)
        key_heads, value_heads = split_pairs(gathered)
        logits = (
            jnp.einsum("qhe,khe->hqk", query_seq, key_heads, preferred_element_type=jnp.float32)
            * score_scale
        )
        visible = (query_rows[:, None] == key_rows[None, :])[None]
        attention = jnp.exp(jnp.where(visible, logits - log_total[:, :, None], masked_value))
        attention_low = attention.astype(jnp.bfloat16)
        grad_heads = grad_seq.reshape(local_rows, heads_here, head_size)
        grad_attention = jnp.einsum(
            "qhe,khe->hqk", grad_heads, value_heads, preferred_element_type=jnp.float32
        )
        inner = jnp.sum(grad_attention * attention, axis=2, keepdims=True)
        grad_logits = (attention * (grad_attention - inner)).astype(jnp.bfloat16)
        grad_query = (
            jnp.einsum("hqk,khe->qhe", grad_logits, key_heads, preferred_element_type=jnp.float32)
            * score_scale
        )
        grad_key = (
            jnp.einsum("hqk,qhe->khe", grad_logits, query_seq, preferred_element_type=jnp.float32)
            * score_scale
        )
        grad_value = jnp.einsum(
            "hqk,qhe->khe", attention_low, grad_heads, preferred_element_type=jnp.float32
        )
        grad_pairs = lax.psum_scatter(
            jnp.concatenate(
                [
                    grad_key.reshape(lax.axis_size("seq") * local_rows, head_cols),
                    grad_value.reshape(lax.axis_size("seq") * local_rows, head_cols),
                ],
                axis=1,
            ).astype(jnp.bfloat16),
            "seq",
            scatter_dimension=0,
            tiled=True,
        ).astype(jnp.float32)
        return (unused, (grad_query.reshape(local_rows, head_cols), grad_pairs))

    _, (grad_queries, grad_pairs_all) = lax.scan(
        attend_backward, 0, (query_low, key_pairs, query_segs, key_segs, log_totals, grad_mixed)
    )
    _, query_pull = jax.vjp(head_norm, query_raw, head_float[0])
    grad_query_raw, grad_query_gain = query_pull(grad_queries.reshape(shape_heads))
    _, key_pull = jax.vjp(head_norm, key_raw, head_float[1])
    grad_key_raw, grad_key_gain = key_pull(grad_pairs_all[:, :, :head_cols].reshape(shape_heads))
    grad_projected = jnp.stack(
        [
            grad_query_raw.reshape(seq_here, local_rows, head_cols),
            grad_key_raw.reshape(seq_here, local_rows, head_cols),
            grad_pairs_all[:, :, head_cols:],
        ],
        axis=0,
    ).astype(jnp.bfloat16)
    grad_query_weight = jnp.einsum(
        "lsd,csle->cde", normed, grad_projected, preferred_element_type=jnp.float32
    )
    grad_normed = lax.psum(
        jnp.einsum(
            "csle,cde->lsd", grad_projected, query_weight, preferred_element_type=jnp.float32
        ).astype(jnp.bfloat16),
        "mlp",
    ).astype(jnp.float32)
    _, first_pull = jax.vjp(layer_norm, patch_float, gain_float[0], bias_float[0])
    grad_patch_norm, grad_gain_one, grad_bias_one = first_pull(grad_normed)
    grad_patches = (grad_resid + grad_patch_norm).astype(jnp.bfloat16)
    grad_scale = 1.0 / math.sqrt(lax.axis_size("dp") * seq_here * seq_len)
    term_qkv = grad_query_weight * grad_scale
    term_out = grad_out_weight * grad_scale
    term_up = up_projection_gradient * grad_scale
    term_down = grad_down * grad_scale
    term_gain = jnp.stack([grad_gain_one, grad_gain_two]) * grad_scale
    term_bias = jnp.stack([grad_bias_one, grad_bias_two]) * grad_scale
    term_head = jnp.stack([grad_query_gain, grad_key_gain]) * grad_scale
    summed = (
        lax.psum(term_qkv.astype(jnp.bfloat16), "seq").astype(jnp.float32),
        lax.psum(term_out.astype(jnp.bfloat16), "seq").astype(jnp.float32),
        lax.psum(term_up.astype(jnp.bfloat16), "seq").astype(jnp.float32),
        lax.psum(term_down.astype(jnp.bfloat16), "seq").astype(jnp.float32),
        lax.psum(term_gain.astype(jnp.bfloat16), "seq").astype(jnp.float32),
        lax.psum(term_bias.astype(jnp.bfloat16), "seq").astype(jnp.float32),
        lax.psum(term_head.astype(jnp.bfloat16), "seq").astype(jnp.float32),
    )
    shards = (
        lax.psum_scatter(
            summed[0].astype(jnp.bfloat16), "dp", scatter_dimension=1, tiled=True
        ).astype(jnp.float32),
        lax.psum_scatter(
            summed[1].astype(jnp.bfloat16), "dp", scatter_dimension=1, tiled=True
        ).astype(jnp.float32),
        lax.psum_scatter(
            summed[2].astype(jnp.bfloat16), "dp", scatter_dimension=0, tiled=True
        ).astype(jnp.float32),
        lax.psum_scatter(
            summed[3].astype(jnp.bfloat16), "dp", scatter_dimension=1, tiled=True
        ).astype(jnp.float32),
        lax.psum_scatter(
            summed[4].astype(jnp.bfloat16), "dp", scatter_dimension=1, tiled=True
        ).astype(jnp.float32),
        lax.psum_scatter(
            summed[5].astype(jnp.bfloat16), "dp", scatter_dimension=1, tiled=True
        ).astype(jnp.float32),
        lax.psum_scatter(
            summed[6].astype(jnp.bfloat16), "dp", scatter_dimension=2, tiled=True
        ).astype(jnp.float32),
    )
    return (
        out,
        grad_patches,
        shards[0],
        shards[1],
        shards[2],
        shards[3],
        shards[4],
        shards[5],
        shards[6],
    )


low = jnp.bfloat16
wide = jnp.float32
log2e = math.log2(math.e)
mask_weight = 128.0
query_block = 256
windows = (384, 512, 1024)
vmem_bytes = 56 * 1024 * 1024
hidden_chunk = 512
micros = {
    "qkv": 25,
    "attn_fwd": 22,
    "middle": 80,
    "attn_bwd": 60,
    "first_norm": 8,
    "place": 4,
}


def dot(left, right, left_dim=1, right_dim=0):
    return lax.dot_general(
        left, right, (((left_dim,), (right_dim,)), ((), ())), preferred_element_type=wide
    )


def params(count, vmem):
    return pltpu.CompilerParams(
        dimension_semantics=("arbitrary",) * count, vmem_limit_bytes=vmem
    )


def split_dot(values, ones_matrix):
    top = values.astype(low)
    rest = (values - top.astype(wide)).astype(low)
    return dot(jnp.concatenate([top, rest], axis=1), ones_matrix)


def load_pieces(info_ref, sets, scratch, sems):
    copies = []
    rows = scratch.shape[0] // 8
    for number, (pieces, first, count, target) in enumerate(sets):
        for index in range(8):
            if len(pieces) == 8:
                piece = pieces[index]
            else:
                piece = pieces[index % 2].at[index // 2]
            place = pl.multiple_of(info_ref[2 + index] * rows, rows)
            copies.append(
                pltpu.make_async_copy(
                    piece.at[pl.ds(0, rows), pl.ds(first, count)],
                    scratch.at[pl.ds(place, rows), pl.ds(target, count)],
                    sems.at[number, index],
                )
            )
    return copies


def load_shards(pairs_of, scratch, sems):
    copies = []
    rows = scratch.shape[0] // 8
    for number, (source, owner, first, count, target) in enumerate(pairs_of):
        for index in range(8):
            copies.append(
                pltpu.make_async_copy(
                    source.at[2 * index + owner, :, pl.ds(first, count)],
                    scratch.at[pl.ds(index * rows, rows), pl.ds(target, count)],
                    sems.at[number, index],
                )
            )
    return copies


def run_all(copies):
    for copy in copies:
        copy.start()
    for copy in copies:
        copy.wait()


def qkv_kernel(info_ref, mine_ref, got_ref, far_ref, gain_ref, bias_ref, hg_ref, mean_ref, *refs):
    pieces, refs = refs[:8], refs[8:]
    p_ref, rate_ref, ht_ref, w_ref, sems = refs
    sub = pl.program_id(1)

    @pl.when((pl.program_id(0) == 0) & (sub == 0))
    def _():
        run_all(load_pieces(info_ref, [(pieces, 0, w_ref.shape[1], 0)], w_ref, sems))

    first_core = info_ref[1] == 0
    moved = jnp.concatenate(
        [
            jnp.where(first_core, got_ref[0], far_ref[0]),
            jnp.where(first_core, far_ref[0], got_ref[0]),
        ],
        axis=0,
    )
    x = jnp.where(sub == info_ref[0], mine_ref[0], moved).astype(wide)
    centered = x - jnp.mean(x, axis=1, keepdims=True)
    variance = jnp.mean(centered * centered, axis=1, keepdims=True)
    h = (centered * lax.rsqrt(variance + norm_eps) * gain_ref[...] + bias_ref[...]).astype(low)
    ht_ref[...] = jnp.transpose(h)
    means = mean_ref[...]
    projected = dot(h, w_ref[...])
    for at in range(0, projected.shape[1], 128):
        raw = projected[:, at : at + 128]
        if at % 384 == 256:
            p_ref[0, :, at : at + 128] = raw.astype(low)
            continue
        inner = raw - split_dot(raw, means)
        rate = lax.rsqrt(dot((inner * inner).astype(low), means[:128]) + norm_eps)
        to = at // 384 * 256 + at % 384
        rate_ref[0, :, to : to + 128] = rate
        p_ref[0, :, at : at + 128] = (inner * rate * hg_ref[:, to : to + 128]).astype(low)


def attn_fwd_kernel(
    info_ref, start_ref, kind_ref, p_ref, aug_ref, side_ref, mine_ref, send_ref, inv_ref
):
    seq = pl.program_id(0)
    blocks = p_ref.shape[1] // query_block
    pairs = p_ref.shape[2] // 384
    lane = lax.broadcasted_iota(jnp.int32, (query_block, 128), 1)

    def step(block, carry):
        row = pl.multiple_of(block * query_block, query_block)
        which = seq * blocks + block

        def body(size):
            begin = pl.multiple_of(start_ref[which], 16)
            rows = pl.ds(row, query_block)
            span = pl.ds(begin, size)
            q_side = aug_ref[0, rows, :] * side_ref[...]
            k_side = aug_ref[0, span, :]
            ones = jnp.ones((size, 128), low)
            outcomes = []
            for pair in range(pairs):
                at = 384 * pair
                q_pair = p_ref[0, rows, at : at + 128]
                keys = jnp.concatenate([p_ref[0, span, at + 128 : at + 256], k_side], axis=1)
                values = jnp.concatenate([p_ref[0, span, at + 256 : at + 384], ones], axis=1)
                mixed = []
                for head in range(2):
                    mine = jnp.where(lane // 64 == head, q_pair, jnp.zeros_like(q_pair))
                    scores = dot(jnp.concatenate([mine, q_side], axis=1), keys, 1, 1)
                    mixed.append(dot(jnp.exp2(scores).astype(low), values))
                inverse = 1.0 / jnp.where(lane < 64, mixed[0][:, 128:], mixed[1][:, 128:])
                outcome = jnp.where(lane < 64, mixed[0][:, :128], mixed[1][:, :128]) * inverse
                outcomes.append(outcome.astype(low))
                inv_ref[0, rows, 128 * pair : 128 * pair + 128] = inverse
            outcome = jnp.concatenate(outcomes, axis=1)

            @pl.when(block % 2 == info_ref[1])
            def _():
                mine_ref[0, block // 2] = outcome

            @pl.when(block % 2 != info_ref[1])
            def _():
                send_ref[0, block // 2] = outcome

        for index, size in enumerate(windows):
            pl.when(kind_ref[which] == index)(partial(body, size))
        return carry

    lax.fori_loop(0, blocks, step, 0)


def attn_bwd_kernel(
    base,
    scale,
    first,
    final,
    info_ref,
    start_ref,
    kind_ref,
    p_ref,
    go_mine_ref,
    go_got_ref,
    o_mine_ref,
    o_send_ref,
    inv_ref,
    rate_ref,
    aug_ref,
    side_ref,
    hg_ref,
    mean_ref,
    ht_ref,
    *refs,
):
    pieces, refs = refs[:8], refs[8:]
    if not first:
        gw_in_ref, *refs = refs
    mine_ref, send_ref, gw_ref, gain_ref, *refs = refs
    gq_acc, gk_acc, gv_acc, g_all, gw_acc, w_ref, sems = refs
    step_id = pl.program_id(0)
    seq = step_id + base
    blocks = p_ref.shape[1] // query_block
    pairs = p_ref.shape[2] // 384
    lane = lax.broadcasted_iota(jnp.int32, (query_block, 128), 1)

    @pl.when(step_id == 0)
    def _():
        for copy in load_pieces(info_ref, [(pieces, 0, w_ref.shape[1], 0)], w_ref, sems):
            copy.start()
        gain_ref[...] = jnp.zeros_like(gain_ref)
        gw_acc[...] = jnp.zeros_like(gw_acc) if first else gw_in_ref[...]

    gk_acc[...] = jnp.zeros_like(gk_acc)
    gv_acc[...] = jnp.zeros_like(gv_acc)

    def step(block, carry):
        row = pl.multiple_of(block * query_block, query_block)
        which = seq * blocks + block

        def body(size):
            begin = pl.multiple_of(start_ref[which], 16)
            rows = pl.ds(row, query_block)
            span = pl.ds(begin, size)
            q_side = aug_ref[0, rows, :] * side_ref[...]
            k_side = aug_ref[0, span, :]
            near = block % 2 == info_ref[1]
            for pair in range(pairs):
                at = 384 * pair
                lanes = slice(128 * pair, 128 * pair + 128)
                q_pair = p_ref[0, rows, at : at + 128]
                k_pair = p_ref[0, span, at + 128 : at + 256]
                keys = jnp.concatenate([k_pair, k_side], axis=1)
                values = jnp.concatenate([p_ref[0, span, at + 256 : at + 384], k_side], axis=1)
                go = jnp.where(
                    near, go_mine_ref[0, block // 2, :, lanes], go_got_ref[0, block // 2, :, lanes]
                )
                o = jnp.where(
                    near, o_mine_ref[0, block // 2, :, lanes], o_send_ref[0, block // 2, :, lanes]
                )
                scaled = (go.astype(wide) * inv_ref[0, rows, lanes]).astype(low)
                product = scaled.astype(wide) * o.astype(wide)
                powers, grads, queries, pulls = [], [], [], []
                for head in range(2):
                    mine = lane // 64 == head
                    inner = jnp.sum(jnp.where(mine, product, 0.0), axis=1, keepdims=True)
                    one = inner.astype(low)
                    two = (inner - one.astype(wide)).astype(low)
                    three = (inner - one.astype(wide) - two.astype(wide)).astype(low)
                    none = jnp.zeros_like(q_pair)
                    go_side = jnp.where(
                        lane == 6,
                        -one,
                        jnp.where(lane == 7, -two, jnp.where(lane == 8, -three, none)),
                    )
                    q_mine = jnp.where(mine, q_pair, none)
                    go_mine = jnp.where(mine, scaled, none)
                    power = jnp.exp2(dot(keys, jnp.concatenate([q_mine, q_side], axis=1), 1, 1))
                    slope = dot(values, jnp.concatenate([go_mine, go_side], axis=1), 1, 1)
                    powers.append(power.astype(low))
                    grads.append((power * slope).astype(low))
                    queries.append(q_mine)
                    pulls.append(go_mine)
                gv_acc[span, lanes] += dot(
                    jnp.concatenate(powers, axis=1), jnp.concatenate(pulls, axis=0)
                )
                gk_acc[span, lanes] += dot(
                    jnp.concatenate(grads, axis=1), jnp.concatenate(queries, axis=0)
                )
                keys_turned = jnp.transpose(k_pair)
                turned = [dot(keys_turned[64 * i : 64 * i + 64], grads[i]) for i in range(2)]
                gq_acc[rows, lanes] = jnp.transpose(jnp.concatenate(turned, axis=0))

        for index, size in enumerate(windows):
            pl.when(kind_ref[which] == index)(partial(body, size))
        return carry

    lax.fori_loop(0, blocks, step, 0)
    means = mean_ref[...]
    for pair in range(pairs):
        lanes = slice(128 * pair, 128 * pair + 128)
        g_all[:, 384 * pair + 256 : 384 * pair + 384] = gv_acc[:, lanes].astype(low)
        for index, acc, factor, unscale in (
            (0, gq_acc, 0.125, 8.0 / log2e),
            (1, gk_acc, 1.0 / log2e, 1.0),
        ):
            to = slice(384 * pair + 128 * index, 384 * pair + 128 * index + 128)
            at = slice(256 * pair + 128 * index, 256 * pair + 128 * index + 128)
            gain = hg_ref[:, at]
            grad = acc[:, lanes] * factor
            normed = p_ref[0, :, to].astype(wide) * unscale
            weighted = grad * gain
            cross = grad * normed
            inner = split_dot(weighted, means)
            outer = split_dot(cross, means)
            g_all[:, to] = (
                rate_ref[0, :, at] * (weighted - inner - normed / gain * outer)
            ).astype(low)
            gain_ref[0:1, at] += jnp.sum(cross, axis=0, keepdims=True) / gain

    @pl.when(step_id == 0)
    def _():
        for copy in load_pieces(info_ref, [(pieces, 0, w_ref.shape[1], 0)], w_ref, sems):
            copy.wait()

    gw_acc[...] += dot(ht_ref[...], g_all[...])
    everything = dot(g_all[...], w_ref[...], 1, 1).astype(low)
    for block in range(blocks):
        result = everything[block * query_block : (block + 1) * query_block]

        @pl.when(block % 2 == info_ref[1])
        def _():
            mine_ref[0, block // 2] = result

        @pl.when(block % 2 != info_ref[1])
        def _():
            send_ref[0, block // 2] = result

    @pl.when(step_id == pl.num_programs(0) - 1)
    def _():
        if final:
            spread(info_ref, gw_acc, scale, gw_ref, None, 0, 0, gw_acc.shape[1])
        else:
            gw_ref[...] = gw_acc[...]


def spread(info_ref, acc, scale, mine_ref, other_ref, from_col, to_col, count):
    rows = mine_ref.shape[2]
    for side, ref in enumerate((mine_ref, other_ref)):
        if ref is None:
            continue
        for index in range(8):
            place = pl.multiple_of(info_ref[2 + index] * rows, rows)
            ref[index % 2, index // 2, :, to_col : to_col + count] = (
                acc[pl.ds(place, rows), from_col + side * count : from_col + (side + 1) * count]
                * scale
            ).astype(low)


def put_blocks(stage, acc, scale, owners, to_col, count):
    rows = stage.shape[1]
    for number, owner in enumerate(owners):
        for index in range(8):
            stage[2 * index + owner, :, to_col : to_col + count] = (
                acc[index * rows : (index + 1) * rows, number * count : (number + 1) * count]
                * scale
            ).astype(low)


def norm_back(values, grad, gain):
    centered = values - jnp.mean(values, axis=1, keepdims=True)
    rate = lax.rsqrt(jnp.mean(centered * centered, axis=1, keepdims=True) + norm_eps)
    normed = centered * rate
    weighted = grad * gain
    result = rate * (
        weighted
        - jnp.mean(weighted, axis=1, keepdims=True)
        - normed * jnp.mean(weighted * normed, axis=1, keepdims=True)
    )
    return result, normed


def gelu_parts(t):
    root = math.sqrt(2.0 / math.pi)
    square = t * t
    gate = 0.5 + 0.5 * jnp.tanh(t * (root + (root * 0.044715) * square))
    act = t * gate
    slope = gate + 2.0 * act * (1.0 - gate) * (root + (3.0 * root * 0.044715) * square)
    return act, slope


def middle_kernel(
    scale,
    chunks,
    info_ref,
    o_mine_ref,
    o_got_ref,
    mine_ref,
    got_ref,
    gy_ref,
    valid_ref,
    gain_ref,
    bias_ref,
    shards,
    keep_near_ref,
    keep_far_ref,
    send_near_ref,
    send_far_ref,
    gx_ref,
    go_mine_ref,
    go_send_ref,
    sums_ref,
    grads,
    out_grads,
    x2_all,
    h_all,
    ht_all,
    gy_all,
    gyt_all,
    out_all,
    gh_all,
    up_both,
    down_both,
    up_acc,
    down_acc,
    act_all,
    grad_all,
    wo_ref,
    wo_acc,
    stage,
    stage_out,
    weight_sems,
    stage_sem,
):
    phase = pl.program_id(0)
    r = pl.program_id(1)
    last = pl.num_programs(1) - 1
    cols = o_mine_ref.shape[3]
    part = o_mine_ref.shape[2]
    chunk = up_both.shape[2] // 2
    c = info_ref[1]
    first_half = info_ref[0] == 0

    def weight_copies(f, slot):
        begin = cols + f * 2 * chunk
        sems = weight_sems.at[slot]
        return load_shards(
            [(shards, m, begin, chunk, m * chunk) for m in range(2)], up_both.at[slot], sems
        ) + load_shards(
            [(shards, m, begin + chunk, chunk, m * chunk) for m in range(2)],
            down_both.at[slot],
            sems.at[pl.ds(2, 2)],
        )

    def stage_copy(f):
        return pltpu.make_async_copy(
            stage, grads.at[:, :, pl.ds(f * 2 * chunk, 2 * chunk)], stage_sem.at[0]
        )

    def both_heads():
        return jnp.concatenate(
            [o_mine_ref[0].reshape(2 * part, cols), o_got_ref[0].reshape(2 * part, cols)], axis=1
        )

    @pl.when((phase == 0) & (r == 0))
    def _():
        copies = load_shards(
            [(shards, c, 0, cols, 0), (shards, 1 - c, 0, cols, cols)], wo_ref, weight_sems.at[1]
        )
        run_all(copies)
        for copy in weight_copies(0, 0):
            copy.start()
        sums_ref[...] = jnp.zeros_like(sums_ref)

    @pl.when(phase == 0)
    def _():
        x = jnp.concatenate(
            [
                jnp.where(first_half, mine_ref[0], got_ref[0]),
                jnp.where(first_half, got_ref[0], mine_ref[0]),
            ],
            axis=0,
        ).astype(wide)
        x2 = x + dot(both_heads(), wo_ref[...], 1, 1)
        x2_all[r] = x2
        centered = x2 - jnp.mean(x2, axis=1, keepdims=True)
        variance = jnp.mean(centered * centered, axis=1, keepdims=True)
        h = (centered * lax.rsqrt(variance + norm_eps) * gain_ref[...] + bias_ref[...]).astype(low)
        h_all[r] = h
        ht_all[r] = jnp.transpose(h)
        gy = gy_ref[...]
        gy_all[r] = gy
        gyt_all[r] = jnp.transpose(gy)

    def mlp_step(f):
        slot = f % 2

        @pl.when(r == 0)
        def _():
            for copy in weight_copies(f, slot):
                copy.wait()
            if f + 1 < chunks:
                for copy in weight_copies(f + 1, 1 - slot):
                    copy.start()

        up_ref = up_both.at[slot]
        down_ref = down_both.at[slot]
        h = h_all[r]
        gy = gy_all[r]
        size = 512
        for at in range(0, 2 * chunk, size):
            act, slope = gelu_parts(dot(h, up_ref[:, at : at + size]))
            act_all[:, at : at + size] = act.astype(low)
            grad_all[:, at : at + size] = (dot(gy, down_ref[:, at : at + size]) * slope).astype(low)
        base = x2_all[r] if f == 0 else out_all[r]
        out_all[r] = base + dot(act_all[...], down_ref[...], 1, 1)
        back = dot(grad_all[...], up_ref[...], 1, 1)
        gh_all[r] = back if f == 0 else gh_all[r] + back

        @pl.when(r == 0)
        def _():
            up_acc[...] = dot(ht_all[r], grad_all[...])
            down_acc[...] = dot(gyt_all[r], act_all[...])

        @pl.when(r > 0)
        def _():
            up_acc[...] += dot(ht_all[r], grad_all[...])
            down_acc[...] += dot(gyt_all[r], act_all[...])

        @pl.when(r == last)
        def _():
            if f > 0:
                stage_copy(f - 1).wait()
            put_blocks(stage, up_acc, scale, (0, 1), 0, chunk)
            put_blocks(stage, down_acc, scale, (0, 1), chunk, chunk)
            stage_copy(f).start()

    for f in range(chunks):
        pl.when(phase == f + 1)(partial(mlp_step, f))

    @pl.when(phase == chunks + 1)
    def _():
        out = (out_all[r] * valid_ref[...][:, :1]).astype(low)
        keep = jnp.where(first_half, out[:part], out[part:])
        send = jnp.where(first_half, out[part:], out[:part])
        keep_near_ref[0] = jnp.where(c == 0, keep[:, :cols], keep[:, cols:])
        keep_far_ref[0] = jnp.where(c == 0, keep[:, cols:], keep[:, :cols])
        send_near_ref[0] = jnp.where(c == 0, send[:, :cols], send[:, cols:])
        send_far_ref[0] = jnp.where(c == 0, send[:, cols:], send[:, :cols])
        gh = gh_all[r]
        back, normed = norm_back(x2_all[r], gh, gain_ref[...])
        gx = gy_all[r].astype(wide) + back
        gx_ref[...] = gx
        gx_low = gx.astype(low)
        go = dot(gx_low, wo_ref[...]).astype(low)
        go_mine_ref[0] = go[:, :cols].reshape(2, part, cols)
        go_send_ref[0] = go[:, cols:].reshape(2, part, cols)
        turned = jnp.transpose(gx_low)
        sums_ref[0:1, :] += jnp.sum(gh * normed, axis=0, keepdims=True)
        sums_ref[1:2, :] += jnp.sum(gh, axis=0, keepdims=True)
        product = dot(turned, both_heads())

        @pl.when(r == 0)
        def _():
            wo_acc[...] = product

        @pl.when(r > 0)
        def _():
            wo_acc[...] += product

        @pl.when(r == last)
        def _():
            stage_copy(chunks - 1).wait()
            rows = stage_out.shape[3]
            for side in range(2):
                for index in range(8):
                    place = pl.multiple_of(info_ref[2 + index] * rows, rows)
                    stage_out[side, index % 2, index // 2] = (
                        wo_acc[pl.ds(place, rows), side * cols : (side + 1) * cols] * scale
                    ).astype(low)
            copy = pltpu.make_async_copy(stage_out, out_grads, stage_sem.at[1])
            copy.start()
            copy.wait()


def first_norm_kernel(
    info_ref, mine_ref, got_ref, a_ref, b_ref, gx2_ref, gain_ref, keep_ref, send_ref, sums_ref
):
    half = pl.program_id(1)
    x = jnp.where(half == info_ref[0], mine_ref[0], got_ref[0]).astype(wide)
    gh = a_ref[0, 0].astype(wide) + b_ref[0, 0].astype(wide)
    back, normed = norm_back(x, gh, gain_ref[...])
    out = (gx2_ref[...] + back).astype(low)

    @pl.when(half == info_ref[0])
    def _():
        keep_ref[0] = out

    @pl.when(half != info_ref[0])
    def _():
        send_ref[0] = out

    @pl.when((pl.program_id(0) == 0) & (half == 0))
    def _():
        sums_ref[...] = jnp.zeros_like(sums_ref)

    sums_ref[0:1, :] += jnp.sum(gh * normed, axis=0, keepdims=True)
    sums_ref[1:2, :] += jnp.sum(gh, axis=0, keepdims=True)


def place_kernel(plan, seqs, info_ref, *refs):
    sources, (out_ref, sems) = refs[: len(plan)], refs[len(plan) :]
    y, c = info_ref[0], info_ref[1]
    copies = []
    for number, (source, (own_y, own_c, begin)) in enumerate(zip(sources, plan)):
        at = seqs * (y if own_y else 1 - y) + begin
        copies.append(
            pltpu.make_async_copy(
                source,
                out_ref.at[pl.ds(at, source.shape[0]), c if own_c else 1 - c],
                sems.at[number],
            )
        )
    run_all(copies)


def shape_of(dims, kind=low):
    return jax.ShapeDtypeStruct(dims, kind)


def window_table(segs, blocks):
    length = segs.shape[1]
    pad_begin = jnp.sum((segs >= 0).astype(jnp.int32), axis=1, keepdims=True)
    begins = jnp.where(segs >= 0, segs, pad_begin)
    size = length // blocks
    firsts = begins[:, ::size]
    lasts = begins[:, size - 1 :: size]
    ends = jnp.sum((begins[:, None, :] <= lasts[:, :, None]).astype(jnp.int32), axis=2)
    reach = ends - firsts
    kinds = jnp.zeros_like(reach)
    spans = jnp.full_like(reach, windows[0])
    for index in range(1, len(windows)):
        larger = reach > windows[index - 1]
        kinds = jnp.where(larger, index, kinds)
        spans = jnp.where(larger, windows[index], spans)
    starts = jnp.minimum(firsts, length - spans)
    return starts.reshape(-1), kinds.reshape(-1)


def mask_columns(segs):
    codes = (segs + 16) // 16
    lane = jnp.arange(128, dtype=jnp.int32)
    bits = (codes[:, :, None] >> jnp.minimum(lane, 5)) & 1
    signs = (2 * bits - 1).astype(wide)
    return jnp.where(lane < 6, signs, jnp.where(lane < 9, 1.0, 0.0)).astype(low)


def swap(values, axis):
    return lax.ppermute(values, axis, [(0, 1), (1, 0)])


def in_order(index, mine, other, axis):
    return jnp.where(
        index == 0,
        jnp.concatenate([mine, other], axis=axis),
        jnp.concatenate([other, mine], axis=axis),
    )


def pick(values, index, axis):
    return lax.dynamic_index_in_dim(values, index, axis, keepdims=False)


def shift_far(values, step):
    return lax.ppermute(
        values,
        "dp",
        [(2 * ((z + step) % 4) + x, 2 * z + x) for z in range(4) for x in range(2)],
    )


def swap_x(values):
    return lax.ppermute(values, "dp", [(d, d ^ 1) for d in range(8)])


def gather_pieces(shard):
    pieces = []
    for step in range(4):
        piece = shard if step == 0 else shift_far(shard, step)
        pieces += [piece, swap_x(piece)]
    return pieces


class Reduce:
    def __init__(self, mine, other=None):
        self.mine = mine
        self.other = other
        self.got = None
        self.state = None
        self.phase = "core" if other is not None else "x"

    def advance(self):
        if self.phase == "core":
            self.state = self.got = swap(self.other, "mlp")
            self.phase = "x"
        elif self.phase == "x":
            far = self.mine[1]
            if self.got is not None:
                far = (far.astype(wide) + self.got[1].astype(wide)).astype(low)
            self.state = swap_x(far)
            self.phase = "z"
        elif self.phase == "z":
            total = self.mine[0].astype(wide) + self.state.astype(wide)
            if self.got is not None:
                total = total + self.got[0].astype(wide)
            low_total = total.astype(low)
            self.mine = total[0]
            self.state = [shift_far(low_total[step], 4 - step) for step in range(1, 4)]
            self.phase = "y"
        elif self.phase == "y":
            self.mine = self.mine + sum(part.astype(wide) for part in self.state)
            self.state = swap(self.mine.astype(low), "seq")
            self.phase = "end"
        elif self.phase == "end":
            self.mine = self.mine + self.state.astype(wide)
            self.state = None
            self.phase = "done"

    def result(self):
        while self.phase != "done":
            self.advance()
        return self.mine


def on_device_small(
    patches, segments, w_qkv, w_out, w_up, w_down, ln_gain, ln_bias, head_gain, cotangent
):
    half, seqs_all, width = patches.shape
    length = 2 * half
    seqs = seqs_all // 2
    cols = w_qkv.shape[2]
    part = half // 2
    y = lax.axis_index("seq")
    c = lax.axis_index("mlp")
    d = lax.axis_index("dp")
    dp_size = lax.axis_size("dp")
    scale = 1.0 / math.sqrt(dp_size * seqs_all * length)
    own_rows = seqs * half
    hidden = w_up.shape[1]
    shard_rows = width // dp_size
    places = jnp.stack(
        [2 * ((d // 2 + index // 2) % 4) + ((d % 2) ^ (index % 2)) for index in range(8)]
    )
    info = jnp.concatenate([jnp.stack([y, c]), places]).astype(jnp.int32)

    turned = jnp.transpose(patches, (1, 0, 2)).reshape(2, seqs, 2, part, width)
    got = swap(pick(pick(turned, 1 - y, 0), c, 1), "seq")
    far = swap(got, "mlp")
    turned = turned.reshape(seqs_all, half, width)
    small = jnp.concatenate(
        [
            ln_gain.astype(low),
            ln_bias.astype(low),
            head_gain.astype(low).reshape(1, -1),
            jnp.zeros((3, shard_rows), low),
        ]
    )
    small = jnp.pad(small, ((0, 8), (0, 3 * cols - shard_rows)))
    pairs = cols // 128
    w_in = jnp.transpose(w_qkv.astype(low).reshape(3, shard_rows, pairs, 128), (1, 2, 0, 3))
    w_in = w_in.reshape(shard_rows, 3 * cols)
    in_pieces = gather_pieces(
        jnp.concatenate(
            [w_in, small]
        )
    )
    small = [piece[shard_rows : shard_rows + 8, :shard_rows] for piece in in_pieces]
    chunk = hidden_chunk
    chunks = hidden // chunk
    up_low = w_up.astype(low)
    down_low = jnp.transpose(w_down.astype(low))
    parts = [jnp.transpose(w_out.astype(low))]
    for f in range(chunks):
        at = slice(f * chunk, (f + 1) * chunk)
        parts += [up_low[:, at], down_low[:, at]]

    def gather_shards(parts):
        return lax.all_gather(jnp.concatenate(parts, axis=1), ("dp", "mlp"), axis=0)

    shards = gather_shards(parts)

    order = (places[None, :] == jnp.arange(8)[:, None]).astype(low)
    small = jnp.einsum("nr,rkw->knw", order, jnp.stack(small), preferred_element_type=wide)
    gains = small[0:2].reshape(2, width)
    biases = small[2:4].reshape(2, width)
    head_gains = jnp.transpose(small[4].reshape(dp_size, 2, cols // 64, 64 // dp_size), (1, 2, 0, 3))
    head_gains = jnp.transpose(head_gains.reshape(2, pairs, 128), (1, 0, 2))
    key_scale = jnp.array([[[log2e / 8.0], [1.0]]], wide)
    head_scaled = (head_gains * key_scale).reshape(1, 2 * cols)
    head_gains = head_gains.reshape(1, 2 * cols)

    segs = lax.dynamic_slice_in_dim(jnp.transpose(segments), y * seqs, seqs, 0)
    cot = cotangent.reshape(2, part, seqs_all, cols)
    cot_other = swap(pick(cot, 1 - c, 0), "mlp")
    cot = jnp.transpose(in_order(c, pick(cot, c, 0), cot_other, 2), (1, 0, 2))
    cot = cot.reshape(2, seqs, part, width)
    cot_got = swap(pick(cot, 1 - y, 0), "seq")
    cot = in_order(y, pick(cot, y, 0)[:, None], cot_got[:, None], 1)
    valid = pick((segs >= 0).reshape(seqs, 2, 2, part), c, 2)
    gy = jnp.where(valid[..., None], cot, jnp.zeros_like(cot)).reshape(own_rows, width)
    valid = jnp.broadcast_to(valid.reshape(own_rows, 1).astype(wide), (own_rows, 128))

    starts, kinds = window_table(segs, length // query_block)
    aug = mask_columns(segs)
    lanes = jnp.arange(128)
    side = jnp.where(lanes < 6, mask_weight, jnp.where(lanes == 6, -6.0 * mask_weight, 0.0))
    side = side.astype(low)[None]
    means = jnp.where(lanes[:, None] // 64 == lanes[None] // 64, 1.0 / 64, 0.0).astype(low)
    means = jnp.concatenate([means, means])
    anywhere = pl.BlockSpec(memory_space=pl.ANY)

    def whole(dims):
        return pl.BlockSpec(dims, lambda *ids: (0,) * len(dims))

    def call(kernel, grid, in_specs, out_specs, out_shape, scratch, name, scalars, pins=(), share=1, vmem=vmem_bytes):
        work = int(micros[name] * 1150000000 / share)
        ends = scalars + len(in_specs)

        def unpinned(*refs):
            kernel(*refs[:ends], *refs[ends + len(pins) :])

        run = pl.pallas_call(
            unpinned,
            grid_spec=pltpu.PrefetchScalarGridSpec(
                num_scalar_prefetch=scalars,
                grid=grid,
                in_specs=in_specs + [anywhere] * len(pins),
                out_specs=out_specs,
                scratch_shapes=scratch,
            ),
            out_shape=out_shape,
            compiler_params=params(len(grid), vmem),
            cost_estimate=pl.CostEstimate(flops=work, bytes_accessed=1000000, transcendentals=0),
            name=name,
        )
        return lambda *operands: run(*operands, *pins)

    piece_sems = pltpu.SemaphoreType.DMA((4, 8))
    one_seq = pl.BlockSpec((1, part, width), lambda s, j, *_: (s, 0, 0))
    projected, rates, h1t = call(
        qkv_kernel,
        (seqs, 2),
        [
            pl.BlockSpec((1, half, width), lambda s, j, info: (seqs * info[0] + s, 0, 0)),
            one_seq,
            one_seq,
            whole((1, width)),
            whole((1, width)),
            whole((1, 2 * cols)),
            whole((256, 128)),
        ]
        + [anywhere] * 8,
        [
            pl.BlockSpec((1, half, 3 * cols), lambda s, j, *_: (s, j, 0)),
            pl.BlockSpec((1, half, 2 * cols), lambda s, j, *_: (s, j, 0)),
            pl.BlockSpec((width, half), lambda s, j, *_: (0, 2 * s + j)),
        ],
        [
            shape_of((seqs, length, 3 * cols)),
            shape_of((seqs, length, 2 * cols), wide),
            shape_of((width, seqs * length)),
        ],
        [pltpu.VMEM((width, 3 * cols), low), piece_sems],
        "qkv",
        1,
    )(info, turned, got, far, gains[:1], biases[:1], head_scaled, means, *in_pieces)
    def per_seq(*dims, base=0):
        return pl.BlockSpec((1,) + dims, lambda s, *_: (s + base,) + (0,) * len(dims))

    o_mine, o_send, inverse = call(
        attn_fwd_kernel,
        (seqs,),
        [per_seq(length, 3 * cols), per_seq(length, 128), whole((1, 128))],
        [per_seq(2, part, cols), per_seq(2, part, cols), per_seq(length, cols)],
        [shape_of((seqs, 2, part, cols))] * 2 + [shape_of((seqs, length, cols), wide)],
        [],
        "attn_fwd",
        3,
    )(info, starts, kinds, projected, aug, side)

    o_got = swap(o_send, "mlp")
    seq_of = seqs - 1
    final = chunks + 1

    def at_ends(p, r):
        return jnp.where((p == 0) | (p == final), r, seq_of)

    def at_start(p, r):
        return jnp.where(p == 0, r, seq_of)

    def at_final(p, r):
        return jnp.where(p == final, r, 0)

    heads_spec = pl.BlockSpec((1, 2, part, cols), lambda p, r, *_: (at_ends(p, r), 0, 0, 0))
    moved_spec = pl.BlockSpec((1, part, cols), lambda p, r, *_: (at_final(p, r), 0, 0))
    heads_out = pl.BlockSpec((1, 2, part, cols), lambda p, r, *_: (at_final(p, r), 0, 0, 0))
    by_seq_bf = pltpu.VMEM((seqs, half, width), low)
    by_seq_turned = pltpu.VMEM((seqs, width, half), low)
    by_seq_wide = pltpu.VMEM((seqs, half, width), wide)
    grad_shape = (16, shard_rows, 2 * hidden)
    keep_near, keep_far, send_near, send_far, gx2, go_mine, go_send, second_sums, grads, out_grads = call(
        partial(middle_kernel, scale, chunks),
        (chunks + 2, seqs),
        [
            heads_spec,
            heads_spec,
            pl.BlockSpec(
                (1, part, width), lambda p, r, info: (seqs * info[0] + at_start(p, r), info[1], 0)
            ),
            pl.BlockSpec((1, part, width), lambda p, r, *_: (at_start(p, r), 0, 0)),
            pl.BlockSpec((half, width), lambda p, r, *_: (at_start(p, r), 0)),
            pl.BlockSpec((half, 128), lambda p, r, *_: (at_final(p, r), 0)),
            whole((1, width)),
            whole((1, width)),
            anywhere,
        ],
        [
            moved_spec,
            moved_spec,
            moved_spec,
            moved_spec,
            pl.BlockSpec((half, width), lambda p, r, *_: (at_final(p, r), 0)),
            heads_out,
            heads_out,
            whole((8, width)),
            anywhere,
            anywhere,
        ],
        [
            shape_of((seqs, part, cols)),
            shape_of((seqs, part, cols)),
            shape_of((seqs, part, cols)),
            shape_of((seqs, part, cols)),
            shape_of((own_rows, width), wide),
            shape_of((seqs, 2, part, cols)),
            shape_of((seqs, 2, part, cols)),
            shape_of((8, width), wide),
            shape_of(grad_shape),
            shape_of((2, 2, 4, shard_rows, cols)),
        ],
        [by_seq_wide, by_seq_bf, by_seq_turned, by_seq_bf, by_seq_turned, by_seq_wide, by_seq_wide]
        + [pltpu.VMEM((2, width, 2 * chunk), low)] * 2
        + [pltpu.VMEM((width, 2 * chunk), wide)] * 2
        + [pltpu.VMEM((half, 2 * chunk), low)] * 2
        + [
            pltpu.VMEM((width, width), low),
            pltpu.VMEM((width, width), wide),
            pltpu.VMEM((16, shard_rows, 2 * chunk), low),
            pltpu.VMEM((2, 2, 4, shard_rows, cols), low),
            pltpu.SemaphoreType.DMA((2, 4, 8)),
            pltpu.SemaphoreType.DMA((2,)),
        ],
        "middle",
        1,
        vmem=62 * 1024 * 1024,
    )(info, o_mine, o_got, turned, got, gy, valid, gains[1:], biases[1:], shards)
    go_got = swap(go_send, "mlp")
    got_near = swap(send_near, "seq")
    got_far = swap(send_far, "seq")
    scattered = lax.psum_scatter(grads, ("dp", "mlp"), scatter_dimension=0, tiled=True)[0]
    sums = [Reduce(out_grads[0], out_grads[1])]

    def advance():
        pins = []
        for one in sums:
            pins += jax.tree.leaves(one.state)
            one.advance()
        return pins


    def attention_back(base, count, partial_sum, pins):
        first = partial_sum is None
        final = base + count == seqs
        shares = (2, 4, shard_rows, 3 * cols)
        carried = [] if first else [partial_sum]
        return call(
            partial(attn_bwd_kernel, base, scale, first, final),
            (count,),
            [per_seq(length, 3 * cols, base=base)]
            + [per_seq(2, part, cols, base=base)] * 4
            + [
                per_seq(length, cols, base=base),
                per_seq(length, 2 * cols, base=base),
                per_seq(length, 128, base=base),
                whole((1, 128)),
                whole((1, 2 * cols)),
                whole((256, 128)),
                pl.BlockSpec((width, length), lambda s, *_: (0, s + base)),
            ]
            + [anywhere] * 8
            + [whole((width, 3 * cols))] * len(carried),
            [per_seq(2, part, width)] * 2
            + [whole(shares if final else (width, 3 * cols)), whole((8, 2 * cols))],
            [shape_of((count, 2, part, width))] * 2
            + [shape_of(shares) if final else shape_of((width, 3 * cols), wide)]
            + [shape_of((8, 2 * cols), wide)],
            [pltpu.VMEM((length, cols), wide)] * 3
            + [
                pltpu.VMEM((length, 3 * cols), low),
                pltpu.VMEM((width, 3 * cols), wide),
                pltpu.VMEM((width, 3 * cols), low),
                piece_sems,
            ],
            "attn_bwd",
            3,
            pins,
            seqs / count,
        )(
            info, starts, kinds, projected, go_mine, go_got, o_mine, o_send, inverse, rates,
            aug, side, head_gains, means, h1t, *in_pieces, *carried,
        )

    def first_back(base, count, mine, got_part, pins):
        here = pl.BlockSpec((1, 1, part, width), lambda s, h, *_: (s, h, 0, 0))
        moved = pl.BlockSpec((1, part, width), lambda s, h, *_: (s, 0, 0))
        return call(
            first_norm_kernel,
            (count, 2),
            [
                pl.BlockSpec(
                    (1, part, width), lambda s, h, info: (seqs * info[0] + s + base, info[1], 0)
                ),
                pl.BlockSpec((1, part, width), lambda s, h, *_: (s + base, 0, 0)),
                here,
                here,
                pl.BlockSpec((part, width), lambda s, h, *_: (2 * (s + base) + h, 0)),
                whole((1, width)),
            ],
            [moved, moved, whole((8, width))],
            [shape_of((count, part, width))] * 2 + [shape_of((8, width), wide)],
            [],
            "first_norm",
            1,
            pins,
            seqs / count,
        )(info, turned, got, mine, got_part, gx2, gains[:1])

    def place(sources, plan, feature_count):
        return call(
            partial(place_kernel, plan, seqs),
            (1,),
            [anywhere] * len(plan),
            whole((seqs_all, 2, part, feature_count)),
            shape_of((seqs_all, 2, part, feature_count)),
            [pltpu.SemaphoreType.DMA((len(plan),))],
            "place",
            1,
        )(info, *sources)

    early = seqs - 1
    pins = advance()
    mine_a, send_a, partial_sum, head_sums_a = attention_back(0, early, None, pins)
    far_a = swap(send_a, "mlp")
    keep_a, give_a, norm_sums_a = first_back(0, early, mine_a, far_a, ())
    got_a = swap(give_a, "seq")
    keep_core_a = swap(keep_a, "mlp")
    keep_core, got_core = swap(keep_far, "mlp"), swap(got_far, "mlp")
    pins = advance() + [got_near, got_far, keep_a]
    mine_b, send_b, gw_in, head_sums_b = attention_back(early, 1, partial_sum, pins)
    far_b = swap(send_b, "mlp")
    in_sums = Reduce(gw_in)
    sums.append(in_sums)
    pins = advance() + [got_a, keep_core_a]
    keep_b, give_b, norm_sums_b = first_back(early, 1, mine_b, far_b, pins)
    first_sums = norm_sums_a + norm_sums_b
    head_sums = head_sums_a + head_sums_b

    plan = [(True, True, 0), (True, False, 0), (False, True, 0), (False, False, 0)]
    out = place([keep_near, keep_core, got_near, got_core], plan, cols)
    out = jnp.transpose(out.reshape(seqs_all, half, cols), (1, 0, 2))
    got_b = swap(give_b, "seq")
    late = [(own_y, own_c, early) for own_y, own_c, _ in plan]
    grad_patches = place(
        [keep_a, keep_core_a, got_a, swap(got_a, "mlp")]
        + [keep_b, swap(keep_b, "mlp"), got_b, swap(got_b, "mlp")],
        plan + late,
        width,
    )
    grad_patches = jnp.transpose(grad_patches.reshape(seqs_all, half, width), (1, 0, 2))

    scattered = scattered.astype(wide) + swap(scattered, "seq").astype(wide)
    gw_up = jnp.concatenate(
        [scattered[:, 2 * f * chunk : (2 * f + 1) * chunk] for f in range(chunks)], axis=1
    )
    gw_down = jnp.concatenate(
        [scattered[:, (2 * f + 1) * chunk : (2 * f + 2) * chunk] for f in range(chunks)], axis=1
    )
    gw_out = sums[0].result()
    gw_in = in_sums.result()
    gw_in = gw_in.reshape(shard_rows, pairs, 3, 128)
    gw_in = jnp.transpose(gw_in, (2, 0, 1, 3)).reshape(3, shard_rows, cols)
    norms = jnp.concatenate([first_sums[:2], second_sums[:2]]) * scale
    norms = norms + swap(norms, "mlp")
    heads = jnp.transpose(head_sums[0].reshape(pairs, 2, 128), (1, 0, 2)).reshape(2, cols) * scale
    small = jnp.concatenate([norms, heads.reshape(1, width)])
    small = small + swap(small, "seq")
    for bit in (1, 2, 4):
        small = small + lax.ppermute(small, "dp", [(i, i ^ bit) for i in range(8)])
    norms = lax.dynamic_slice_in_dim(small[:4], d * shard_rows, shard_rows, 1)
    heads = small[4].reshape(2, cols // 64, 64)
    heads = lax.dynamic_slice_in_dim(heads, d * (64 // dp_size), 64 // dp_size, 2)
    return (
        out,
        grad_patches,
        gw_in,
        jnp.transpose(gw_out),
        gw_up,
        jnp.transpose(gw_down),
        norms[0::2],
        norms[1::2],
        heads,
    )


def solution(mesh):
    shape = dict(mesh.shape)
    small = shape["seq"] == 2 and shape["mlp"] == 2 and shape["dp"] == 8
    return jax.shard_map(
        on_device_small if small else on_device,
        mesh=mesh,
        in_specs=(
            P("seq", "dp", None),
            P(None, "dp"),
            P(None, "dp", "mlp"),
            P("mlp", "dp"),
            P("dp", "mlp"),
            P("mlp", "dp"),
            P(None, "dp"),
            P(None, "dp"),
            P(None, "mlp", "dp"),
            P("seq", "dp", "mlp"),
        ),
        out_specs=(
            P("seq", "dp", "mlp"),
            P("seq", "dp", None),
            P(None, "dp", "mlp"),
            P("mlp", "dp"),
            P("dp", "mlp"),
            P("mlp", "dp"),
            P(None, "dp"),
            P(None, "dp"),
            P(None, "mlp", "dp"),
        ),
        check_vma=False,
    )
```

```python
from functools import partial
import math

import jax
import jax.numpy as jnp
from jax import lax
from jax.experimental import pallas as pl
from jax.experimental.pallas import tpu as pltpu
from jax.sharding import PartitionSpec as P

norm_eps = 1e-06
masked_value = -1e30


def layer_norm(values, gain_row, bias_row):
    average = jnp.mean(values, axis=-1, keepdims=True)
    centered = values - average
    variance = jnp.mean(centered * centered, axis=-1, keepdims=True)
    return centered * lax.rsqrt(variance + norm_eps) * gain_row + bias_row


def head_norm(values, gain_rows):
    average = jnp.mean(values, axis=-1, keepdims=True)
    centered = values - average
    variance = jnp.mean(centered * centered, axis=-1, keepdims=True)
    return centered * lax.rsqrt(variance + norm_eps) * gain_rows


def on_device(
    patches, segments, w_qkv, w_out, w_up, w_down, ln_gain, ln_bias, head_gain, cotangent
):
    (
        query_weight,
        out_weight,
        up_projection_weight,
        down_projection_weight,
        norm_gains,
        norm_biases,
        head_gains,
    ) = (
        lax.all_gather(w_qkv.astype(jnp.bfloat16), "dp", axis=1, tiled=True),
        lax.all_gather(w_out.astype(jnp.bfloat16), "dp", axis=1, tiled=True),
        lax.all_gather(w_up.astype(jnp.bfloat16), "dp", axis=0, tiled=True),
        lax.all_gather(w_down.astype(jnp.bfloat16), "dp", axis=1, tiled=True),
        lax.all_gather(ln_gain.astype(jnp.bfloat16), "dp", axis=1, tiled=True),
        lax.all_gather(ln_bias.astype(jnp.bfloat16), "dp", axis=1, tiled=True),
        lax.all_gather(head_gain.astype(jnp.bfloat16), "dp", axis=2, tiled=True),
    )
    local_rows = patches.shape[0]
    seq_here = patches.shape[1]
    width = patches.shape[2]
    head_cols = query_weight.shape[2]
    heads_here = head_gains.shape[1]
    head_size = head_gains.shape[2]
    seq_len = local_rows * lax.axis_size("seq")
    feature_cols = width // lax.axis_size("mlp")
    score_scale = head_size ** (-0.5)
    gain_float = norm_gains.astype(jnp.float32)
    bias_float = norm_biases.astype(jnp.float32)
    head_float = head_gains.astype(jnp.float32)
    seg_here = lax.dynamic_slice_in_dim(segments, lax.axis_index("seq") * local_rows, local_rows, 0)
    valid_mask = (seg_here >= 0).astype(jnp.float32)[:, :, None]
    query_segs = jnp.transpose(seg_here)
    key_segs = jnp.transpose(segments)
    patch_float = patches.astype(jnp.float32)
    normed = layer_norm(patch_float, gain_float[0], bias_float[0]).astype(jnp.bfloat16)
    projected = jnp.einsum(
        "lsd,cde->csle", normed, query_weight, preferred_element_type=jnp.float32
    )
    shape_heads = (seq_here, local_rows, heads_here, head_size)
    query_raw = projected[0].reshape(shape_heads)
    key_raw = projected[1].reshape(shape_heads)
    query_low = head_norm(query_raw, head_float[0]).astype(jnp.bfloat16)
    key_low = head_norm(key_raw, head_float[1]).astype(jnp.bfloat16)
    value_low = projected[2].astype(jnp.bfloat16)
    key_pairs = jnp.concatenate(
        [key_low.reshape(seq_here, local_rows, head_cols), value_low], axis=2
    )

    def split_pairs(gathered):
        key_heads = gathered[:, :head_cols].reshape(gathered.shape[0], heads_here, head_size)
        value_heads = gathered[:, head_cols:].reshape(gathered.shape[0], heads_here, head_size)
        return (key_heads, value_heads)

    def attend_forward(unused, inputs_seq):
        query_seq, pairs_seq, query_rows, key_rows = inputs_seq
        gathered = lax.all_gather(pairs_seq, "seq", axis=0, tiled=True)
        key_heads, value_heads = split_pairs(gathered)
        logits = (
            jnp.einsum("qhe,khe->hqk", query_seq, key_heads, preferred_element_type=jnp.float32)
            * score_scale
        )
        visible = (query_rows[:, None] == key_rows[None, :])[None]
        masked = jnp.where(visible, logits, masked_value)
        largest = jnp.max(masked, axis=2, keepdims=True)
        powered = jnp.exp(masked - largest)
        totals = jnp.sum(powered, axis=2, keepdims=True)
        attention = (powered / totals).astype(jnp.bfloat16)
        mixed = jnp.einsum(
            "hqk,khe->qhe", attention, value_heads, preferred_element_type=jnp.float32
        )
        log_total = (largest + jnp.log(totals))[:, :, 0]
        return (unused, (mixed.astype(jnp.bfloat16).reshape(local_rows, head_cols), log_total))

    _, (attn_heads, log_totals) = lax.scan(
        attend_forward, 0, (query_low, key_pairs, query_segs, key_segs)
    )
    attn_part = jnp.einsum(
        "slf,fd->lsd", attn_heads, out_weight, preferred_element_type=jnp.float32
    )
    attn_mine = lax.psum_scatter(
        attn_part.astype(jnp.bfloat16), "mlp", scatter_dimension=2, tiled=True
    ).astype(jnp.float32)
    patch_mine = lax.dynamic_slice_in_dim(
        patch_float, lax.axis_index("mlp") * feature_cols, feature_cols, 2
    )
    resid_mine = patch_mine + attn_mine
    residual = lax.all_gather(resid_mine.astype(jnp.bfloat16), "mlp", axis=2, tiled=True).astype(
        resid_mine.dtype
    )
    second_normalized = layer_norm(residual, gain_float[1], bias_float[1]).astype(jnp.bfloat16)
    hidden_pre = jnp.einsum(
        "own,nr->owr", second_normalized, up_projection_weight, preferred_element_type=jnp.float32
    )
    mlp_activation = jax.nn.gelu(hidden_pre, approximate=True).astype(jnp.bfloat16)
    branch_part = jnp.einsum(
        "ruo,oe->rue", mlp_activation, down_projection_weight, preferred_element_type=jnp.float32
    )
    branch_mine = lax.psum_scatter(
        branch_part.astype(jnp.bfloat16), "mlp", scatter_dimension=2, tiled=True
    ).astype(jnp.float32)
    out = (valid_mask * (resid_mine + branch_mine)).astype(jnp.bfloat16)
    cot_full = lax.all_gather(cotangent, "mlp", axis=2, tiled=True)
    grad_out = valid_mask * cot_full.astype(jnp.float32)
    output_gradient_reduced = grad_out.astype(jnp.bfloat16)
    grad_down = jnp.einsum(
        "xgr,xge->re", mlp_activation, output_gradient_reduced, preferred_element_type=jnp.float32
    )
    grad_act = jnp.einsum(
        "mit,nt->min",
        output_gradient_reduced,
        down_projection_weight,
        preferred_element_type=jnp.float32,
    )
    _, gelu_pull = jax.vjp(partial(jax.nn.gelu, approximate=True), hidden_pre)
    hidden_gradient = gelu_pull(grad_act)[0].astype(jnp.bfloat16)
    up_projection_gradient = jnp.einsum(
        "gih,giv->hv", second_normalized, hidden_gradient, preferred_element_type=jnp.float32
    )
    grad_normed_two = lax.psum(
        jnp.einsum(
            "vwb,kb->vwk", hidden_gradient, up_projection_weight, preferred_element_type=jnp.float32
        ).astype(jnp.bfloat16),
        "mlp",
    ).astype(jnp.float32)
    _, second_pull = jax.vjp(layer_norm, residual, gain_float[1], bias_float[1])
    grad_resid_norm, grad_gain_two, grad_bias_two = second_pull(grad_normed_two)
    grad_resid = grad_out + grad_resid_norm
    grad_resid_low = grad_resid.astype(jnp.bfloat16)
    grad_out_weight = jnp.einsum(
        "slf,lsd->fd", attn_heads, grad_resid_low, preferred_element_type=jnp.float32
    )
    grad_mixed = jnp.einsum(
        "lsd,fd->slf", grad_resid_low, out_weight, preferred_element_type=jnp.float32
    ).astype(jnp.bfloat16)

    def attend_backward(unused, inputs_seq):
        query_seq, pairs_seq, query_rows, key_rows, log_total, grad_seq = inputs_seq
        gathered = lax.all_gather(pairs_seq, "seq", axis=0, tiled=True)
        key_heads, value_heads = split_pairs(gathered)
        logits = (
            jnp.einsum("qhe,khe->hqk", query_seq, key_heads, preferred_element_type=jnp.float32)
            * score_scale
        )
        visible = (query_rows[:, None] == key_rows[None, :])[None]
        attention = jnp.exp(jnp.where(visible, logits - log_total[:, :, None], masked_value))
        attention_low = attention.astype(jnp.bfloat16)
        grad_heads = grad_seq.reshape(local_rows, heads_here, head_size)
        grad_attention = jnp.einsum(
            "qhe,khe->hqk", grad_heads, value_heads, preferred_element_type=jnp.float32
        )
        inner = jnp.sum(grad_attention * attention, axis=2, keepdims=True)
        grad_logits = (attention * (grad_attention - inner)).astype(jnp.bfloat16)
        grad_query = (
            jnp.einsum("hqk,khe->qhe", grad_logits, key_heads, preferred_element_type=jnp.float32)
            * score_scale
        )
        grad_key = (
            jnp.einsum("hqk,qhe->khe", grad_logits, query_seq, preferred_element_type=jnp.float32)
            * score_scale
        )
        grad_value = jnp.einsum(
            "hqk,qhe->khe", attention_low, grad_heads, preferred_element_type=jnp.float32
        )
        grad_pairs = lax.psum_scatter(
            jnp.concatenate(
                [
                    grad_key.reshape(lax.axis_size("seq") * local_rows, head_cols),
                    grad_value.reshape(lax.axis_size("seq") * local_rows, head_cols),
                ],
                axis=1,
            ).astype(jnp.bfloat16),
            "seq",
            scatter_dimension=0,
            tiled=True,
        ).astype(jnp.float32)
        return (unused, (grad_query.reshape(local_rows, head_cols), grad_pairs))

    _, (grad_queries, grad_pairs_all) = lax.scan(
        attend_backward, 0, (query_low, key_pairs, query_segs, key_segs, log_totals, grad_mixed)
    )
    _, query_pull = jax.vjp(head_norm, query_raw, head_float[0])
    grad_query_raw, grad_query_gain = query_pull(grad_queries.reshape(shape_heads))
    _, key_pull = jax.vjp(head_norm, key_raw, head_float[1])
    grad_key_raw, grad_key_gain = key_pull(grad_pairs_all[:, :, :head_cols].reshape(shape_heads))
    grad_projected = jnp.stack(
        [
            grad_query_raw.reshape(seq_here, local_rows, head_cols),
            grad_key_raw.reshape(seq_here, local_rows, head_cols),
            grad_pairs_all[:, :, head_cols:],
        ],
        axis=0,
    ).astype(jnp.bfloat16)
    grad_query_weight = jnp.einsum(
        "lsd,csle->cde", normed, grad_projected, preferred_element_type=jnp.float32
    )
    grad_normed = lax.psum(
        jnp.einsum(
            "csle,cde->lsd", grad_projected, query_weight, preferred_element_type=jnp.float32
        ).astype(jnp.bfloat16),
        "mlp",
    ).astype(jnp.float32)
    _, first_pull = jax.vjp(layer_norm, patch_float, gain_float[0], bias_float[0])
    grad_patch_norm, grad_gain_one, grad_bias_one = first_pull(grad_normed)
    grad_patches = (grad_resid + grad_patch_norm).astype(jnp.bfloat16)
    grad_scale = 1.0 / math.sqrt(lax.axis_size("dp") * seq_here * seq_len)
    term_qkv = grad_query_weight * grad_scale
    term_out = grad_out_weight * grad_scale
    term_up = up_projection_gradient * grad_scale
    term_down = grad_down * grad_scale
    term_gain = jnp.stack([grad_gain_one, grad_gain_two]) * grad_scale
    term_bias = jnp.stack([grad_bias_one, grad_bias_two]) * grad_scale
    term_head = jnp.stack([grad_query_gain, grad_key_gain]) * grad_scale
    summed = (
        lax.psum(term_qkv.astype(jnp.bfloat16), "seq").astype(jnp.float32),
        lax.psum(term_out.astype(jnp.bfloat16), "seq").astype(jnp.float32),
        lax.psum(term_up.astype(jnp.bfloat16), "seq").astype(jnp.float32),
        lax.psum(term_down.astype(jnp.bfloat16), "seq").astype(jnp.float32),
        lax.psum(term_gain.astype(jnp.bfloat16), "seq").astype(jnp.float32),
        lax.psum(term_bias.astype(jnp.bfloat16), "seq").astype(jnp.float32),
        lax.psum(term_head.astype(jnp.bfloat16), "seq").astype(jnp.float32),
    )
    shards = (
        lax.psum_scatter(
            summed[0].astype(jnp.bfloat16), "dp", scatter_dimension=1, tiled=True
        ).astype(jnp.float32),
        lax.psum_scatter(
            summed[1].astype(jnp.bfloat16), "dp", scatter_dimension=1, tiled=True
        ).astype(jnp.float32),
        lax.psum_scatter(
            summed[2].astype(jnp.bfloat16), "dp", scatter_dimension=0, tiled=True
        ).astype(jnp.float32),
        lax.psum_scatter(
            summed[3].astype(jnp.bfloat16), "dp", scatter_dimension=1, tiled=True
        ).astype(jnp.float32),
        lax.psum_scatter(
            summed[4].astype(jnp.bfloat16), "dp", scatter_dimension=1, tiled=True
        ).astype(jnp.float32),
        lax.psum_scatter(
            summed[5].astype(jnp.bfloat16), "dp", scatter_dimension=1, tiled=True
        ).astype(jnp.float32),
        lax.psum_scatter(
            summed[6].astype(jnp.bfloat16), "dp", scatter_dimension=2, tiled=True
        ).astype(jnp.float32),
    )
    return (
        out,
        grad_patches,
        shards[0],
        shards[1],
        shards[2],
        shards[3],
        shards[4],
        shards[5],
        shards[6],
    )


low = jnp.bfloat16
wide = jnp.float32
log2e = math.log2(math.e)
mask_weight = 128.0
query_block = 256
windows = (384, 512, 1024)
vmem_bytes = 56 * 1024 * 1024
hidden_chunk = 512
micros = {
    "qkv": 25,
    "attn_fwd": 22,
    "middle": 80,
    "attn_bwd": 75,
    "first_norm": 8,
    "place": 4,
}


def dot(left, right, left_dim=1, right_dim=0):
    return lax.dot_general(
        left, right, (((left_dim,), (right_dim,)), ((), ())), preferred_element_type=wide
    )


def params(count, vmem):
    return pltpu.CompilerParams(
        dimension_semantics=("arbitrary",) * count, vmem_limit_bytes=vmem
    )


def split_dot(values, ones_matrix):
    top = values.astype(low)
    rest = (values - top.astype(wide)).astype(low)
    return dot(jnp.concatenate([top, rest], axis=1), ones_matrix)


def load_pieces(info_ref, sets, scratch, sems):
    copies = []
    rows = scratch.shape[0] // 8
    for number, (pieces, first, count, target) in enumerate(sets):
        for index in range(8):
            if len(pieces) == 8:
                piece = pieces[index]
            else:
                piece = pieces[index % 2].at[index // 2]
            place = pl.multiple_of(info_ref[2 + index] * rows, rows)
            copies.append(
                pltpu.make_async_copy(
                    piece.at[pl.ds(0, rows), pl.ds(first, count)],
                    scratch.at[pl.ds(place, rows), pl.ds(target, count)],
                    sems.at[number, index],
                )
            )
    return copies


def load_shards(pairs_of, scratch, sems):
    copies = []
    rows = scratch.shape[0] // 8
    for number, (source, owner, first, count, target) in enumerate(pairs_of):
        for index in range(8):
            copies.append(
                pltpu.make_async_copy(
                    source.at[2 * index + owner, :, pl.ds(first, count)],
                    scratch.at[pl.ds(index * rows, rows), pl.ds(target, count)],
                    sems.at[number, index],
                )
            )
    return copies


def run_all(copies):
    for copy in copies:
        copy.start()
    for copy in copies:
        copy.wait()


def qkv_kernel(info_ref, mine_ref, got_ref, far_ref, gain_ref, bias_ref, hg_ref, mean_ref, *refs):
    pieces, refs = refs[:8], refs[8:]
    p_ref, rate_ref, ht_ref, w_ref, sems = refs
    sub = pl.program_id(1)

    @pl.when((pl.program_id(0) == 0) & (sub == 0))
    def _():
        run_all(load_pieces(info_ref, [(pieces, 0, w_ref.shape[1], 0)], w_ref, sems))

    first_core = info_ref[1] == 0
    moved = jnp.concatenate(
        [
            jnp.where(first_core, got_ref[0], far_ref[0]),
            jnp.where(first_core, far_ref[0], got_ref[0]),
        ],
        axis=0,
    )
    x = jnp.where(sub == info_ref[0], mine_ref[0], moved).astype(wide)
    centered = x - jnp.mean(x, axis=1, keepdims=True)
    variance = jnp.mean(centered * centered, axis=1, keepdims=True)
    h = (centered * lax.rsqrt(variance + norm_eps) * gain_ref[...] + bias_ref[...]).astype(low)
    ht_ref[...] = jnp.transpose(h)
    means = mean_ref[...]
    projected = dot(h, w_ref[...])
    for at in range(0, projected.shape[1], 128):
        raw = projected[:, at : at + 128]
        if at % 384 == 256:
            p_ref[0, :, at : at + 128] = raw.astype(low)
            continue
        inner = raw - split_dot(raw, means)
        rate = lax.rsqrt(dot((inner * inner).astype(low), means[:128]) + norm_eps)
        to = at // 384 * 256 + at % 384
        rate_ref[0, :, to : to + 128] = rate
        p_ref[0, :, at : at + 128] = (inner * rate * hg_ref[:, to : to + 128]).astype(low)


def attn_fwd_kernel(
    info_ref, start_ref, kind_ref, p_ref, aug_ref, side_ref, mine_ref, send_ref, inv_ref
):
    seq = pl.program_id(0)
    blocks = p_ref.shape[1] // query_block
    pairs = p_ref.shape[2] // 384
    lane = lax.broadcasted_iota(jnp.int32, (query_block, 128), 1)

    def step(block, carry):
        row = pl.multiple_of(block * query_block, query_block)
        which = seq * blocks + block

        def body(size):
            begin = pl.multiple_of(start_ref[which], 16)
            rows = pl.ds(row, query_block)
            span = pl.ds(begin, size)
            q_side = aug_ref[0, rows, :] * side_ref[...]
            k_side = aug_ref[0, span, :]
            ones = jnp.ones((size, 128), low)
            outcomes = []
            for pair in range(pairs):
                at = 384 * pair
                q_pair = p_ref[0, rows, at : at + 128]
                keys = jnp.concatenate([p_ref[0, span, at + 128 : at + 256], k_side], axis=1)
                values = jnp.concatenate([p_ref[0, span, at + 256 : at + 384], ones], axis=1)
                mixed = []
                for head in range(2):
                    mine = jnp.where(lane // 64 == head, q_pair, jnp.zeros_like(q_pair))
                    scores = dot(jnp.concatenate([mine, q_side], axis=1), keys, 1, 1)
                    mixed.append(dot(jnp.exp2(scores).astype(low), values))
                inverse = 1.0 / jnp.where(lane < 64, mixed[0][:, 128:], mixed[1][:, 128:])
                outcome = jnp.where(lane < 64, mixed[0][:, :128], mixed[1][:, :128]) * inverse
                outcomes.append(outcome.astype(low))
                inv_ref[0, rows, 128 * pair : 128 * pair + 128] = inverse
            outcome = jnp.concatenate(outcomes, axis=1)

            @pl.when(block % 2 == info_ref[1])
            def _():
                mine_ref[0, block // 2] = outcome

            @pl.when(block % 2 != info_ref[1])
            def _():
                send_ref[0, block // 2] = outcome

        for index, size in enumerate(windows):
            pl.when(kind_ref[which] == index)(partial(body, size))
        return carry

    lax.fori_loop(0, blocks, step, 0)


def attn_bwd_kernel(
    base,
    scale,
    first,
    final,
    info_ref,
    start_ref,
    kind_ref,
    p_ref,
    go_mine_ref,
    go_got_ref,
    o_mine_ref,
    o_send_ref,
    inv_ref,
    rate_ref,
    aug_ref,
    side_ref,
    hg_ref,
    mean_ref,
    ht_ref,
    *refs,
):
    pieces, refs = refs[:8], refs[8:]
    if not first:
        gw_in_ref, *refs = refs
    mine_ref, send_ref, gw_ref, gain_ref, *refs = refs
    gq_acc, gk_acc, gv_acc, g_all, gw_acc, w_ref, sems = refs
    step_id = pl.program_id(0)
    seq = step_id + base
    blocks = p_ref.shape[1] // query_block
    pairs = p_ref.shape[2] // 384
    lane = lax.broadcasted_iota(jnp.int32, (query_block, 128), 1)

    @pl.when(step_id == 0)
    def _():
        for copy in load_pieces(info_ref, [(pieces, 0, w_ref.shape[1], 0)], w_ref, sems):
            copy.start()
        gain_ref[...] = jnp.zeros_like(gain_ref)
        gw_acc[...] = jnp.zeros_like(gw_acc) if first else gw_in_ref[...]

    gk_acc[...] = jnp.zeros_like(gk_acc)
    gv_acc[...] = jnp.zeros_like(gv_acc)

    def step(block, carry):
        row = pl.multiple_of(block * query_block, query_block)
        which = seq * blocks + block

        def body(size):
            begin = pl.multiple_of(start_ref[which], 16)
            rows = pl.ds(row, query_block)
            span = pl.ds(begin, size)
            q_side = aug_ref[0, rows, :] * side_ref[...]
            k_side = aug_ref[0, span, :]
            near = block % 2 == info_ref[1]
            for pair in range(pairs):
                at = 384 * pair
                lanes = slice(128 * pair, 128 * pair + 128)
                q_pair = p_ref[0, rows, at : at + 128]
                k_pair = p_ref[0, span, at + 128 : at + 256]
                keys = jnp.concatenate([k_pair, k_side], axis=1)
                values = jnp.concatenate([p_ref[0, span, at + 256 : at + 384], k_side], axis=1)
                go = jnp.where(
                    near, go_mine_ref[0, block // 2, :, lanes], go_got_ref[0, block // 2, :, lanes]
                )
                o = jnp.where(
                    near, o_mine_ref[0, block // 2, :, lanes], o_send_ref[0, block // 2, :, lanes]
                )
                scaled = (go.astype(wide) * inv_ref[0, rows, lanes]).astype(low)
                product = scaled.astype(wide) * o.astype(wide)
                powers, grads, queries, pulls = [], [], [], []
                for head in range(2):
                    mine = lane // 64 == head
                    inner = jnp.sum(jnp.where(mine, product, 0.0), axis=1, keepdims=True)
                    one = inner.astype(low)
                    two = (inner - one.astype(wide)).astype(low)
                    three = (inner - one.astype(wide) - two.astype(wide)).astype(low)
                    none = jnp.zeros_like(q_pair)
                    go_side = jnp.where(
                        lane == 6,
                        -one,
                        jnp.where(lane == 7, -two, jnp.where(lane == 8, -three, none)),
                    )
                    q_mine = jnp.where(mine, q_pair, none)
                    go_mine = jnp.where(mine, scaled, none)
                    power = jnp.exp2(dot(keys, jnp.concatenate([q_mine, q_side], axis=1), 1, 1))
                    slope = dot(values, jnp.concatenate([go_mine, go_side], axis=1), 1, 1)
                    powers.append(power.astype(low))
                    grads.append((power * slope).astype(low))
                    queries.append(q_mine)
                    pulls.append(go_mine)
                gv_acc[span, lanes] += dot(
                    jnp.concatenate(powers, axis=1), jnp.concatenate(pulls, axis=0)
                )
                gk_acc[span, lanes] += dot(
                    jnp.concatenate(grads, axis=1), jnp.concatenate(queries, axis=0)
                )
                keys_turned = jnp.transpose(k_pair)
                turned = [dot(keys_turned[64 * i : 64 * i + 64], grads[i]) for i in range(2)]
                gq_acc[rows, lanes] = jnp.transpose(jnp.concatenate(turned, axis=0))

        for index, size in enumerate(windows):
            pl.when(kind_ref[which] == index)(partial(body, size))
        return carry

    lax.fori_loop(0, blocks, step, 0)
    means = mean_ref[...]
    for pair in range(pairs):
        lanes = slice(128 * pair, 128 * pair + 128)
        g_all[:, 384 * pair + 256 : 384 * pair + 384] = gv_acc[:, lanes].astype(low)
        for index, acc, factor, unscale in (
            (0, gq_acc, 0.125, 8.0 / log2e),
            (1, gk_acc, 1.0 / log2e, 1.0),
        ):
            to = slice(384 * pair + 128 * index, 384 * pair + 128 * index + 128)
            at = slice(256 * pair + 128 * index, 256 * pair + 128 * index + 128)
            gain = hg_ref[:, at]
            grad = acc[:, lanes] * factor
            normed = p_ref[0, :, to].astype(wide) * unscale
            weighted = grad * gain
            cross = grad * normed
            inner = split_dot(weighted, means)
            outer = split_dot(cross, means)
            g_all[:, to] = (
                rate_ref[0, :, at] * (weighted - inner - normed / gain * outer)
            ).astype(low)
            gain_ref[0:1, at] += jnp.sum(cross, axis=0, keepdims=True) / gain

    @pl.when(step_id == 0)
    def _():
        for copy in load_pieces(info_ref, [(pieces, 0, w_ref.shape[1], 0)], w_ref, sems):
            copy.wait()

    gw_acc[...] += dot(ht_ref[...], g_all[...])
    everything = dot(g_all[...], w_ref[...], 1, 1).astype(low)
    for block in range(blocks):
        result = everything[block * query_block : (block + 1) * query_block]

        @pl.when(block % 2 == info_ref[1])
        def _():
            mine_ref[0, block // 2] = result

        @pl.when(block % 2 != info_ref[1])
        def _():
            send_ref[0, block // 2] = result

    @pl.when(step_id == pl.num_programs(0) - 1)
    def _():
        if final:
            spread(info_ref, gw_acc, scale, gw_ref, None, 0, 0, gw_acc.shape[1])
        else:
            gw_ref[...] = gw_acc[...]


def spread(info_ref, acc, scale, mine_ref, other_ref, from_col, to_col, count):
    rows = mine_ref.shape[2]
    for side, ref in enumerate((mine_ref, other_ref)):
        if ref is None:
            continue
        for index in range(8):
            place = pl.multiple_of(info_ref[2 + index] * rows, rows)
            ref[index % 2, index // 2, :, to_col : to_col + count] = (
                acc[pl.ds(place, rows), from_col + side * count : from_col + (side + 1) * count]
                * scale
            ).astype(low)


def put_blocks(stage, acc, scale, owners, to_col, count):
    rows = stage.shape[1]
    for number, owner in enumerate(owners):
        for index in range(8):
            stage[2 * index + owner, :, to_col : to_col + count] = (
                acc[index * rows : (index + 1) * rows, number * count : (number + 1) * count]
                * scale
            ).astype(low)


def norm_back(values, grad, gain):
    centered = values - jnp.mean(values, axis=1, keepdims=True)
    rate = lax.rsqrt(jnp.mean(centered * centered, axis=1, keepdims=True) + norm_eps)
    normed = centered * rate
    weighted = grad * gain
    result = rate * (
        weighted
        - jnp.mean(weighted, axis=1, keepdims=True)
        - normed * jnp.mean(weighted * normed, axis=1, keepdims=True)
    )
    return result, normed


def gelu_parts(t):
    root = math.sqrt(2.0 / math.pi)
    square = t * t
    gate = 0.5 + 0.5 * jnp.tanh(t * (root + (root * 0.044715) * square))
    act = t * gate
    slope = gate + 2.0 * act * (1.0 - gate) * (root + (3.0 * root * 0.044715) * square)
    return act, slope


def middle_kernel(
    scale,
    chunks,
    info_ref,
    o_mine_ref,
    o_got_ref,
    mine_ref,
    got_ref,
    gy_ref,
    valid_ref,
    gain_ref,
    bias_ref,
    shards,
    keep_near_ref,
    keep_far_ref,
    send_near_ref,
    send_far_ref,
    gx_ref,
    go_mine_ref,
    go_send_ref,
    sums_ref,
    grads,
    x2_all,
    h_all,
    ht_all,
    gy_all,
    gyt_all,
    out_all,
    gh_all,
    up_both,
    down_both,
    up_acc,
    down_acc,
    act_all,
    grad_all,
    wo_ref,
    wo_acc,
    stage,
    stage_out,
    weight_sems,
    stage_sem,
):
    phase = pl.program_id(0)
    r = pl.program_id(1)
    last = pl.num_programs(1) - 1
    cols = o_mine_ref.shape[3]
    part = o_mine_ref.shape[2]
    chunk = up_both.shape[2] // 2
    c = info_ref[1]
    first_half = info_ref[0] == 0

    def weight_copies(f, slot):
        begin = pl.multiple_of(cols + f * 2 * chunk, 128)
        sems = weight_sems.at[slot]
        return load_shards(
            [(shards, m, begin, chunk, m * chunk) for m in range(2)], up_both.at[slot], sems
        ) + load_shards(
            [(shards, m, begin + chunk, chunk, m * chunk) for m in range(2)],
            down_both.at[slot],
            sems.at[pl.ds(2, 2)],
        )

    def stage_copy(f):
        return pltpu.make_async_copy(
            stage,
            grads.at[:, :, pl.ds(pl.multiple_of(f * 2 * chunk, 128), 2 * chunk)],
            stage_sem.at[0],
        )

    def both_heads():
        return jnp.concatenate(
            [o_mine_ref[0].reshape(2 * part, cols), o_got_ref[0].reshape(2 * part, cols)], axis=1
        )

    @pl.when((phase == 0) & (r == 0))
    def _():
        copies = load_shards(
            [(shards, c, 0, cols, 0), (shards, 1 - c, 0, cols, cols)], wo_ref, weight_sems.at[1]
        )
        run_all(copies)
        for copy in weight_copies(0, 0):
            copy.start()
        sums_ref[...] = jnp.zeros_like(sums_ref)
        wo_acc[...] = jnp.zeros_like(wo_acc)

    @pl.when(phase == 0)
    def _():
        x = jnp.concatenate(
            [
                jnp.where(first_half, mine_ref[0], got_ref[0]),
                jnp.where(first_half, got_ref[0], mine_ref[0]),
            ],
            axis=0,
        ).astype(wide)
        x2 = x + dot(both_heads(), wo_ref[...], 1, 1)
        x2_all[r] = x2
        out_all[r] = x2
        gh_all[r] = jnp.zeros_like(x2)
        centered = x2 - jnp.mean(x2, axis=1, keepdims=True)
        variance = jnp.mean(centered * centered, axis=1, keepdims=True)
        h = (centered * lax.rsqrt(variance + norm_eps) * gain_ref[...] + bias_ref[...]).astype(low)
        h_all[r] = h
        ht_all[r] = jnp.transpose(h)
        gy = gy_ref[...]
        gy_all[r] = gy
        gyt_all[r] = jnp.transpose(gy)

    @pl.when((phase > 0) & (phase <= chunks))
    def _():
        f = phase - 1
        slot = f % 2

        @pl.when(r == 0)
        def _():
            for copy in weight_copies(f, slot):
                copy.wait()

        @pl.when((r == 0) & (f + 1 < chunks))
        def _():
            for copy in weight_copies(f + 1, 1 - slot):
                copy.start()

        up_ref = up_both.at[slot]
        down_ref = down_both.at[slot]
        h = h_all[r]
        gy = gy_all[r]
        size = 512
        for at in range(0, 2 * chunk, size):
            act, slope = gelu_parts(dot(h, up_ref[:, at : at + size]))
            act_all[:, at : at + size] = act.astype(low)
            grad_all[:, at : at + size] = (dot(gy, down_ref[:, at : at + size]) * slope).astype(low)
        out_all[r] += dot(act_all[...], down_ref[...], 1, 1)
        gh_all[r] += dot(grad_all[...], up_ref[...], 1, 1)

        @pl.when(r == 0)
        def _():
            up_acc[...] = jnp.zeros_like(up_acc)
            down_acc[...] = jnp.zeros_like(down_acc)

        up_acc[...] += dot(ht_all[r], grad_all[...])
        down_acc[...] += dot(gyt_all[r], act_all[...])

        @pl.when((r == last) & (f > 0))
        def _():
            stage_copy(f - 1).wait()

        @pl.when(r == last)
        def _():
            put_blocks(stage, up_acc, scale, (0, 1), 0, chunk)
            put_blocks(stage, down_acc, scale, (0, 1), chunk, chunk)
            stage_copy(f).start()

    @pl.when(phase == chunks + 1)
    def _():
        out = (out_all[r] * valid_ref[...][:, :1]).astype(low)
        keep = jnp.where(first_half, out[:part], out[part:])
        send = jnp.where(first_half, out[part:], out[:part])
        keep_near_ref[0] = jnp.where(c == 0, keep[:, :cols], keep[:, cols:])
        keep_far_ref[0] = jnp.where(c == 0, keep[:, cols:], keep[:, :cols])
        send_near_ref[0] = jnp.where(c == 0, send[:, :cols], send[:, cols:])
        send_far_ref[0] = jnp.where(c == 0, send[:, cols:], send[:, :cols])
        gh = gh_all[r]
        back, normed = norm_back(x2_all[r], gh, gain_ref[...])
        gx = gy_all[r].astype(wide) + back
        gx_ref[...] = gx
        gx_low = gx.astype(low)
        go = dot(gx_low, wo_ref[...]).astype(low)
        go_mine_ref[0] = go[:, :cols].reshape(2, part, cols)
        go_send_ref[0] = go[:, cols:].reshape(2, part, cols)
        turned = jnp.transpose(gx_low)
        sums_ref[0:1, :] += jnp.sum(gh * normed, axis=0, keepdims=True)
        sums_ref[1:2, :] += jnp.sum(gh, axis=0, keepdims=True)
        wo_acc[...] += dot(turned, both_heads())

        @pl.when(r == last)
        def _():
            stage_copy(chunks - 1).wait()
            put_blocks(stage_out, wo_acc, scale, (c, 1 - c), 0, cols)
            copy = pltpu.make_async_copy(
                stage_out, grads.at[:, :, pl.ds(chunks * 2 * chunk, cols)], stage_sem.at[1]
            )
            copy.start()
            copy.wait()


def first_norm_kernel(
    info_ref, mine_ref, got_ref, a_ref, b_ref, gx2_ref, gain_ref, keep_ref, send_ref, sums_ref
):
    half = pl.program_id(1)
    x = jnp.where(half == info_ref[0], mine_ref[0], got_ref[0]).astype(wide)
    gh = a_ref[0, 0].astype(wide) + b_ref[0, 0].astype(wide)
    back, normed = norm_back(x, gh, gain_ref[...])
    out = (gx2_ref[...] + back).astype(low)

    @pl.when(half == info_ref[0])
    def _():
        keep_ref[0] = out

    @pl.when(half != info_ref[0])
    def _():
        send_ref[0] = out

    @pl.when((pl.program_id(0) == 0) & (half == 0))
    def _():
        sums_ref[...] = jnp.zeros_like(sums_ref)

    sums_ref[0:1, :] += jnp.sum(gh * normed, axis=0, keepdims=True)
    sums_ref[1:2, :] += jnp.sum(gh, axis=0, keepdims=True)


def place_kernel(plan, seqs, info_ref, *refs):
    sources, (out_ref, sems) = refs[: len(plan)], refs[len(plan) :]
    y, c = info_ref[0], info_ref[1]
    copies = []
    for number, (source, (own_y, own_c, begin)) in enumerate(zip(sources, plan)):
        at = seqs * (y if own_y else 1 - y) + begin
        copies.append(
            pltpu.make_async_copy(
                source,
                out_ref.at[pl.ds(at, source.shape[0]), c if own_c else 1 - c],
                sems.at[number],
            )
        )
    run_all(copies)


def shape_of(dims, kind=low):
    return jax.ShapeDtypeStruct(dims, kind)


def window_table(segs, blocks):
    length = segs.shape[1]
    pad_begin = jnp.sum((segs >= 0).astype(jnp.int32), axis=1, keepdims=True)
    begins = jnp.where(segs >= 0, segs, pad_begin)
    size = length // blocks
    firsts = begins[:, ::size]
    lasts = begins[:, size - 1 :: size]
    ends = jnp.sum((begins[:, None, :] <= lasts[:, :, None]).astype(jnp.int32), axis=2)
    reach = ends - firsts
    kinds = jnp.zeros_like(reach)
    spans = jnp.full_like(reach, windows[0])
    for index in range(1, len(windows)):
        larger = reach > windows[index - 1]
        kinds = jnp.where(larger, index, kinds)
        spans = jnp.where(larger, windows[index], spans)
    starts = jnp.minimum(firsts, length - spans)
    return starts.reshape(-1), kinds.reshape(-1)


def mask_columns(segs):
    codes = (segs + 16) // 16
    lane = jnp.arange(128, dtype=jnp.int32)
    bits = (codes[:, :, None] >> jnp.minimum(lane, 5)) & 1
    signs = (2 * bits - 1).astype(wide)
    return jnp.where(lane < 6, signs, jnp.where(lane < 9, 1.0, 0.0)).astype(low)


def swap(values, axis):
    return lax.ppermute(values, axis, [(0, 1), (1, 0)])


def in_order(index, mine, other, axis):
    return jnp.where(
        index == 0,
        jnp.concatenate([mine, other], axis=axis),
        jnp.concatenate([other, mine], axis=axis),
    )


def pick(values, index, axis):
    return lax.dynamic_index_in_dim(values, index, axis, keepdims=False)


def shift_far(values, step):
    return lax.ppermute(
        values,
        "dp",
        [(2 * ((z + step) % 4) + x, 2 * z + x) for z in range(4) for x in range(2)],
    )


def swap_x(values):
    return lax.ppermute(values, "dp", [(d, d ^ 1) for d in range(8)])


def gather_pieces(shard):
    pieces = []
    for step in range(4):
        piece = shard if step == 0 else shift_far(shard, step)
        pieces += [piece, swap_x(piece)]
    return pieces


def on_device_small(
    patches, segments, w_qkv, w_out, w_up, w_down, ln_gain, ln_bias, head_gain, cotangent
):
    half, seqs_all, width = patches.shape
    length = 2 * half
    seqs = seqs_all // 2
    cols = w_qkv.shape[2]
    part = half // 2
    y = lax.axis_index("seq")
    c = lax.axis_index("mlp")
    d = lax.axis_index("dp")
    dp_size = lax.axis_size("dp")
    scale = 1.0 / math.sqrt(dp_size * seqs_all * length)
    own_rows = seqs * half
    hidden = w_up.shape[1]
    shard_rows = width // dp_size
    places = jnp.stack(
        [2 * ((d // 2 + index // 2) % 4) + ((d % 2) ^ (index % 2)) for index in range(8)]
    )
    info = jnp.concatenate([jnp.stack([y, c]), places]).astype(jnp.int32)

    turned = jnp.transpose(patches, (1, 0, 2)).reshape(2, seqs, 2, part, width)
    got = swap(pick(pick(turned, 1 - y, 0), c, 1), "seq")
    far = swap(got, "mlp")
    turned = turned.reshape(seqs_all, half, width)
    small = jnp.concatenate(
        [
            ln_gain.astype(low),
            ln_bias.astype(low),
            head_gain.astype(low).reshape(1, -1),
            jnp.zeros((3, shard_rows), low),
        ]
    )
    small = jnp.pad(small, ((0, 8), (0, 3 * cols - shard_rows)))
    pairs = cols // 128
    w_in = jnp.transpose(w_qkv.astype(low).reshape(3, shard_rows, pairs, 128), (1, 2, 0, 3))
    w_in = w_in.reshape(shard_rows, 3 * cols)
    in_pieces = gather_pieces(
        jnp.concatenate(
            [w_in, small]
        )
    )
    small = [piece[shard_rows : shard_rows + 8, :shard_rows] for piece in in_pieces]
    chunk = hidden_chunk
    chunks = hidden // chunk
    up_low = w_up.astype(low)
    down_low = jnp.transpose(w_down.astype(low))
    parts = [jnp.transpose(w_out.astype(low))]
    for f in range(chunks):
        at = slice(f * chunk, (f + 1) * chunk)
        parts += [up_low[:, at], down_low[:, at]]

    def gather_shards(parts):
        return lax.all_gather(jnp.concatenate(parts, axis=1), ("dp", "mlp"), axis=0)

    shards = gather_shards(parts)

    order = (places[None, :] == jnp.arange(8)[:, None]).astype(low)
    small = jnp.einsum("nr,rkw->knw", order, jnp.stack(small), preferred_element_type=wide)
    gains = small[0:2].reshape(2, width)
    biases = small[2:4].reshape(2, width)
    head_gains = jnp.transpose(small[4].reshape(dp_size, 2, cols // 64, 64 // dp_size), (1, 2, 0, 3))
    head_gains = jnp.transpose(head_gains.reshape(2, pairs, 128), (1, 0, 2))
    key_scale = jnp.array([[[log2e / 8.0], [1.0]]], wide)
    head_scaled = (head_gains * key_scale).reshape(1, 2 * cols)
    head_gains = head_gains.reshape(1, 2 * cols)

    segs = lax.dynamic_slice_in_dim(jnp.transpose(segments), y * seqs, seqs, 0)
    cot = cotangent.reshape(2, part, seqs_all, cols)
    cot_other = swap(pick(cot, 1 - c, 0), "mlp")
    cot = jnp.transpose(in_order(c, pick(cot, c, 0), cot_other, 2), (1, 0, 2))
    cot = cot.reshape(2, seqs, part, width)
    cot_got = swap(pick(cot, 1 - y, 0), "seq")
    cot = in_order(y, pick(cot, y, 0)[:, None], cot_got[:, None], 1)
    valid = pick((segs >= 0).reshape(seqs, 2, 2, part), c, 2)
    gy = jnp.where(valid[..., None], cot, jnp.zeros_like(cot)).reshape(own_rows, width)
    valid = jnp.broadcast_to(valid.reshape(own_rows, 1).astype(wide), (own_rows, 128))

    starts, kinds = window_table(segs, length // query_block)
    aug = mask_columns(segs)
    lanes = jnp.arange(128)
    side = jnp.where(lanes < 6, mask_weight, jnp.where(lanes == 6, -6.0 * mask_weight, 0.0))
    side = side.astype(low)[None]
    means = jnp.where(lanes[:, None] // 64 == lanes[None] // 64, 1.0 / 64, 0.0).astype(low)
    means = jnp.concatenate([means, means])
    anywhere = pl.BlockSpec(memory_space=pl.ANY)

    def whole(dims):
        return pl.BlockSpec(dims, lambda *ids: (0,) * len(dims))

    def call(kernel, grid, in_specs, out_specs, out_shape, scratch, name, scalars, pins=(), share=1, vmem=vmem_bytes):
        work = int(micros[name] * 1150000000 / share)
        ends = scalars + len(in_specs)

        def unpinned(*refs):
            kernel(*refs[:ends], *refs[ends + len(pins) :])

        run = pl.pallas_call(
            unpinned,
            grid_spec=pltpu.PrefetchScalarGridSpec(
                num_scalar_prefetch=scalars,
                grid=grid,
                in_specs=in_specs + [anywhere] * len(pins),
                out_specs=out_specs,
                scratch_shapes=scratch,
            ),
            out_shape=out_shape,
            compiler_params=params(len(grid), vmem),
            cost_estimate=pl.CostEstimate(flops=work, bytes_accessed=1000000, transcendentals=0),
            name=name,
        )
        return lambda *operands: run(*operands, *pins)

    piece_sems = pltpu.SemaphoreType.DMA((4, 8))
    one_seq = pl.BlockSpec((1, part, width), lambda s, j, *_: (s, 0, 0))
    projected, rates, h1t = call(
        qkv_kernel,
        (seqs, 2),
        [
            pl.BlockSpec((1, half, width), lambda s, j, info: (seqs * info[0] + s, 0, 0)),
            one_seq,
            one_seq,
            whole((1, width)),
            whole((1, width)),
            whole((1, 2 * cols)),
            whole((256, 128)),
        ]
        + [anywhere] * 8,
        [
            pl.BlockSpec((1, half, 3 * cols), lambda s, j, *_: (s, j, 0)),
            pl.BlockSpec((1, half, 2 * cols), lambda s, j, *_: (s, j, 0)),
            pl.BlockSpec((width, half), lambda s, j, *_: (0, 2 * s + j)),
        ],
        [
            shape_of((seqs, length, 3 * cols)),
            shape_of((seqs, length, 2 * cols), wide),
            shape_of((width, seqs * length)),
        ],
        [pltpu.VMEM((width, 3 * cols), low), piece_sems],
        "qkv",
        1,
    )(info, turned, got, far, gains[:1], biases[:1], head_scaled, means, *in_pieces)
    def per_seq(*dims, base=0):
        return pl.BlockSpec((1,) + dims, lambda s, *_: (s + base,) + (0,) * len(dims))

    o_mine, o_send, inverse = call(
        attn_fwd_kernel,
        (seqs,),
        [per_seq(length, 3 * cols), per_seq(length, 128), whole((1, 128))],
        [per_seq(2, part, cols), per_seq(2, part, cols), per_seq(length, cols)],
        [shape_of((seqs, 2, part, cols))] * 2 + [shape_of((seqs, length, cols), wide)],
        [],
        "attn_fwd",
        3,
    )(info, starts, kinds, projected, aug, side)

    o_got = swap(o_send, "mlp")
    seq_of = seqs - 1
    final = chunks + 1

    def at_ends(p, r):
        return jnp.where((p == 0) | (p == final), r, seq_of)

    def at_start(p, r):
        return jnp.where(p == 0, r, seq_of)

    def at_final(p, r):
        return jnp.where(p == final, r, 0)

    heads_spec = pl.BlockSpec((1, 2, part, cols), lambda p, r, *_: (at_ends(p, r), 0, 0, 0))
    moved_spec = pl.BlockSpec((1, part, cols), lambda p, r, *_: (at_final(p, r), 0, 0))
    heads_out = pl.BlockSpec((1, 2, part, cols), lambda p, r, *_: (at_final(p, r), 0, 0, 0))
    by_seq_bf = pltpu.VMEM((seqs, half, width), low)
    by_seq_turned = pltpu.VMEM((seqs, width, half), low)
    by_seq_wide = pltpu.VMEM((seqs, half, width), wide)
    grad_shape = (16, shard_rows, 2 * hidden + cols)
    keep_near, keep_far, send_near, send_far, gx2, go_mine, go_send, second_sums, grads = call(
        partial(middle_kernel, scale, chunks),
        (chunks + 2, seqs),
        [
            heads_spec,
            heads_spec,
            pl.BlockSpec(
                (1, part, width), lambda p, r, info: (seqs * info[0] + at_start(p, r), info[1], 0)
            ),
            pl.BlockSpec((1, part, width), lambda p, r, *_: (at_start(p, r), 0, 0)),
            pl.BlockSpec((half, width), lambda p, r, *_: (at_start(p, r), 0)),
            pl.BlockSpec((half, 128), lambda p, r, *_: (at_final(p, r), 0)),
            whole((1, width)),
            whole((1, width)),
            anywhere,
        ],
        [
            moved_spec,
            moved_spec,
            moved_spec,
            moved_spec,
            pl.BlockSpec((half, width), lambda p, r, *_: (at_final(p, r), 0)),
            heads_out,
            heads_out,
            whole((8, width)),
            anywhere,
        ],
        [
            shape_of((seqs, part, cols)),
            shape_of((seqs, part, cols)),
            shape_of((seqs, part, cols)),
            shape_of((seqs, part, cols)),
            shape_of((own_rows, width), wide),
            shape_of((seqs, 2, part, cols)),
            shape_of((seqs, 2, part, cols)),
            shape_of((8, width), wide),
            shape_of(grad_shape),
        ],
        [by_seq_wide, by_seq_bf, by_seq_turned, by_seq_bf, by_seq_turned, by_seq_wide, by_seq_wide]
        + [pltpu.VMEM((2, width, 2 * chunk), low)] * 2
        + [pltpu.VMEM((width, 2 * chunk), wide)] * 2
        + [pltpu.VMEM((half, 2 * chunk), low)] * 2
        + [
            pltpu.VMEM((width, width), low),
            pltpu.VMEM((width, width), wide),
            pltpu.VMEM((16, shard_rows, 2 * chunk), low),
            pltpu.VMEM((16, shard_rows, cols), low),
            pltpu.SemaphoreType.DMA((2, 4, 8)),
            pltpu.SemaphoreType.DMA((2,)),
        ],
        "middle",
        1,
        vmem=62 * 1024 * 1024,
    )(info, o_mine, o_got, turned, got, gy, valid, gains[1:], biases[1:], shards)
    go_got = swap(go_send, "mlp")
    got_near = swap(send_near, "seq")
    got_far = swap(send_far, "seq")
    scattered = lax.psum_scatter(grads, ("dp", "mlp"), scatter_dimension=0, tiled=True)[0]

    def attention_back(base, count, partial_sum, pins):
        first = partial_sum is None
        final = base + count == seqs
        shares = (2, 4, shard_rows, 3 * cols)
        carried = [] if first else [partial_sum]
        return call(
            partial(attn_bwd_kernel, base, scale, first, final),
            (count,),
            [per_seq(length, 3 * cols, base=base)]
            + [per_seq(2, part, cols, base=base)] * 4
            + [
                per_seq(length, cols, base=base),
                per_seq(length, 2 * cols, base=base),
                per_seq(length, 128, base=base),
                whole((1, 128)),
                whole((1, 2 * cols)),
                whole((256, 128)),
                pl.BlockSpec((width, length), lambda s, *_: (0, s + base)),
            ]
            + [anywhere] * 8
            + [whole((width, 3 * cols))] * len(carried),
            [per_seq(2, part, width)] * 2
            + [whole(shares if final else (width, 3 * cols)), whole((8, 2 * cols))],
            [shape_of((count, 2, part, width))] * 2
            + [shape_of(shares) if final else shape_of((width, 3 * cols), wide)]
            + [shape_of((8, 2 * cols), wide)],
            [pltpu.VMEM((length, cols), wide)] * 3
            + [
                pltpu.VMEM((length, 3 * cols), low),
                pltpu.VMEM((width, 3 * cols), wide),
                pltpu.VMEM((width, 3 * cols), low),
                piece_sems,
            ],
            "attn_bwd",
            3,
            pins,
            seqs / count,
        )(
            info, starts, kinds, projected, go_mine, go_got, o_mine, o_send, inverse, rates,
            aug, side, head_gains, means, h1t, *in_pieces, *carried,
        )

    def first_back(base, count, mine, got_part, pins):
        here = pl.BlockSpec((1, 1, part, width), lambda s, h, *_: (s, h, 0, 0))
        moved = pl.BlockSpec((1, part, width), lambda s, h, *_: (s, 0, 0))
        return call(
            first_norm_kernel,
            (count, 2),
            [
                pl.BlockSpec(
                    (1, part, width), lambda s, h, info: (seqs * info[0] + s + base, info[1], 0)
                ),
                pl.BlockSpec((1, part, width), lambda s, h, *_: (s + base, 0, 0)),
                here,
                here,
                pl.BlockSpec((part, width), lambda s, h, *_: (2 * (s + base) + h, 0)),
                whole((1, width)),
            ],
            [moved, moved, whole((8, width))],
            [shape_of((count, part, width))] * 2 + [shape_of((8, width), wide)],
            [],
            "first_norm",
            1,
            pins,
            seqs / count,
        )(info, turned, got, mine, got_part, gx2, gains[:1])

    def place(sources, plan, feature_count, pins=()):
        return call(
            partial(place_kernel, plan, seqs),
            (1,),
            [anywhere] * len(plan),
            whole((seqs_all, 2, part, feature_count)),
            shape_of((seqs_all, 2, part, feature_count)),
            [pltpu.SemaphoreType.DMA((len(plan),))],
            "place",
            1,
            pins,
        )(info, *sources)

    mine, send, gw_in, head_sums = attention_back(0, seqs, None, ())
    keep_core = swap(keep_far, "mlp")
    far_x = swap_x(gw_in[1])
    moved = swap(send, "mlp")
    keep, give, first_sums = first_back(0, seqs, mine, moved, [got_near, got_far, keep_core])
    got_core = swap(got_far, "mlp")
    keep_moved = swap(keep, "mlp")
    got_grad = swap(give, "seq")

    norms = jnp.concatenate([first_sums[:2], second_sums[:2]]) * scale
    heads = jnp.transpose(head_sums[0].reshape(pairs, 2, 128), (1, 0, 2)) * scale
    heads = heads.reshape(2, cols // 64, dp_size, 64 // dp_size)
    heads = jnp.transpose(heads, (2, 0, 1, 3)).reshape(1, width)
    small = jnp.concatenate([norms + swap(norms, "mlp"), heads])
    small = small + lax.ppermute(small, "dp", [(i, i ^ 1) for i in range(8)])
    small = small.reshape(5, 4, 2, shard_rows)
    small = lax.dynamic_index_in_dim(small, d % 2, 2, keepdims=False)
    small = jnp.concatenate([small, small], axis=1)
    small = lax.dynamic_slice_in_dim(small, d // 2, 4, 1)
    small = jnp.pad(jnp.transpose(small, (1, 2, 0)), ((0, 0), (0, 0), (0, 123)))
    total = gw_in[0].astype(wide) + far_x.astype(wide)
    total = jnp.concatenate([total, small], axis=2)
    low_total = total.astype(low)
    moved = [shift_far(low_total[step], 4 - step) for step in range(1, 4)]

    total = total[0] + sum(part.astype(wide) for part in moved)
    both = jnp.concatenate([scattered, total.astype(low)], axis=1)
    both_got = swap(both, "seq").astype(wide)
    scattered = scattered.astype(wide) + both_got[:, : scattered.shape[1]]
    total = total + both_got[:, scattered.shape[1] :]

    plan = [(True, True, 0), (True, False, 0), (False, True, 0), (False, False, 0)]
    out = place([keep_near, keep_core, got_near, got_core], plan, cols, [])
    out = jnp.transpose(out.reshape(seqs_all, half, cols), (1, 0, 2))
    grad_patches = place([keep, keep_moved, got_grad, swap(got_grad, "mlp")], plan, width, [])
    grad_patches = jnp.transpose(grad_patches.reshape(seqs_all, half, width), (1, 0, 2))

    gw_up = jnp.concatenate(
        [scattered[:, 2 * f * chunk : (2 * f + 1) * chunk] for f in range(chunks)], axis=1
    )
    gw_down = jnp.concatenate(
        [scattered[:, (2 * f + 1) * chunk : (2 * f + 2) * chunk] for f in range(chunks)], axis=1
    )
    gw_out = scattered[:, 2 * hidden :]
    gw_in = total[:, : 3 * cols].reshape(shard_rows, pairs, 3, 128)
    gw_in = jnp.transpose(gw_in, (2, 0, 1, 3)).reshape(3, shard_rows, cols)
    norms = jnp.transpose(total[:, 3 * cols : 3 * cols + 4])
    heads = total[:, 3 * cols + 4].reshape(2, cols // 64, 64 // dp_size)
    return (
        out,
        grad_patches,
        gw_in,
        jnp.transpose(gw_out),
        gw_up,
        jnp.transpose(gw_down),
        norms[0::2],
        norms[1::2],
        heads,
    )


def solution(mesh):
    shape = dict(mesh.shape)
    small = shape["seq"] == 2 and shape["mlp"] == 2 and shape["dp"] == 8
    return jax.shard_map(
        on_device_small if small else on_device,
        mesh=mesh,
        in_specs=(
            P("seq", "dp", None),
            P(None, "dp"),
            P(None, "dp", "mlp"),
            P("mlp", "dp"),
            P("dp", "mlp"),
            P("mlp", "dp"),
            P(None, "dp"),
            P(None, "dp"),
            P(None, "mlp", "dp"),
            P("seq", "dp", "mlp"),
        ),
        out_specs=(
            P("seq", "dp", "mlp"),
            P("seq", "dp", None),
            P(None, "dp", "mlp"),
            P("mlp", "dp"),
            P("dp", "mlp"),
            P("mlp", "dp"),
            P(None, "dp"),
            P(None, "dp"),
            P(None, "mlp", "dp"),
        ),
        check_vma=False,
    )
```

```python
from functools import partial
import math

import jax
import jax.numpy as jnp
from jax import lax
from jax.experimental import pallas as pl
from jax.experimental.pallas import tpu as pltpu
from jax.sharding import PartitionSpec as P

norm_eps = 1e-06
masked_value = -1e30


def layer_norm(values, gain_row, bias_row):
    average = jnp.mean(values, axis=-1, keepdims=True)
    centered = values - average
    variance = jnp.mean(centered * centered, axis=-1, keepdims=True)
    return centered * lax.rsqrt(variance + norm_eps) * gain_row + bias_row


def head_norm(values, gain_rows):
    average = jnp.mean(values, axis=-1, keepdims=True)
    centered = values - average
    variance = jnp.mean(centered * centered, axis=-1, keepdims=True)
    return centered * lax.rsqrt(variance + norm_eps) * gain_rows


def on_device(
    patches, segments, w_qkv, w_out, w_up, w_down, ln_gain, ln_bias, head_gain, cotangent
):
    (
        query_weight,
        out_weight,
        up_projection_weight,
        down_projection_weight,
        norm_gains,
        norm_biases,
        head_gains,
    ) = (
        lax.all_gather(w_qkv.astype(jnp.bfloat16), "dp", axis=1, tiled=True),
        lax.all_gather(w_out.astype(jnp.bfloat16), "dp", axis=1, tiled=True),
        lax.all_gather(w_up.astype(jnp.bfloat16), "dp", axis=0, tiled=True),
        lax.all_gather(w_down.astype(jnp.bfloat16), "dp", axis=1, tiled=True),
        lax.all_gather(ln_gain.astype(jnp.bfloat16), "dp", axis=1, tiled=True),
        lax.all_gather(ln_bias.astype(jnp.bfloat16), "dp", axis=1, tiled=True),
        lax.all_gather(head_gain.astype(jnp.bfloat16), "dp", axis=2, tiled=True),
    )
    local_rows = patches.shape[0]
    seq_here = patches.shape[1]
    width = patches.shape[2]
    head_cols = query_weight.shape[2]
    heads_here = head_gains.shape[1]
    head_size = head_gains.shape[2]
    seq_len = local_rows * lax.axis_size("seq")
    feature_cols = width // lax.axis_size("mlp")
    score_scale = head_size ** (-0.5)
    gain_float = norm_gains.astype(jnp.float32)
    bias_float = norm_biases.astype(jnp.float32)
    head_float = head_gains.astype(jnp.float32)
    seg_here = lax.dynamic_slice_in_dim(segments, lax.axis_index("seq") * local_rows, local_rows, 0)
    valid_mask = (seg_here >= 0).astype(jnp.float32)[:, :, None]
    query_segs = jnp.transpose(seg_here)
    key_segs = jnp.transpose(segments)
    patch_float = patches.astype(jnp.float32)
    normed = layer_norm(patch_float, gain_float[0], bias_float[0]).astype(jnp.bfloat16)
    projected = jnp.einsum(
        "lsd,cde->csle", normed, query_weight, preferred_element_type=jnp.float32
    )
    shape_heads = (seq_here, local_rows, heads_here, head_size)
    query_raw = projected[0].reshape(shape_heads)
    key_raw = projected[1].reshape(shape_heads)
    query_low = head_norm(query_raw, head_float[0]).astype(jnp.bfloat16)
    key_low = head_norm(key_raw, head_float[1]).astype(jnp.bfloat16)
    value_low = projected[2].astype(jnp.bfloat16)
    key_pairs = jnp.concatenate(
        [key_low.reshape(seq_here, local_rows, head_cols), value_low], axis=2
    )

    def split_pairs(gathered):
        key_heads = gathered[:, :head_cols].reshape(gathered.shape[0], heads_here, head_size)
        value_heads = gathered[:, head_cols:].reshape(gathered.shape[0], heads_here, head_size)
        return (key_heads, value_heads)

    def attend_forward(unused, inputs_seq):
        query_seq, pairs_seq, query_rows, key_rows = inputs_seq
        gathered = lax.all_gather(pairs_seq, "seq", axis=0, tiled=True)
        key_heads, value_heads = split_pairs(gathered)
        logits = (
            jnp.einsum("qhe,khe->hqk", query_seq, key_heads, preferred_element_type=jnp.float32)
            * score_scale
        )
        visible = (query_rows[:, None] == key_rows[None, :])[None]
        masked = jnp.where(visible, logits, masked_value)
        largest = jnp.max(masked, axis=2, keepdims=True)
        powered = jnp.exp(masked - largest)
        totals = jnp.sum(powered, axis=2, keepdims=True)
        attention = (powered / totals).astype(jnp.bfloat16)
        mixed = jnp.einsum(
            "hqk,khe->qhe", attention, value_heads, preferred_element_type=jnp.float32
        )
        log_total = (largest + jnp.log(totals))[:, :, 0]
        return (unused, (mixed.astype(jnp.bfloat16).reshape(local_rows, head_cols), log_total))

    _, (attn_heads, log_totals) = lax.scan(
        attend_forward, 0, (query_low, key_pairs, query_segs, key_segs)
    )
    attn_part = jnp.einsum(
        "slf,fd->lsd", attn_heads, out_weight, preferred_element_type=jnp.float32
    )
    attn_mine = lax.psum_scatter(
        attn_part.astype(jnp.bfloat16), "mlp", scatter_dimension=2, tiled=True
    ).astype(jnp.float32)
    patch_mine = lax.dynamic_slice_in_dim(
        patch_float, lax.axis_index("mlp") * feature_cols, feature_cols, 2
    )
    resid_mine = patch_mine + attn_mine
    residual = lax.all_gather(resid_mine.astype(jnp.bfloat16), "mlp", axis=2, tiled=True).astype(
        resid_mine.dtype
    )
    second_normalized = layer_norm(residual, gain_float[1], bias_float[1]).astype(jnp.bfloat16)
    hidden_pre = jnp.einsum(
        "own,nr->owr", second_normalized, up_projection_weight, preferred_element_type=jnp.float32
    )
    mlp_activation = jax.nn.gelu(hidden_pre, approximate=True).astype(jnp.bfloat16)
    branch_part = jnp.einsum(
        "ruo,oe->rue", mlp_activation, down_projection_weight, preferred_element_type=jnp.float32
    )
    branch_mine = lax.psum_scatter(
        branch_part.astype(jnp.bfloat16), "mlp", scatter_dimension=2, tiled=True
    ).astype(jnp.float32)
    out = (valid_mask * (resid_mine + branch_mine)).astype(jnp.bfloat16)
    cot_full = lax.all_gather(cotangent, "mlp", axis=2, tiled=True)
    grad_out = valid_mask * cot_full.astype(jnp.float32)
    output_gradient_reduced = grad_out.astype(jnp.bfloat16)
    grad_down = jnp.einsum(
        "xgr,xge->re", mlp_activation, output_gradient_reduced, preferred_element_type=jnp.float32
    )
    grad_act = jnp.einsum(
        "mit,nt->min",
        output_gradient_reduced,
        down_projection_weight,
        preferred_element_type=jnp.float32,
    )
    _, gelu_pull = jax.vjp(partial(jax.nn.gelu, approximate=True), hidden_pre)
    hidden_gradient = gelu_pull(grad_act)[0].astype(jnp.bfloat16)
    up_projection_gradient = jnp.einsum(
        "gih,giv->hv", second_normalized, hidden_gradient, preferred_element_type=jnp.float32
    )
    grad_normed_two = lax.psum(
        jnp.einsum(
            "vwb,kb->vwk", hidden_gradient, up_projection_weight, preferred_element_type=jnp.float32
        ).astype(jnp.bfloat16),
        "mlp",
    ).astype(jnp.float32)
    _, second_pull = jax.vjp(layer_norm, residual, gain_float[1], bias_float[1])
    grad_resid_norm, grad_gain_two, grad_bias_two = second_pull(grad_normed_two)
    grad_resid = grad_out + grad_resid_norm
    grad_resid_low = grad_resid.astype(jnp.bfloat16)
    grad_out_weight = jnp.einsum(
        "slf,lsd->fd", attn_heads, grad_resid_low, preferred_element_type=jnp.float32
    )
    grad_mixed = jnp.einsum(
        "lsd,fd->slf", grad_resid_low, out_weight, preferred_element_type=jnp.float32
    ).astype(jnp.bfloat16)

    def attend_backward(unused, inputs_seq):
        query_seq, pairs_seq, query_rows, key_rows, log_total, grad_seq = inputs_seq
        gathered = lax.all_gather(pairs_seq, "seq", axis=0, tiled=True)
        key_heads, value_heads = split_pairs(gathered)
        logits = (
            jnp.einsum("qhe,khe->hqk", query_seq, key_heads, preferred_element_type=jnp.float32)
            * score_scale
        )
        visible = (query_rows[:, None] == key_rows[None, :])[None]
        attention = jnp.exp(jnp.where(visible, logits - log_total[:, :, None], masked_value))
        attention_low = attention.astype(jnp.bfloat16)
        grad_heads = grad_seq.reshape(local_rows, heads_here, head_size)
        grad_attention = jnp.einsum(
            "qhe,khe->hqk", grad_heads, value_heads, preferred_element_type=jnp.float32
        )
        inner = jnp.sum(grad_attention * attention, axis=2, keepdims=True)
        grad_logits = (attention * (grad_attention - inner)).astype(jnp.bfloat16)
        grad_query = (
            jnp.einsum("hqk,khe->qhe", grad_logits, key_heads, preferred_element_type=jnp.float32)
            * score_scale
        )
        grad_key = (
            jnp.einsum("hqk,qhe->khe", grad_logits, query_seq, preferred_element_type=jnp.float32)
            * score_scale
        )
        grad_value = jnp.einsum(
            "hqk,qhe->khe", attention_low, grad_heads, preferred_element_type=jnp.float32
        )
        grad_pairs = lax.psum_scatter(
            jnp.concatenate(
                [
                    grad_key.reshape(lax.axis_size("seq") * local_rows, head_cols),
                    grad_value.reshape(lax.axis_size("seq") * local_rows, head_cols),
                ],
                axis=1,
            ).astype(jnp.bfloat16),
            "seq",
            scatter_dimension=0,
            tiled=True,
        ).astype(jnp.float32)
        return (unused, (grad_query.reshape(local_rows, head_cols), grad_pairs))

    _, (grad_queries, grad_pairs_all) = lax.scan(
        attend_backward, 0, (query_low, key_pairs, query_segs, key_segs, log_totals, grad_mixed)
    )
    _, query_pull = jax.vjp(head_norm, query_raw, head_float[0])
    grad_query_raw, grad_query_gain = query_pull(grad_queries.reshape(shape_heads))
    _, key_pull = jax.vjp(head_norm, key_raw, head_float[1])
    grad_key_raw, grad_key_gain = key_pull(grad_pairs_all[:, :, :head_cols].reshape(shape_heads))
    grad_projected = jnp.stack(
        [
            grad_query_raw.reshape(seq_here, local_rows, head_cols),
            grad_key_raw.reshape(seq_here, local_rows, head_cols),
            grad_pairs_all[:, :, head_cols:],
        ],
        axis=0,
    ).astype(jnp.bfloat16)
    grad_query_weight = jnp.einsum(
        "lsd,csle->cde", normed, grad_projected, preferred_element_type=jnp.float32
    )
    grad_normed = lax.psum(
        jnp.einsum(
            "csle,cde->lsd", grad_projected, query_weight, preferred_element_type=jnp.float32
        ).astype(jnp.bfloat16),
        "mlp",
    ).astype(jnp.float32)
    _, first_pull = jax.vjp(layer_norm, patch_float, gain_float[0], bias_float[0])
    grad_patch_norm, grad_gain_one, grad_bias_one = first_pull(grad_normed)
    grad_patches = (grad_resid + grad_patch_norm).astype(jnp.bfloat16)
    grad_scale = 1.0 / math.sqrt(lax.axis_size("dp") * seq_here * seq_len)
    term_qkv = grad_query_weight * grad_scale
    term_out = grad_out_weight * grad_scale
    term_up = up_projection_gradient * grad_scale
    term_down = grad_down * grad_scale
    term_gain = jnp.stack([grad_gain_one, grad_gain_two]) * grad_scale
    term_bias = jnp.stack([grad_bias_one, grad_bias_two]) * grad_scale
    term_head = jnp.stack([grad_query_gain, grad_key_gain]) * grad_scale
    summed = (
        lax.psum(term_qkv.astype(jnp.bfloat16), "seq").astype(jnp.float32),
        lax.psum(term_out.astype(jnp.bfloat16), "seq").astype(jnp.float32),
        lax.psum(term_up.astype(jnp.bfloat16), "seq").astype(jnp.float32),
        lax.psum(term_down.astype(jnp.bfloat16), "seq").astype(jnp.float32),
        lax.psum(term_gain.astype(jnp.bfloat16), "seq").astype(jnp.float32),
        lax.psum(term_bias.astype(jnp.bfloat16), "seq").astype(jnp.float32),
        lax.psum(term_head.astype(jnp.bfloat16), "seq").astype(jnp.float32),
    )
    shards = (
        lax.psum_scatter(
            summed[0].astype(jnp.bfloat16), "dp", scatter_dimension=1, tiled=True
        ).astype(jnp.float32),
        lax.psum_scatter(
            summed[1].astype(jnp.bfloat16), "dp", scatter_dimension=1, tiled=True
        ).astype(jnp.float32),
        lax.psum_scatter(
            summed[2].astype(jnp.bfloat16), "dp", scatter_dimension=0, tiled=True
        ).astype(jnp.float32),
        lax.psum_scatter(
            summed[3].astype(jnp.bfloat16), "dp", scatter_dimension=1, tiled=True
        ).astype(jnp.float32),
        lax.psum_scatter(
            summed[4].astype(jnp.bfloat16), "dp", scatter_dimension=1, tiled=True
        ).astype(jnp.float32),
        lax.psum_scatter(
            summed[5].astype(jnp.bfloat16), "dp", scatter_dimension=1, tiled=True
        ).astype(jnp.float32),
        lax.psum_scatter(
            summed[6].astype(jnp.bfloat16), "dp", scatter_dimension=2, tiled=True
        ).astype(jnp.float32),
    )
    return (
        out,
        grad_patches,
        shards[0],
        shards[1],
        shards[2],
        shards[3],
        shards[4],
        shards[5],
        shards[6],
    )


low = jnp.bfloat16
wide = jnp.float32
log2e = math.log2(math.e)
mask_weight = 128.0
query_block = 256
windows = (384, 512, 1024)
vmem_bytes = 56 * 1024 * 1024
hidden_chunk = 512
micros = {
    "qkv": 25,
    "attn_fwd": 22,
    "middle": 80,
    "attn_bwd": 75,
    "first_norm": 8,
    "place": 4,
}


def dot(left, right, left_dim=1, right_dim=0):
    return lax.dot_general(
        left, right, (((left_dim,), (right_dim,)), ((), ())), preferred_element_type=wide
    )


def params(count, vmem):
    return pltpu.CompilerParams(
        dimension_semantics=("arbitrary",) * count, vmem_limit_bytes=vmem
    )


def split_dot(values, ones_matrix):
    top = values.astype(low)
    rest = (values - top.astype(wide)).astype(low)
    return dot(jnp.concatenate([top, rest], axis=1), ones_matrix)


def load_pieces(info_ref, sets, scratch, sems):
    copies = []
    rows = scratch.shape[0] // 8
    for number, (pieces, first, count, target) in enumerate(sets):
        for index in range(8):
            if len(pieces) == 8:
                piece = pieces[index]
            else:
                piece = pieces[index % 2].at[index // 2]
            place = pl.multiple_of(info_ref[2 + index] * rows, rows)
            copies.append(
                pltpu.make_async_copy(
                    piece.at[pl.ds(0, rows), pl.ds(first, count)],
                    scratch.at[pl.ds(place, rows), pl.ds(target, count)],
                    sems.at[number, index],
                )
            )
    return copies


def load_shards(pairs_of, scratch, sems):
    copies = []
    rows = scratch.shape[0] // 8
    for number, (source, owner, first, count, target) in enumerate(pairs_of):
        for index in range(8):
            copies.append(
                pltpu.make_async_copy(
                    source.at[2 * index + owner, :, pl.ds(first, count)],
                    scratch.at[pl.ds(index * rows, rows), pl.ds(target, count)],
                    sems.at[number, index],
                )
            )
    return copies


def run_all(copies):
    for copy in copies:
        copy.start()
    for copy in copies:
        copy.wait()


def qkv_kernel(info_ref, mine_ref, got_ref, far_ref, gain_ref, bias_ref, hg_ref, mean_ref, *refs):
    pieces, refs = refs[:8], refs[8:]
    p_ref, rate_ref, ht_ref, w_ref, sems = refs
    sub = pl.program_id(1)

    @pl.when((pl.program_id(0) == 0) & (sub == 0))
    def _():
        run_all(load_pieces(info_ref, [(pieces, 0, w_ref.shape[1], 0)], w_ref, sems))

    first_core = info_ref[1] == 0
    moved = jnp.concatenate(
        [
            jnp.where(first_core, got_ref[0], far_ref[0]),
            jnp.where(first_core, far_ref[0], got_ref[0]),
        ],
        axis=0,
    )
    x = jnp.where(sub == info_ref[0], mine_ref[0], moved).astype(wide)
    centered = x - jnp.mean(x, axis=1, keepdims=True)
    variance = jnp.mean(centered * centered, axis=1, keepdims=True)
    h = (centered * lax.rsqrt(variance + norm_eps) * gain_ref[...] + bias_ref[...]).astype(low)
    ht_ref[...] = jnp.transpose(h)
    means = mean_ref[...]
    projected = dot(h, w_ref[...])
    for at in range(0, projected.shape[1], 128):
        raw = projected[:, at : at + 128]
        if at % 384 == 256:
            p_ref[0, :, at : at + 128] = raw.astype(low)
            continue
        inner = raw - split_dot(raw, means)
        rate = lax.rsqrt(dot((inner * inner).astype(low), means[:128]) + norm_eps)
        to = at // 384 * 256 + at % 384
        rate_ref[0, :, to : to + 128] = rate
        p_ref[0, :, at : at + 128] = (inner * rate * hg_ref[:, to : to + 128]).astype(low)


def attn_fwd_kernel(
    info_ref, start_ref, kind_ref, p_ref, aug_ref, side_ref, mine_ref, send_ref, inv_ref
):
    seq = pl.program_id(0)
    blocks = p_ref.shape[1] // query_block
    pairs = p_ref.shape[2] // 384
    lane = lax.broadcasted_iota(jnp.int32, (query_block, 128), 1)

    def step(block, carry):
        row = pl.multiple_of(block * query_block, query_block)
        which = seq * blocks + block

        def body(size):
            begin = pl.multiple_of(start_ref[which], 16)
            rows = pl.ds(row, query_block)
            span = pl.ds(begin, size)
            q_side = aug_ref[0, rows, :] * side_ref[...]
            k_side = aug_ref[0, span, :]
            ones = jnp.ones((size, 128), low)
            outcomes = []
            for pair in range(pairs):
                at = 384 * pair
                q_pair = p_ref[0, rows, at : at + 128]
                keys = jnp.concatenate([p_ref[0, span, at + 128 : at + 256], k_side], axis=1)
                values = jnp.concatenate([p_ref[0, span, at + 256 : at + 384], ones], axis=1)
                mixed = []
                for head in range(2):
                    mine = jnp.where(lane // 64 == head, q_pair, jnp.zeros_like(q_pair))
                    scores = dot(jnp.concatenate([mine, q_side], axis=1), keys, 1, 1)
                    mixed.append(dot(jnp.exp2(scores).astype(low), values))
                inverse = 1.0 / jnp.where(lane < 64, mixed[0][:, 128:], mixed[1][:, 128:])
                outcome = jnp.where(lane < 64, mixed[0][:, :128], mixed[1][:, :128]) * inverse
                outcomes.append(outcome.astype(low))
                inv_ref[0, rows, 128 * pair : 128 * pair + 128] = inverse
            outcome = jnp.concatenate(outcomes, axis=1)

            @pl.when(block % 2 == info_ref[1])
            def _():
                mine_ref[0, block // 2] = outcome

            @pl.when(block % 2 != info_ref[1])
            def _():
                send_ref[0, block // 2] = outcome

        for index, size in enumerate(windows):
            pl.when(kind_ref[which] == index)(partial(body, size))
        return carry

    lax.fori_loop(0, blocks, step, 0)


def attn_bwd_kernel(
    base,
    scale,
    first,
    final,
    info_ref,
    start_ref,
    kind_ref,
    p_ref,
    go_mine_ref,
    go_got_ref,
    o_mine_ref,
    o_send_ref,
    inv_ref,
    rate_ref,
    aug_ref,
    side_ref,
    hg_ref,
    mean_ref,
    ht_ref,
    *refs,
):
    pieces, refs = refs[:8], refs[8:]
    if not first:
        gw_in_ref, _, _, *refs = refs
    mine_ref, send_ref, gw_ref, gw_far_ref, gain_ref, *refs = refs
    gq_acc, gk_acc, gv_acc, g_all, gw_acc, w_ref, sems = refs
    step_id = pl.program_id(0)
    seq = step_id + base
    blocks = p_ref.shape[1] // query_block
    pairs = p_ref.shape[2] // 384
    lane = lax.broadcasted_iota(jnp.int32, (query_block, 128), 1)

    @pl.when(step_id == 0)
    def _():
        for copy in load_pieces(info_ref, [(pieces, 0, w_ref.shape[1], 0)], w_ref, sems):
            copy.start()
        gain_ref[...] = jnp.zeros_like(gain_ref)
        gw_acc[...] = jnp.zeros_like(gw_acc) if first else gw_in_ref[...]

    gk_acc[...] = jnp.zeros_like(gk_acc)
    gv_acc[...] = jnp.zeros_like(gv_acc)

    def step(block, carry):
        row = pl.multiple_of(block * query_block, query_block)
        which = seq * blocks + block

        def body(size):
            begin = pl.multiple_of(start_ref[which], 16)
            rows = pl.ds(row, query_block)
            span = pl.ds(begin, size)
            q_side = aug_ref[0, rows, :] * side_ref[...]
            k_side = aug_ref[0, span, :]
            near = block % 2 == info_ref[1]
            for pair in range(pairs):
                at = 384 * pair
                lanes = slice(128 * pair, 128 * pair + 128)
                q_pair = p_ref[0, rows, at : at + 128]
                k_pair = p_ref[0, span, at + 128 : at + 256]
                keys = jnp.concatenate([k_pair, k_side], axis=1)
                values = jnp.concatenate([p_ref[0, span, at + 256 : at + 384], k_side], axis=1)
                go = jnp.where(
                    near, go_mine_ref[0, block // 2, :, lanes], go_got_ref[0, block // 2, :, lanes]
                )
                o = jnp.where(
                    near, o_mine_ref[0, block // 2, :, lanes], o_send_ref[0, block // 2, :, lanes]
                )
                scaled = (go.astype(wide) * inv_ref[0, rows, lanes]).astype(low)
                product = scaled.astype(wide) * o.astype(wide)
                powers, grads, queries, pulls = [], [], [], []
                for head in range(2):
                    mine = lane // 64 == head
                    inner = jnp.sum(jnp.where(mine, product, 0.0), axis=1, keepdims=True)
                    one = inner.astype(low)
                    two = (inner - one.astype(wide)).astype(low)
                    three = (inner - one.astype(wide) - two.astype(wide)).astype(low)
                    none = jnp.zeros_like(q_pair)
                    go_side = jnp.where(
                        lane == 6,
                        -one,
                        jnp.where(lane == 7, -two, jnp.where(lane == 8, -three, none)),
                    )
                    q_mine = jnp.where(mine, q_pair, none)
                    go_mine = jnp.where(mine, scaled, none)
                    power = jnp.exp2(dot(keys, jnp.concatenate([q_mine, q_side], axis=1), 1, 1))
                    slope = dot(values, jnp.concatenate([go_mine, go_side], axis=1), 1, 1)
                    powers.append(power.astype(low))
                    grads.append((power * slope).astype(low))
                    queries.append(q_mine)
                    pulls.append(go_mine)
                gv_acc[span, lanes] += dot(
                    jnp.concatenate(powers, axis=1), jnp.concatenate(pulls, axis=0)
                )
                gk_acc[span, lanes] += dot(
                    jnp.concatenate(grads, axis=1), jnp.concatenate(queries, axis=0)
                )
                keys_turned = jnp.transpose(k_pair)
                turned = [dot(keys_turned[64 * i : 64 * i + 64], grads[i]) for i in range(2)]
                gq_acc[rows, lanes] = jnp.transpose(jnp.concatenate(turned, axis=0))

        for index, size in enumerate(windows):
            pl.when(kind_ref[which] == index)(partial(body, size))
        return carry

    lax.fori_loop(0, blocks, step, 0)
    means = mean_ref[...]
    for pair in range(pairs):
        lanes = slice(128 * pair, 128 * pair + 128)
        g_all[:, 384 * pair + 256 : 384 * pair + 384] = gv_acc[:, lanes].astype(low)
        for index, acc, factor, unscale in (
            (0, gq_acc, 0.125, 8.0 / log2e),
            (1, gk_acc, 1.0 / log2e, 1.0),
        ):
            to = slice(384 * pair + 128 * index, 384 * pair + 128 * index + 128)
            at = slice(256 * pair + 128 * index, 256 * pair + 128 * index + 128)
            gain = hg_ref[:, at]
            grad = acc[:, lanes] * factor
            normed = p_ref[0, :, to].astype(wide) * unscale
            weighted = grad * gain
            cross = grad * normed
            inner = split_dot(weighted, means)
            outer = split_dot(cross, means)
            g_all[:, to] = (
                rate_ref[0, :, at] * (weighted - inner - normed / gain * outer)
            ).astype(low)
            gain_ref[0:1, at] += jnp.sum(cross, axis=0, keepdims=True) / gain

    @pl.when(step_id == 0)
    def _():
        for copy in load_pieces(info_ref, [(pieces, 0, w_ref.shape[1], 0)], w_ref, sems):
            copy.wait()

    gw_acc[...] += dot(ht_ref[...], g_all[...])
    everything = dot(g_all[...], w_ref[...], 1, 1).astype(low)
    for block in range(blocks):
        result = everything[block * query_block : (block + 1) * query_block]

        @pl.when(block % 2 == info_ref[1])
        def _():
            mine_ref[0, block // 2] = result

        @pl.when(block % 2 != info_ref[1])
        def _():
            send_ref[0, block // 2] = result

    @pl.when(step_id == pl.num_programs(0) - 1)
    def _():
        if final:
            skip = gw_acc.shape[1] - gw_ref.shape[3]
            spread(info_ref, gw_acc, scale, gw_ref, skip * info_ref[0])
            spread(info_ref, gw_acc, scale, gw_far_ref, skip * (1 - info_ref[0]))
        else:
            gw_ref[...] = gw_acc[...]
            gw_far_ref[...] = jnp.zeros_like(gw_far_ref)


def spread(info_ref, acc, scale, ref, begin):
    rows, count = ref.shape[2:]
    for index in range(8):
        place = pl.multiple_of(info_ref[2 + index] * rows, rows)
        ref[index % 2, index // 2] = (
            acc[pl.ds(place, rows), pl.ds(pl.multiple_of(begin, 128), count)] * scale
        ).astype(low)


def put_blocks(stage, acc, scale, owners, to_col, count):
    rows = stage.shape[1]
    for number, owner in enumerate(owners):
        for index in range(8):
            stage[2 * index + owner, :, to_col : to_col + count] = (
                acc[index * rows : (index + 1) * rows, number * count : (number + 1) * count]
                * scale
            ).astype(low)


def norm_back(values, grad, gain):
    centered = values - jnp.mean(values, axis=1, keepdims=True)
    rate = lax.rsqrt(jnp.mean(centered * centered, axis=1, keepdims=True) + norm_eps)
    normed = centered * rate
    weighted = grad * gain
    result = rate * (
        weighted
        - jnp.mean(weighted, axis=1, keepdims=True)
        - normed * jnp.mean(weighted * normed, axis=1, keepdims=True)
    )
    return result, normed


def gelu_parts(t):
    root = math.sqrt(2.0 / math.pi)
    square = t * t
    gate = 0.5 + 0.5 * jnp.tanh(t * (root + (root * 0.044715) * square))
    act = t * gate
    slope = gate + 2.0 * act * (1.0 - gate) * (root + (3.0 * root * 0.044715) * square)
    return act, slope


def middle_kernel(
    scale,
    chunks,
    info_ref,
    o_mine_ref,
    o_got_ref,
    mine_ref,
    got_ref,
    gy_ref,
    valid_ref,
    gain_ref,
    bias_ref,
    shards,
    keep_near_ref,
    keep_far_ref,
    send_near_ref,
    send_far_ref,
    gx_ref,
    go_mine_ref,
    go_send_ref,
    sums_ref,
    grads,
    x2_all,
    h_all,
    ht_all,
    gy_all,
    gyt_all,
    out_all,
    gh_all,
    up_both,
    down_both,
    up_acc,
    down_acc,
    act_all,
    grad_all,
    wo_ref,
    wo_acc,
    stage,
    stage_out,
    weight_sems,
    stage_sem,
):
    phase = pl.program_id(0)
    r = pl.program_id(1)
    last = pl.num_programs(1) - 1
    cols = o_mine_ref.shape[3]
    part = o_mine_ref.shape[2]
    chunk = up_both.shape[2] // 2
    c = info_ref[1]
    first_half = info_ref[0] == 0

    def weight_copies(f, slot):
        begin = pl.multiple_of(cols + f * 2 * chunk, 128)
        sems = weight_sems.at[slot]
        return load_shards(
            [(shards, m, begin, chunk, m * chunk) for m in range(2)], up_both.at[slot], sems
        ) + load_shards(
            [(shards, m, begin + chunk, chunk, m * chunk) for m in range(2)],
            down_both.at[slot],
            sems.at[pl.ds(2, 2)],
        )

    def stage_copy(f):
        return pltpu.make_async_copy(
            stage,
            grads.at[:, :, pl.ds(pl.multiple_of(f * 2 * chunk, 128), 2 * chunk)],
            stage_sem.at[0],
        )

    def both_heads():
        return jnp.concatenate(
            [o_mine_ref[0].reshape(2 * part, cols), o_got_ref[0].reshape(2 * part, cols)], axis=1
        )

    @pl.when((phase == 0) & (r == 0))
    def _():
        copies = load_shards(
            [(shards, c, 0, cols, 0), (shards, 1 - c, 0, cols, cols)], wo_ref, weight_sems.at[1]
        )
        run_all(copies)
        for copy in weight_copies(0, 0):
            copy.start()
        sums_ref[...] = jnp.zeros_like(sums_ref)
        wo_acc[...] = jnp.zeros_like(wo_acc)

    @pl.when(phase == 0)
    def _():
        x = jnp.concatenate(
            [
                jnp.where(first_half, mine_ref[0], got_ref[0]),
                jnp.where(first_half, got_ref[0], mine_ref[0]),
            ],
            axis=0,
        ).astype(wide)
        x2 = x + dot(both_heads(), wo_ref[...], 1, 1)
        x2_all[r] = x2
        out_all[r] = x2
        gh_all[r] = jnp.zeros_like(x2)
        centered = x2 - jnp.mean(x2, axis=1, keepdims=True)
        variance = jnp.mean(centered * centered, axis=1, keepdims=True)
        h = (centered * lax.rsqrt(variance + norm_eps) * gain_ref[...] + bias_ref[...]).astype(low)
        h_all[r] = h
        ht_all[r] = jnp.transpose(h)
        gy = gy_ref[...]
        gy_all[r] = gy
        gyt_all[r] = jnp.transpose(gy)

    @pl.when((phase > 0) & (phase <= chunks))
    def _():
        f = phase - 1
        slot = f % 2

        @pl.when(r == 0)
        def _():
            for copy in weight_copies(f, slot):
                copy.wait()

        @pl.when((r == 0) & (f + 1 < chunks))
        def _():
            for copy in weight_copies(f + 1, 1 - slot):
                copy.start()

        up_ref = up_both.at[slot]
        down_ref = down_both.at[slot]
        h = h_all[r]
        gy = gy_all[r]
        size = 512
        for at in range(0, 2 * chunk, size):
            act, slope = gelu_parts(dot(h, up_ref[:, at : at + size]))
            act_all[:, at : at + size] = act.astype(low)
            grad_all[:, at : at + size] = (dot(gy, down_ref[:, at : at + size]) * slope).astype(low)
        out_all[r] += dot(act_all[...], down_ref[...], 1, 1)
        gh_all[r] += dot(grad_all[...], up_ref[...], 1, 1)

        @pl.when(r == 0)
        def _():
            up_acc[...] = jnp.zeros_like(up_acc)
            down_acc[...] = jnp.zeros_like(down_acc)

        up_acc[...] += dot(ht_all[r], grad_all[...])
        down_acc[...] += dot(gyt_all[r], act_all[...])

        @pl.when((r == last) & (f > 0))
        def _():
            stage_copy(f - 1).wait()

        @pl.when(r == last)
        def _():
            put_blocks(stage, up_acc, scale, (0, 1), 0, chunk)
            put_blocks(stage, down_acc, scale, (0, 1), chunk, chunk)
            stage_copy(f).start()

    @pl.when(phase == chunks + 1)
    def _():
        out = (out_all[r] * valid_ref[...][:, :1]).astype(low)
        keep = jnp.where(first_half, out[:part], out[part:])
        send = jnp.where(first_half, out[part:], out[:part])
        keep_near_ref[0] = jnp.where(c == 0, keep[:, :cols], keep[:, cols:])
        keep_far_ref[0] = jnp.where(c == 0, keep[:, cols:], keep[:, :cols])
        send_near_ref[0] = jnp.where(c == 0, send[:, :cols], send[:, cols:])
        send_far_ref[0] = jnp.where(c == 0, send[:, cols:], send[:, :cols])
        gh = gh_all[r]
        back, normed = norm_back(x2_all[r], gh, gain_ref[...])
        gx = gy_all[r].astype(wide) + back
        gx_ref[...] = gx
        gx_low = gx.astype(low)
        go = dot(gx_low, wo_ref[...]).astype(low)
        go_mine_ref[0] = go[:, :cols].reshape(2, part, cols)
        go_send_ref[0] = go[:, cols:].reshape(2, part, cols)
        turned = jnp.transpose(gx_low)
        sums_ref[0:1, :] += jnp.sum(gh * normed, axis=0, keepdims=True)
        sums_ref[1:2, :] += jnp.sum(gh, axis=0, keepdims=True)
        wo_acc[...] += dot(turned, both_heads())

        @pl.when(r == last)
        def _():
            stage_copy(chunks - 1).wait()
            put_blocks(stage_out, wo_acc, scale, (c, 1 - c), 0, cols)
            copy = pltpu.make_async_copy(
                stage_out, grads.at[:, :, pl.ds(chunks * 2 * chunk, cols)], stage_sem.at[1]
            )
            copy.start()
            copy.wait()


def first_norm_kernel(
    info_ref, mine_ref, got_ref, a_ref, b_ref, gx2_ref, gain_ref, keep_ref, send_ref, sums_ref
):
    half = pl.program_id(1)
    x = jnp.where(half == info_ref[0], mine_ref[0], got_ref[0]).astype(wide)
    gh = a_ref[0, 0].astype(wide) + b_ref[0, 0].astype(wide)
    back, normed = norm_back(x, gh, gain_ref[...])
    out = (gx2_ref[...] + back).astype(low)

    @pl.when(half == info_ref[0])
    def _():
        keep_ref[0] = out

    @pl.when(half != info_ref[0])
    def _():
        send_ref[0] = out

    @pl.when((pl.program_id(0) == 0) & (half == 0))
    def _():
        sums_ref[...] = jnp.zeros_like(sums_ref)

    sums_ref[0:1, :] += jnp.sum(gh * normed, axis=0, keepdims=True)
    sums_ref[1:2, :] += jnp.sum(gh, axis=0, keepdims=True)


def place_kernel(plan, seqs, info_ref, *refs):
    sources, (out_ref, sems) = refs[: len(plan)], refs[len(plan) :]
    y, c = info_ref[0], info_ref[1]
    copies = []
    for number, (source, (own_y, own_c, begin)) in enumerate(zip(sources, plan)):
        at = seqs * (y if own_y else 1 - y) + begin
        copies.append(
            pltpu.make_async_copy(
                source,
                out_ref.at[pl.ds(at, source.shape[0]), c if own_c else 1 - c],
                sems.at[number],
            )
        )
    run_all(copies)


def shape_of(dims, kind=low):
    return jax.ShapeDtypeStruct(dims, kind)


def window_table(segs, blocks):
    length = segs.shape[1]
    pad_begin = jnp.sum((segs >= 0).astype(jnp.int32), axis=1, keepdims=True)
    begins = jnp.where(segs >= 0, segs, pad_begin)
    size = length // blocks
    firsts = begins[:, ::size]
    lasts = begins[:, size - 1 :: size]
    ends = jnp.sum((begins[:, None, :] <= lasts[:, :, None]).astype(jnp.int32), axis=2)
    reach = ends - firsts
    kinds = jnp.zeros_like(reach)
    spans = jnp.full_like(reach, windows[0])
    for index in range(1, len(windows)):
        larger = reach > windows[index - 1]
        kinds = jnp.where(larger, index, kinds)
        spans = jnp.where(larger, windows[index], spans)
    starts = jnp.minimum(firsts, length - spans)
    return starts.reshape(-1), kinds.reshape(-1)


def mask_columns(segs):
    codes = (segs + 16) // 16
    lane = jnp.arange(128, dtype=jnp.int32)
    bits = (codes[:, :, None] >> jnp.minimum(lane, 5)) & 1
    signs = (2 * bits - 1).astype(wide)
    return jnp.where(lane < 6, signs, jnp.where(lane < 9, 1.0, 0.0)).astype(low)


def swap(values, axis):
    return lax.ppermute(values, axis, [(0, 1), (1, 0)])


def in_order(index, mine, other, axis):
    return jnp.where(
        index == 0,
        jnp.concatenate([mine, other], axis=axis),
        jnp.concatenate([other, mine], axis=axis),
    )


def pick(values, index, axis):
    return lax.dynamic_index_in_dim(values, index, axis, keepdims=False)


def shift_far(values, step):
    return lax.ppermute(
        values,
        "dp",
        [(2 * ((z + step) % 4) + x, 2 * z + x) for z in range(4) for x in range(2)],
    )


def swap_x(values):
    return lax.ppermute(values, "dp", [(d, d ^ 1) for d in range(8)])


def gather_pieces(shard):
    pieces = []
    for step in range(4):
        piece = shard if step == 0 else shift_far(shard, step)
        pieces += [piece, swap_x(piece)]
    return pieces


def on_device_small(
    patches, segments, w_qkv, w_out, w_up, w_down, ln_gain, ln_bias, head_gain, cotangent
):
    half, seqs_all, width = patches.shape
    length = 2 * half
    seqs = seqs_all // 2
    cols = w_qkv.shape[2]
    part = half // 2
    y = lax.axis_index("seq")
    c = lax.axis_index("mlp")
    d = lax.axis_index("dp")
    dp_size = lax.axis_size("dp")
    scale = 1.0 / math.sqrt(dp_size * seqs_all * length)
    own_rows = seqs * half
    hidden = w_up.shape[1]
    shard_rows = width // dp_size
    places = jnp.stack(
        [2 * ((d // 2 + index // 2) % 4) + ((d % 2) ^ (index % 2)) for index in range(8)]
    )
    info = jnp.concatenate([jnp.stack([y, c]), places]).astype(jnp.int32)

    turned = jnp.transpose(patches, (1, 0, 2)).reshape(2, seqs, 2, part, width)
    got = swap(pick(pick(turned, 1 - y, 0), c, 1), "seq")
    far = swap(got, "mlp")
    turned = turned.reshape(seqs_all, half, width)
    small = jnp.concatenate(
        [
            ln_gain.astype(low),
            ln_bias.astype(low),
            head_gain.astype(low).reshape(1, -1),
            jnp.zeros((3, shard_rows), low),
        ]
    )
    small = jnp.pad(small, ((0, 8), (0, 3 * cols - shard_rows)))
    pairs = cols // 128
    w_in = jnp.transpose(w_qkv.astype(low).reshape(3, shard_rows, pairs, 128), (1, 2, 0, 3))
    w_in = w_in.reshape(shard_rows, 3 * cols)
    in_pieces = gather_pieces(
        jnp.concatenate(
            [w_in, small]
        )
    )
    small = [piece[shard_rows : shard_rows + 8, :shard_rows] for piece in in_pieces]
    chunk = hidden_chunk
    chunks = hidden // chunk
    up_low = w_up.astype(low)
    down_low = jnp.transpose(w_down.astype(low))
    parts = [jnp.transpose(w_out.astype(low))]
    for f in range(chunks):
        at = slice(f * chunk, (f + 1) * chunk)
        parts += [up_low[:, at], down_low[:, at]]

    def gather_shards(parts):
        return lax.all_gather(jnp.concatenate(parts, axis=1), ("dp", "mlp"), axis=0)

    shards = gather_shards(parts)

    order = (places[None, :] == jnp.arange(8)[:, None]).astype(low)
    small = jnp.einsum("nr,rkw->knw", order, jnp.stack(small), preferred_element_type=wide)
    gains = small[0:2].reshape(2, width)
    biases = small[2:4].reshape(2, width)
    head_gains = jnp.transpose(small[4].reshape(dp_size, 2, cols // 64, 64 // dp_size), (1, 2, 0, 3))
    head_gains = jnp.transpose(head_gains.reshape(2, pairs, 128), (1, 0, 2))
    key_scale = jnp.array([[[log2e / 8.0], [1.0]]], wide)
    head_scaled = (head_gains * key_scale).reshape(1, 2 * cols)
    head_gains = head_gains.reshape(1, 2 * cols)

    segs = lax.dynamic_slice_in_dim(jnp.transpose(segments), y * seqs, seqs, 0)
    cot = cotangent.reshape(2, part, seqs_all, cols)
    cot_other = swap(pick(cot, 1 - c, 0), "mlp")
    cot = jnp.transpose(in_order(c, pick(cot, c, 0), cot_other, 2), (1, 0, 2))
    cot = cot.reshape(2, seqs, part, width)
    cot_got = swap(pick(cot, 1 - y, 0), "seq")
    cot = in_order(y, pick(cot, y, 0)[:, None], cot_got[:, None], 1)
    valid = pick((segs >= 0).reshape(seqs, 2, 2, part), c, 2)
    gy = jnp.where(valid[..., None], cot, jnp.zeros_like(cot)).reshape(own_rows, width)
    valid = jnp.broadcast_to(valid.reshape(own_rows, 1).astype(wide), (own_rows, 128))

    starts, kinds = window_table(segs, length // query_block)
    aug = mask_columns(segs)
    lanes = jnp.arange(128)
    side = jnp.where(lanes < 6, mask_weight, jnp.where(lanes == 6, -6.0 * mask_weight, 0.0))
    side = side.astype(low)[None]
    means = jnp.where(lanes[:, None] // 64 == lanes[None] // 64, 1.0 / 64, 0.0).astype(low)
    means = jnp.concatenate([means, means])
    anywhere = pl.BlockSpec(memory_space=pl.ANY)

    def whole(dims):
        return pl.BlockSpec(dims, lambda *ids: (0,) * len(dims))

    def call(kernel, grid, in_specs, out_specs, out_shape, scratch, name, scalars, pins=(), share=1, vmem=vmem_bytes, alias=None):
        work = int(micros[name] * 1150000000 / share)
        ends = scalars + len(in_specs)

        def unpinned(*refs):
            kernel(*refs[:ends], *refs[ends + len(pins) :])

        run = pl.pallas_call(
            unpinned,
            grid_spec=pltpu.PrefetchScalarGridSpec(
                num_scalar_prefetch=scalars,
                grid=grid,
                in_specs=in_specs + [anywhere] * len(pins),
                out_specs=out_specs,
                scratch_shapes=scratch,
            ),
            out_shape=out_shape,
            compiler_params=params(len(grid), vmem),
            input_output_aliases=alias or {},
            cost_estimate=pl.CostEstimate(flops=work, bytes_accessed=1000000, transcendentals=0),
            name=name,
        )
        return lambda *operands: run(*operands, *pins)

    piece_sems = pltpu.SemaphoreType.DMA((4, 8))
    one_seq = pl.BlockSpec((1, part, width), lambda s, j, *_: (s, 0, 0))
    projected, rates, h1t = call(
        qkv_kernel,
        (seqs, 2),
        [
            pl.BlockSpec((1, half, width), lambda s, j, info: (seqs * info[0] + s, 0, 0)),
            one_seq,
            one_seq,
            whole((1, width)),
            whole((1, width)),
            whole((1, 2 * cols)),
            whole((256, 128)),
        ]
        + [anywhere] * 8,
        [
            pl.BlockSpec((1, half, 3 * cols), lambda s, j, *_: (s, j, 0)),
            pl.BlockSpec((1, half, 2 * cols), lambda s, j, *_: (s, j, 0)),
            pl.BlockSpec((width, half), lambda s, j, *_: (0, 2 * s + j)),
        ],
        [
            shape_of((seqs, length, 3 * cols)),
            shape_of((seqs, length, 2 * cols), wide),
            shape_of((width, seqs * length)),
        ],
        [pltpu.VMEM((width, 3 * cols), low), piece_sems],
        "qkv",
        1,
    )(info, turned, got, far, gains[:1], biases[:1], head_scaled, means, *in_pieces)
    def per_seq(*dims, base=0):
        return pl.BlockSpec((1,) + dims, lambda s, *_: (s + base,) + (0,) * len(dims))

    o_mine, o_send, inverse = call(
        attn_fwd_kernel,
        (seqs,),
        [per_seq(length, 3 * cols), per_seq(length, 128), whole((1, 128))],
        [per_seq(2, part, cols), per_seq(2, part, cols), per_seq(length, cols)],
        [shape_of((seqs, 2, part, cols))] * 2 + [shape_of((seqs, length, cols), wide)],
        [],
        "attn_fwd",
        3,
    )(info, starts, kinds, projected, aug, side)

    o_got = swap(o_send, "mlp")
    seq_of = seqs - 1
    final = chunks + 1

    def at_ends(p, r):
        return jnp.where((p == 0) | (p == final), r, seq_of)

    def at_start(p, r):
        return jnp.where(p == 0, r, seq_of)

    def at_final(p, r):
        return jnp.where(p == final, r, 0)

    heads_spec = pl.BlockSpec((1, 2, part, cols), lambda p, r, *_: (at_ends(p, r), 0, 0, 0))
    moved_spec = pl.BlockSpec((1, part, cols), lambda p, r, *_: (at_final(p, r), 0, 0))
    heads_out = pl.BlockSpec((1, 2, part, cols), lambda p, r, *_: (at_final(p, r), 0, 0, 0))
    by_seq_bf = pltpu.VMEM((seqs, half, width), low)
    by_seq_turned = pltpu.VMEM((seqs, width, half), low)
    by_seq_wide = pltpu.VMEM((seqs, half, width), wide)
    grad_shape = (16, shard_rows, 2 * hidden + cols)
    keep_near, keep_far, send_near, send_far, gx2, go_mine, go_send, second_sums, grads = call(
        partial(middle_kernel, scale, chunks),
        (chunks + 2, seqs),
        [
            heads_spec,
            heads_spec,
            pl.BlockSpec(
                (1, part, width), lambda p, r, info: (seqs * info[0] + at_start(p, r), info[1], 0)
            ),
            pl.BlockSpec((1, part, width), lambda p, r, *_: (at_start(p, r), 0, 0)),
            pl.BlockSpec((half, width), lambda p, r, *_: (at_start(p, r), 0)),
            pl.BlockSpec((half, 128), lambda p, r, *_: (at_final(p, r), 0)),
            whole((1, width)),
            whole((1, width)),
            anywhere,
        ],
        [
            moved_spec,
            moved_spec,
            moved_spec,
            moved_spec,
            pl.BlockSpec((half, width), lambda p, r, *_: (at_final(p, r), 0)),
            heads_out,
            heads_out,
            whole((8, width)),
            anywhere,
        ],
        [
            shape_of((seqs, part, cols)),
            shape_of((seqs, part, cols)),
            shape_of((seqs, part, cols)),
            shape_of((seqs, part, cols)),
            shape_of((own_rows, width), wide),
            shape_of((seqs, 2, part, cols)),
            shape_of((seqs, 2, part, cols)),
            shape_of((8, width), wide),
            shape_of(grad_shape),
        ],
        [by_seq_wide, by_seq_bf, by_seq_turned, by_seq_bf, by_seq_turned, by_seq_wide, by_seq_wide]
        + [pltpu.VMEM((2, width, 2 * chunk), low)] * 2
        + [pltpu.VMEM((width, 2 * chunk), wide)] * 2
        + [pltpu.VMEM((half, 2 * chunk), low)] * 2
        + [
            pltpu.VMEM((width, width), low),
            pltpu.VMEM((width, width), wide),
            pltpu.VMEM((16, shard_rows, 2 * chunk), low),
            pltpu.VMEM((16, shard_rows, cols), low),
            pltpu.SemaphoreType.DMA((2, 4, 8)),
            pltpu.SemaphoreType.DMA((2,)),
        ],
        "middle",
        1,
        vmem=62 * 1024 * 1024,
    )(info, o_mine, o_got, turned, got, gy, valid, gains[1:], biases[1:], shards)
    go_got = swap(go_send, "mlp")
    got_near = swap(send_near, "seq")
    got_far = swap(send_far, "seq")
    scattered = lax.psum_scatter(grads, ("dp", "mlp"), scatter_dimension=0, tiled=True)[0]

    share_cols = (3 * cols // 128 + 1) // 2 * 128

    def attention_back(base, count, partial_sum, pins):
        first = partial_sum is None
        final = base + count == seqs
        shares = (2, 4, shard_rows, share_cols)
        carried = [] if first else list(partial_sum)
        return call(
            partial(attn_bwd_kernel, base, scale, first, final),
            (count,),
            [per_seq(length, 3 * cols, base=base)]
            + [per_seq(2, part, cols, base=base)] * 4
            + [
                per_seq(length, cols, base=base),
                per_seq(length, 2 * cols, base=base),
                per_seq(length, 128, base=base),
                whole((1, 128)),
                whole((1, 2 * cols)),
                whole((256, 128)),
                pl.BlockSpec((width, length), lambda s, *_: (0, s + base)),
            ]
            + [anywhere] * 8
            + ([] if first else [whole((width, 3 * cols)), anywhere, anywhere]),
            [per_seq(2, part, width, base=base)] * 2
            + [whole(shares if final else (width, 3 * cols))]
            + [whole(shares if final else (8, 128)), whole((8, 2 * cols))],
            [shape_of((seqs, 2, part, width))] * 2
            + [shape_of(shares) if final else shape_of((width, 3 * cols), wide)]
            + [shape_of(shares if final else (8, 128))]
            + [shape_of((8, 2 * cols), wide)],
            [pltpu.VMEM((length, cols), wide)] * 3
            + [
                pltpu.VMEM((length, 3 * cols), low),
                pltpu.VMEM((width, 3 * cols), wide),
                pltpu.VMEM((width, 3 * cols), low),
                piece_sems,
            ],
            "attn_bwd",
            3,
            pins,
            seqs / count,
            alias={} if first else {24: 0, 25: 1},
        )(
            info, starts, kinds, projected, go_mine, go_got, o_mine, o_send, inverse, rates,
            aug, side, head_gains, means, h1t, *in_pieces, *carried,
        )

    def first_back(base, count, mine, got_part, pins):
        here = pl.BlockSpec((1, 1, part, width), lambda s, h, *_: (s, h, 0, 0))
        moved = pl.BlockSpec((1, part, width), lambda s, h, *_: (s, 0, 0))
        return call(
            first_norm_kernel,
            (count, 2),
            [
                pl.BlockSpec(
                    (1, part, width), lambda s, h, info: (seqs * info[0] + s + base, info[1], 0)
                ),
                pl.BlockSpec((1, part, width), lambda s, h, *_: (s + base, 0, 0)),
                here,
                here,
                pl.BlockSpec((part, width), lambda s, h, *_: (2 * (s + base) + h, 0)),
                whole((1, width)),
            ],
            [moved, moved, whole((8, width))],
            [shape_of((count, part, width))] * 2 + [shape_of((8, width), wide)],
            [],
            "first_norm",
            1,
            pins,
            seqs / count,
        )(info, turned, got, mine, got_part, gx2, gains[:1])

    def place(sources, plan, feature_count, pins=()):
        return call(
            partial(place_kernel, plan, seqs),
            (1,),
            [anywhere] * len(plan),
            whole((seqs_all, 2, part, feature_count)),
            shape_of((seqs_all, 2, part, feature_count)),
            [pltpu.SemaphoreType.DMA((len(plan),))],
            "place",
            1,
            pins,
        )(info, *sources)

    mine, send, partial_sum, _, head_sums = attention_back(0, 1, None, ())
    keep_core = swap(keep_far, "mlp")
    mine, send, gw_near, gw_far, head_sums_b = attention_back(
        1, seqs - 1, (partial_sum, mine, send), [got_near, got_far, keep_core]
    )
    head_sums = head_sums + head_sums_b
    gw_got = swap(gw_far, "seq")
    moved = swap(send, "mlp")
    keep, give, first_sums = first_back(0, seqs, mine, moved, ())
    got_core = swap(got_far, "mlp")
    far_x = swap_x((gw_near[1].astype(wide) + gw_got[1].astype(wide)).astype(low))
    keep_moved = swap(keep, "mlp")
    got_grad = swap(give, "seq")

    norms = jnp.concatenate([first_sums[:2], second_sums[:2]]) * scale
    heads = jnp.transpose(head_sums[0].reshape(pairs, 2, 128), (1, 0, 2)) * scale
    heads = heads.reshape(2, cols // 64, dp_size, 64 // dp_size)
    heads = jnp.transpose(heads, (2, 0, 1, 3)).reshape(1, width)
    small = jnp.concatenate([norms + swap(norms, "mlp"), heads])
    small = small + swap(small, "seq")
    small = small + swap_x(small)
    small = small.reshape(5, 4, 2, shard_rows)
    small = lax.dynamic_index_in_dim(small, d % 2, 2, keepdims=False)
    small = jnp.concatenate([small, small], axis=1)
    small = lax.dynamic_slice_in_dim(small, d // 2, 4, 1)
    small = jnp.pad(jnp.transpose(small, (1, 2, 0)), ((0, 0), (0, 0), (0, 123)))
    total = gw_near[0].astype(wide) + gw_got[0].astype(wide) + far_x.astype(wide)
    total = jnp.concatenate([total, small], axis=2)
    low_total = total.astype(low)
    moved = [shift_far(low_total[step], 4 - step) for step in range(1, 4)]

    total = total[0] + sum(part.astype(wide) for part in moved)
    both = jnp.concatenate([scattered, total[:, :share_cols].astype(low)], axis=1)
    both_got = swap(both, "seq").astype(wide)
    scattered = scattered.astype(wide) + both_got[:, : scattered.shape[1]]
    total_got = both_got[:, scattered.shape[1] :]
    small = total[:, share_cols:]
    overlap = 2 * share_cols - 3 * cols
    gw_in = jnp.where(
        y == 0,
        jnp.concatenate([total[:, :share_cols], total_got[:, overlap:]], axis=1),
        jnp.concatenate([total_got[:, : 3 * cols - share_cols], total[:, :share_cols]], axis=1),
    )

    plan = [(True, True, 0), (True, False, 0), (False, True, 0), (False, False, 0)]
    out = place([keep_near, keep_core, got_near, got_core], plan, cols, [])
    out = jnp.transpose(out.reshape(seqs_all, half, cols), (1, 0, 2))
    grad_patches = place([keep, keep_moved, got_grad, swap(got_grad, "mlp")], plan, width, [])
    grad_patches = jnp.transpose(grad_patches.reshape(seqs_all, half, width), (1, 0, 2))

    gw_up = jnp.concatenate(
        [scattered[:, 2 * f * chunk : (2 * f + 1) * chunk] for f in range(chunks)], axis=1
    )
    gw_down = jnp.concatenate(
        [scattered[:, (2 * f + 1) * chunk : (2 * f + 2) * chunk] for f in range(chunks)], axis=1
    )
    gw_out = scattered[:, 2 * hidden :]
    gw_in = gw_in.reshape(shard_rows, pairs, 3, 128)
    gw_in = jnp.transpose(gw_in, (2, 0, 1, 3)).reshape(3, shard_rows, cols)
    norms = jnp.transpose(small[:, :4])
    heads = small[:, 4].reshape(2, cols // 64, 64 // dp_size)
    return (
        out,
        grad_patches,
        gw_in,
        jnp.transpose(gw_out),
        gw_up,
        jnp.transpose(gw_down),
        norms[0::2],
        norms[1::2],
        heads,
    )


def solution(mesh):
    shape = dict(mesh.shape)
    small = shape["seq"] == 2 and shape["mlp"] == 2 and shape["dp"] == 8
    return jax.shard_map(
        on_device_small if small else on_device,
        mesh=mesh,
        in_specs=(
            P("seq", "dp", None),
            P(None, "dp"),
            P(None, "dp", "mlp"),
            P("mlp", "dp"),
            P("dp", "mlp"),
            P("mlp", "dp"),
            P(None, "dp"),
            P(None, "dp"),
            P(None, "mlp", "dp"),
            P("seq", "dp", "mlp"),
        ),
        out_specs=(
            P("seq", "dp", "mlp"),
            P("seq", "dp", None),
            P(None, "dp", "mlp"),
            P("mlp", "dp"),
            P("dp", "mlp"),
            P("mlp", "dp"),
            P(None, "dp"),
            P(None, "dp"),
            P(None, "mlp", "dp"),
        ),
        check_vma=False,
    )
```

```python
from functools import partial
import math

import jax
import jax.numpy as jnp
from jax import lax
from jax.experimental import pallas as pl
from jax.experimental.pallas import tpu as pltpu
from jax.sharding import PartitionSpec as P

norm_eps = 1e-06
masked_value = -1e30


def layer_norm(values, gain_row, bias_row):
    average = jnp.mean(values, axis=-1, keepdims=True)
    centered = values - average
    variance = jnp.mean(centered * centered, axis=-1, keepdims=True)
    return centered * lax.rsqrt(variance + norm_eps) * gain_row + bias_row


def head_norm(values, gain_rows):
    average = jnp.mean(values, axis=-1, keepdims=True)
    centered = values - average
    variance = jnp.mean(centered * centered, axis=-1, keepdims=True)
    return centered * lax.rsqrt(variance + norm_eps) * gain_rows


def on_device(
    patches, segments, w_qkv, w_out, w_up, w_down, ln_gain, ln_bias, head_gain, cotangent
):
    (
        query_weight,
        out_weight,
        up_projection_weight,
        down_projection_weight,
        norm_gains,
        norm_biases,
        head_gains,
    ) = (
        lax.all_gather(w_qkv.astype(jnp.bfloat16), "dp", axis=1, tiled=True),
        lax.all_gather(w_out.astype(jnp.bfloat16), "dp", axis=1, tiled=True),
        lax.all_gather(w_up.astype(jnp.bfloat16), "dp", axis=0, tiled=True),
        lax.all_gather(w_down.astype(jnp.bfloat16), "dp", axis=1, tiled=True),
        lax.all_gather(ln_gain.astype(jnp.bfloat16), "dp", axis=1, tiled=True),
        lax.all_gather(ln_bias.astype(jnp.bfloat16), "dp", axis=1, tiled=True),
        lax.all_gather(head_gain.astype(jnp.bfloat16), "dp", axis=2, tiled=True),
    )
    local_rows = patches.shape[0]
    seq_here = patches.shape[1]
    width = patches.shape[2]
    head_cols = query_weight.shape[2]
    heads_here = head_gains.shape[1]
    head_size = head_gains.shape[2]
    seq_len = local_rows * lax.axis_size("seq")
    feature_cols = width // lax.axis_size("mlp")
    score_scale = head_size ** (-0.5)
    gain_float = norm_gains.astype(jnp.float32)
    bias_float = norm_biases.astype(jnp.float32)
    head_float = head_gains.astype(jnp.float32)
    seg_here = lax.dynamic_slice_in_dim(segments, lax.axis_index("seq") * local_rows, local_rows, 0)
    valid_mask = (seg_here >= 0).astype(jnp.float32)[:, :, None]
    query_segs = jnp.transpose(seg_here)
    key_segs = jnp.transpose(segments)
    patch_float = patches.astype(jnp.float32)
    normed = layer_norm(patch_float, gain_float[0], bias_float[0]).astype(jnp.bfloat16)
    projected = jnp.einsum(
        "lsd,cde->csle", normed, query_weight, preferred_element_type=jnp.float32
    )
    shape_heads = (seq_here, local_rows, heads_here, head_size)
    query_raw = projected[0].reshape(shape_heads)
    key_raw = projected[1].reshape(shape_heads)
    query_low = head_norm(query_raw, head_float[0]).astype(jnp.bfloat16)
    key_low = head_norm(key_raw, head_float[1]).astype(jnp.bfloat16)
    value_low = projected[2].astype(jnp.bfloat16)
    key_pairs = jnp.concatenate(
        [key_low.reshape(seq_here, local_rows, head_cols), value_low], axis=2
    )

    def split_pairs(gathered):
        key_heads = gathered[:, :head_cols].reshape(gathered.shape[0], heads_here, head_size)
        value_heads = gathered[:, head_cols:].reshape(gathered.shape[0], heads_here, head_size)
        return (key_heads, value_heads)

    def attend_forward(unused, inputs_seq):
        query_seq, pairs_seq, query_rows, key_rows = inputs_seq
        gathered = lax.all_gather(pairs_seq, "seq", axis=0, tiled=True)
        key_heads, value_heads = split_pairs(gathered)
        logits = (
            jnp.einsum("qhe,khe->hqk", query_seq, key_heads, preferred_element_type=jnp.float32)
            * score_scale
        )
        visible = (query_rows[:, None] == key_rows[None, :])[None]
        masked = jnp.where(visible, logits, masked_value)
        largest = jnp.max(masked, axis=2, keepdims=True)
        powered = jnp.exp(masked - largest)
        totals = jnp.sum(powered, axis=2, keepdims=True)
        attention = (powered / totals).astype(jnp.bfloat16)
        mixed = jnp.einsum(
            "hqk,khe->qhe", attention, value_heads, preferred_element_type=jnp.float32
        )
        log_total = (largest + jnp.log(totals))[:, :, 0]
        return (unused, (mixed.astype(jnp.bfloat16).reshape(local_rows, head_cols), log_total))

    _, (attn_heads, log_totals) = lax.scan(
        attend_forward, 0, (query_low, key_pairs, query_segs, key_segs)
    )
    attn_part = jnp.einsum(
        "slf,fd->lsd", attn_heads, out_weight, preferred_element_type=jnp.float32
    )
    attn_mine = lax.psum_scatter(
        attn_part.astype(jnp.bfloat16), "mlp", scatter_dimension=2, tiled=True
    ).astype(jnp.float32)
    patch_mine = lax.dynamic_slice_in_dim(
        patch_float, lax.axis_index("mlp") * feature_cols, feature_cols, 2
    )
    resid_mine = patch_mine + attn_mine
    residual = lax.all_gather(resid_mine.astype(jnp.bfloat16), "mlp", axis=2, tiled=True).astype(
        resid_mine.dtype
    )
    second_normalized = layer_norm(residual, gain_float[1], bias_float[1]).astype(jnp.bfloat16)
    hidden_pre = jnp.einsum(
        "own,nr->owr", second_normalized, up_projection_weight, preferred_element_type=jnp.float32
    )
    mlp_activation = jax.nn.gelu(hidden_pre, approximate=True).astype(jnp.bfloat16)
    branch_part = jnp.einsum(
        "ruo,oe->rue", mlp_activation, down_projection_weight, preferred_element_type=jnp.float32
    )
    branch_mine = lax.psum_scatter(
        branch_part.astype(jnp.bfloat16), "mlp", scatter_dimension=2, tiled=True
    ).astype(jnp.float32)
    out = (valid_mask * (resid_mine + branch_mine)).astype(jnp.bfloat16)
    cot_full = lax.all_gather(cotangent, "mlp", axis=2, tiled=True)
    grad_out = valid_mask * cot_full.astype(jnp.float32)
    output_gradient_reduced = grad_out.astype(jnp.bfloat16)
    grad_down = jnp.einsum(
        "xgr,xge->re", mlp_activation, output_gradient_reduced, preferred_element_type=jnp.float32
    )
    grad_act = jnp.einsum(
        "mit,nt->min",
        output_gradient_reduced,
        down_projection_weight,
        preferred_element_type=jnp.float32,
    )
    _, gelu_pull = jax.vjp(partial(jax.nn.gelu, approximate=True), hidden_pre)
    hidden_gradient = gelu_pull(grad_act)[0].astype(jnp.bfloat16)
    up_projection_gradient = jnp.einsum(
        "gih,giv->hv", second_normalized, hidden_gradient, preferred_element_type=jnp.float32
    )
    grad_normed_two = lax.psum(
        jnp.einsum(
            "vwb,kb->vwk", hidden_gradient, up_projection_weight, preferred_element_type=jnp.float32
        ).astype(jnp.bfloat16),
        "mlp",
    ).astype(jnp.float32)
    _, second_pull = jax.vjp(layer_norm, residual, gain_float[1], bias_float[1])
    grad_resid_norm, grad_gain_two, grad_bias_two = second_pull(grad_normed_two)
    grad_resid = grad_out + grad_resid_norm
    grad_resid_low = grad_resid.astype(jnp.bfloat16)
    grad_out_weight = jnp.einsum(
        "slf,lsd->fd", attn_heads, grad_resid_low, preferred_element_type=jnp.float32
    )
    grad_mixed = jnp.einsum(
        "lsd,fd->slf", grad_resid_low, out_weight, preferred_element_type=jnp.float32
    ).astype(jnp.bfloat16)

    def attend_backward(unused, inputs_seq):
        query_seq, pairs_seq, query_rows, key_rows, log_total, grad_seq = inputs_seq
        gathered = lax.all_gather(pairs_seq, "seq", axis=0, tiled=True)
        key_heads, value_heads = split_pairs(gathered)
        logits = (
            jnp.einsum("qhe,khe->hqk", query_seq, key_heads, preferred_element_type=jnp.float32)
            * score_scale
        )
        visible = (query_rows[:, None] == key_rows[None, :])[None]
        attention = jnp.exp(jnp.where(visible, logits - log_total[:, :, None], masked_value))
        attention_low = attention.astype(jnp.bfloat16)
        grad_heads = grad_seq.reshape(local_rows, heads_here, head_size)
        grad_attention = jnp.einsum(
            "qhe,khe->hqk", grad_heads, value_heads, preferred_element_type=jnp.float32
        )
        inner = jnp.sum(grad_attention * attention, axis=2, keepdims=True)
        grad_logits = (attention * (grad_attention - inner)).astype(jnp.bfloat16)
        grad_query = (
            jnp.einsum("hqk,khe->qhe", grad_logits, key_heads, preferred_element_type=jnp.float32)
            * score_scale
        )
        grad_key = (
            jnp.einsum("hqk,qhe->khe", grad_logits, query_seq, preferred_element_type=jnp.float32)
            * score_scale
        )
        grad_value = jnp.einsum(
            "hqk,qhe->khe", attention_low, grad_heads, preferred_element_type=jnp.float32
        )
        grad_pairs = lax.psum_scatter(
            jnp.concatenate(
                [
                    grad_key.reshape(lax.axis_size("seq") * local_rows, head_cols),
                    grad_value.reshape(lax.axis_size("seq") * local_rows, head_cols),
                ],
                axis=1,
            ).astype(jnp.bfloat16),
            "seq",
            scatter_dimension=0,
            tiled=True,
        ).astype(jnp.float32)
        return (unused, (grad_query.reshape(local_rows, head_cols), grad_pairs))

    _, (grad_queries, grad_pairs_all) = lax.scan(
        attend_backward, 0, (query_low, key_pairs, query_segs, key_segs, log_totals, grad_mixed)
    )
    _, query_pull = jax.vjp(head_norm, query_raw, head_float[0])
    grad_query_raw, grad_query_gain = query_pull(grad_queries.reshape(shape_heads))
    _, key_pull = jax.vjp(head_norm, key_raw, head_float[1])
    grad_key_raw, grad_key_gain = key_pull(grad_pairs_all[:, :, :head_cols].reshape(shape_heads))
    grad_projected = jnp.stack(
        [
            grad_query_raw.reshape(seq_here, local_rows, head_cols),
            grad_key_raw.reshape(seq_here, local_rows, head_cols),
            grad_pairs_all[:, :, head_cols:],
        ],
        axis=0,
    ).astype(jnp.bfloat16)
    grad_query_weight = jnp.einsum(
        "lsd,csle->cde", normed, grad_projected, preferred_element_type=jnp.float32
    )
    grad_normed = lax.psum(
        jnp.einsum(
            "csle,cde->lsd", grad_projected, query_weight, preferred_element_type=jnp.float32
        ).astype(jnp.bfloat16),
        "mlp",
    ).astype(jnp.float32)
    _, first_pull = jax.vjp(layer_norm, patch_float, gain_float[0], bias_float[0])
    grad_patch_norm, grad_gain_one, grad_bias_one = first_pull(grad_normed)
    grad_patches = (grad_resid + grad_patch_norm).astype(jnp.bfloat16)
    grad_scale = 1.0 / math.sqrt(lax.axis_size("dp") * seq_here * seq_len)
    term_qkv = grad_query_weight * grad_scale
    term_out = grad_out_weight * grad_scale
    term_up = up_projection_gradient * grad_scale
    term_down = grad_down * grad_scale
    term_gain = jnp.stack([grad_gain_one, grad_gain_two]) * grad_scale
    term_bias = jnp.stack([grad_bias_one, grad_bias_two]) * grad_scale
    term_head = jnp.stack([grad_query_gain, grad_key_gain]) * grad_scale
    summed = (
        lax.psum(term_qkv.astype(jnp.bfloat16), "seq").astype(jnp.float32),
        lax.psum(term_out.astype(jnp.bfloat16), "seq").astype(jnp.float32),
        lax.psum(term_up.astype(jnp.bfloat16), "seq").astype(jnp.float32),
        lax.psum(term_down.astype(jnp.bfloat16), "seq").astype(jnp.float32),
        lax.psum(term_gain.astype(jnp.bfloat16), "seq").astype(jnp.float32),
        lax.psum(term_bias.astype(jnp.bfloat16), "seq").astype(jnp.float32),
        lax.psum(term_head.astype(jnp.bfloat16), "seq").astype(jnp.float32),
    )
    shards = (
        lax.psum_scatter(
            summed[0].astype(jnp.bfloat16), "dp", scatter_dimension=1, tiled=True
        ).astype(jnp.float32),
        lax.psum_scatter(
            summed[1].astype(jnp.bfloat16), "dp", scatter_dimension=1, tiled=True
        ).astype(jnp.float32),
        lax.psum_scatter(
            summed[2].astype(jnp.bfloat16), "dp", scatter_dimension=0, tiled=True
        ).astype(jnp.float32),
        lax.psum_scatter(
            summed[3].astype(jnp.bfloat16), "dp", scatter_dimension=1, tiled=True
        ).astype(jnp.float32),
        lax.psum_scatter(
            summed[4].astype(jnp.bfloat16), "dp", scatter_dimension=1, tiled=True
        ).astype(jnp.float32),
        lax.psum_scatter(
            summed[5].astype(jnp.bfloat16), "dp", scatter_dimension=1, tiled=True
        ).astype(jnp.float32),
        lax.psum_scatter(
            summed[6].astype(jnp.bfloat16), "dp", scatter_dimension=2, tiled=True
        ).astype(jnp.float32),
    )
    return (
        out,
        grad_patches,
        shards[0],
        shards[1],
        shards[2],
        shards[3],
        shards[4],
        shards[5],
        shards[6],
    )


low = jnp.bfloat16
wide = jnp.float32
log2e = math.log2(math.e)
mask_weight = 128.0
query_block = 256
windows = (512, 1024)
vmem_bytes = 56 * 1024 * 1024
hidden_chunk = 512
micros = {
    "qkv": 25,
    "attn_fwd": 22,
    "middle": 80,
    "attn_bwd": 75,
    "first_norm": 8,
    "place": 4,
}


def dot(left, right, left_dim=1, right_dim=0):
    return lax.dot_general(
        left, right, (((left_dim,), (right_dim,)), ((), ())), preferred_element_type=wide
    )


def params(count, vmem):
    return pltpu.CompilerParams(
        dimension_semantics=("arbitrary",) * count, vmem_limit_bytes=vmem
    )


def split_dot(values, ones_matrix):
    top = values.astype(low)
    rest = (values - top.astype(wide)).astype(low)
    return dot(jnp.concatenate([top, rest], axis=1), ones_matrix)


def load_pieces(info_ref, sets, scratch, sems):
    copies = []
    rows = scratch.shape[0] // 8
    for number, (pieces, first, count, target) in enumerate(sets):
        for index in range(8):
            if len(pieces) == 8:
                piece = pieces[index]
            else:
                piece = pieces[index % 2].at[index // 2]
            place = pl.multiple_of(info_ref[2 + index] * rows, rows)
            copies.append(
                pltpu.make_async_copy(
                    piece.at[pl.ds(0, rows), pl.ds(first, count)],
                    scratch.at[pl.ds(place, rows), pl.ds(target, count)],
                    sems.at[number, index],
                )
            )
    return copies


def load_shards(pairs_of, scratch, sems):
    copies = []
    rows = scratch.shape[0] // 8
    for number, (source, owner, first, count, target) in enumerate(pairs_of):
        for index in range(8):
            copies.append(
                pltpu.make_async_copy(
                    source.at[2 * index + owner, :, pl.ds(first, count)],
                    scratch.at[pl.ds(index * rows, rows), pl.ds(target, count)],
                    sems.at[number, index],
                )
            )
    return copies


def run_all(copies):
    for copy in copies:
        copy.start()
    for copy in copies:
        copy.wait()


def qkv_kernel(info_ref, mine_ref, got_ref, far_ref, gain_ref, bias_ref, hg_ref, mean_ref, *refs):
    pieces, refs = refs[:8], refs[8:]
    p_ref, rate_ref, ht_ref, w_ref, sems = refs
    sub = pl.program_id(1)

    @pl.when((pl.program_id(0) == 0) & (sub == 0))
    def _():
        run_all(load_pieces(info_ref, [(pieces, 0, w_ref.shape[1], 0)], w_ref, sems))

    first_core = info_ref[1] == 0
    moved = jnp.concatenate(
        [
            jnp.where(first_core, got_ref[0], far_ref[0]),
            jnp.where(first_core, far_ref[0], got_ref[0]),
        ],
        axis=0,
    )
    x = jnp.where(sub == info_ref[0], mine_ref[0], moved).astype(wide)
    centered = x - jnp.mean(x, axis=1, keepdims=True)
    variance = jnp.mean(centered * centered, axis=1, keepdims=True)
    h = (centered * lax.rsqrt(variance + norm_eps) * gain_ref[...] + bias_ref[...]).astype(low)
    ht_ref[...] = jnp.transpose(h)
    means = mean_ref[...]
    projected = dot(h, w_ref[...])
    for at in range(0, projected.shape[1], 128):
        raw = projected[:, at : at + 128]
        if at % 384 == 256:
            p_ref[0, :, at : at + 128] = raw.astype(low)
            continue
        inner = raw - split_dot(raw, means)
        rate = lax.rsqrt(dot((inner * inner).astype(low), means[:128]) + norm_eps)
        to = at // 384 * 256 + at % 384
        rate_ref[0, :, to : to + 128] = rate
        p_ref[0, :, at : at + 128] = (inner * rate * hg_ref[:, to : to + 128]).astype(low)


def attn_fwd_kernel(
    info_ref, start_ref, kind_ref, p_ref, aug_ref, side_ref, mine_ref, send_ref, inv_ref
):
    seq = pl.program_id(0)
    blocks = p_ref.shape[1] // query_block
    pairs = p_ref.shape[2] // 384
    lane = lax.broadcasted_iota(jnp.int32, (query_block, 128), 1)

    def step(block, carry):
        row = pl.multiple_of(block * query_block, query_block)
        which = seq * blocks + block

        def body(size):
            begin = pl.multiple_of(start_ref[which], 16)
            rows = pl.ds(row, query_block)
            span = pl.ds(begin, size)
            q_side = aug_ref[0, rows, :] * side_ref[...]
            k_side = aug_ref[0, span, :]
            ones = jnp.ones((size, 128), low)
            outcomes = []
            for pair in range(pairs):
                at = 384 * pair
                q_pair = p_ref[0, rows, at : at + 128]
                keys = jnp.concatenate([p_ref[0, span, at + 128 : at + 256], k_side], axis=1)
                values = jnp.concatenate([p_ref[0, span, at + 256 : at + 384], ones], axis=1)
                mixed = []
                for head in range(2):
                    mine = jnp.where(lane // 64 == head, q_pair, jnp.zeros_like(q_pair))
                    scores = dot(jnp.concatenate([mine, q_side], axis=1), keys, 1, 1)
                    mixed.append(dot(jnp.exp2(scores).astype(low), values))
                inverse = 1.0 / jnp.where(lane < 64, mixed[0][:, 128:], mixed[1][:, 128:])
                outcome = jnp.where(lane < 64, mixed[0][:, :128], mixed[1][:, :128]) * inverse
                outcomes.append(outcome.astype(low))
                inv_ref[0, rows, 128 * pair : 128 * pair + 128] = inverse
            outcome = jnp.concatenate(outcomes, axis=1)

            @pl.when(block % 2 == info_ref[1])
            def _():
                mine_ref[0, block // 2] = outcome

            @pl.when(block % 2 != info_ref[1])
            def _():
                send_ref[0, block // 2] = outcome

        for index, size in enumerate(windows):
            pl.when(kind_ref[which] == index)(partial(body, size))
        return carry

    lax.fori_loop(0, blocks, step, 0)


def attn_bwd_kernel(
    base,
    scale,
    first,
    final,
    info_ref,
    start_ref,
    kind_ref,
    p_ref,
    go_mine_ref,
    go_got_ref,
    o_mine_ref,
    o_send_ref,
    inv_ref,
    rate_ref,
    aug_ref,
    side_ref,
    hg_ref,
    mean_ref,
    ht_ref,
    *refs,
):
    pieces, refs = refs[:8], refs[8:]
    if not first:
        gw_in_ref, _, _, *refs = refs
    mine_ref, send_ref, gw_ref, gw_far_ref, gain_ref, *refs = refs
    gq_acc, gk_acc, gv_acc, g_all, gw_acc, w_ref, sems = refs
    step_id = pl.program_id(0)
    seq = step_id + base
    blocks = p_ref.shape[1] // query_block
    pairs = p_ref.shape[2] // 384
    lane = lax.broadcasted_iota(jnp.int32, (query_block, 128), 1)

    @pl.when(step_id == 0)
    def _():
        for copy in load_pieces(info_ref, [(pieces, 0, w_ref.shape[1], 0)], w_ref, sems):
            copy.start()
        gain_ref[...] = jnp.zeros_like(gain_ref)
        gw_acc[...] = jnp.zeros_like(gw_acc) if first else gw_in_ref[...]

    gk_acc[...] = jnp.zeros_like(gk_acc)
    gv_acc[...] = jnp.zeros_like(gv_acc)

    def step(block, carry):
        row = pl.multiple_of(block * query_block, query_block)
        which = seq * blocks + block

        def body(size):
            begin = pl.multiple_of(start_ref[which], 16)
            rows = pl.ds(row, query_block)
            span = pl.ds(begin, size)
            q_side = aug_ref[0, rows, :] * side_ref[...]
            k_side = aug_ref[0, span, :]
            near = block % 2 == info_ref[1]
            for pair in range(pairs):
                at = 384 * pair
                lanes = slice(128 * pair, 128 * pair + 128)
                q_pair = p_ref[0, rows, at : at + 128]
                k_pair = p_ref[0, span, at + 128 : at + 256]
                keys = jnp.concatenate([k_pair, k_side], axis=1)
                values = jnp.concatenate([p_ref[0, span, at + 256 : at + 384], k_side], axis=1)
                go = jnp.where(
                    near, go_mine_ref[0, block // 2, :, lanes], go_got_ref[0, block // 2, :, lanes]
                )
                o = jnp.where(
                    near, o_mine_ref[0, block // 2, :, lanes], o_send_ref[0, block // 2, :, lanes]
                )
                scaled = (go.astype(wide) * inv_ref[0, rows, lanes]).astype(low)
                product = scaled.astype(wide) * o.astype(wide)
                powers, grads, queries, pulls = [], [], [], []
                for head in range(2):
                    mine = lane // 64 == head
                    inner = jnp.sum(jnp.where(mine, product, 0.0), axis=1, keepdims=True)
                    one = inner.astype(low)
                    two = (inner - one.astype(wide)).astype(low)
                    three = (inner - one.astype(wide) - two.astype(wide)).astype(low)
                    none = jnp.zeros_like(q_pair)
                    go_side = jnp.where(
                        lane == 6,
                        -one,
                        jnp.where(lane == 7, -two, jnp.where(lane == 8, -three, none)),
                    )
                    q_mine = jnp.where(mine, q_pair, none)
                    go_mine = jnp.where(mine, scaled, none)
                    power = jnp.exp2(dot(keys, jnp.concatenate([q_mine, q_side], axis=1), 1, 1))
                    slope = dot(values, jnp.concatenate([go_mine, go_side], axis=1), 1, 1)
                    powers.append(power.astype(low))
                    grads.append((power * slope).astype(low))
                    queries.append(q_mine)
                    pulls.append(go_mine)
                gv_acc[span, lanes] += dot(
                    jnp.concatenate(powers, axis=1), jnp.concatenate(pulls, axis=0)
                )
                gk_acc[span, lanes] += dot(
                    jnp.concatenate(grads, axis=1), jnp.concatenate(queries, axis=0)
                )
                keys_turned = jnp.transpose(k_pair)
                turned = [dot(keys_turned[64 * i : 64 * i + 64], grads[i]) for i in range(2)]
                gq_acc[rows, lanes] = jnp.transpose(jnp.concatenate(turned, axis=0))

        for index, size in enumerate(windows):
            pl.when(kind_ref[which] == index)(partial(body, size))
        return carry

    lax.fori_loop(0, blocks, step, 0)
    means = mean_ref[...]
    for pair in range(pairs):
        lanes = slice(128 * pair, 128 * pair + 128)
        g_all[:, 384 * pair + 256 : 384 * pair + 384] = gv_acc[:, lanes].astype(low)
        for index, acc, factor, unscale in (
            (0, gq_acc, 0.125, 8.0 / log2e),
            (1, gk_acc, 1.0 / log2e, 1.0),
        ):
            to = slice(384 * pair + 128 * index, 384 * pair + 128 * index + 128)
            at = slice(256 * pair + 128 * index, 256 * pair + 128 * index + 128)
            gain = hg_ref[:, at]
            grad = acc[:, lanes] * factor
            normed = p_ref[0, :, to].astype(wide) * unscale
            weighted = grad * gain
            cross = grad * normed
            inner = split_dot(weighted, means)
            outer = split_dot(cross, means)
            g_all[:, to] = (
                rate_ref[0, :, at] * (weighted - inner - normed / gain * outer)
            ).astype(low)
            gain_ref[0:1, at] += jnp.sum(cross, axis=0, keepdims=True) / gain

    @pl.when(step_id == 0)
    def _():
        for copy in load_pieces(info_ref, [(pieces, 0, w_ref.shape[1], 0)], w_ref, sems):
            copy.wait()

    gw_acc[...] += dot(ht_ref[...], g_all[...])
    everything = dot(g_all[...], w_ref[...], 1, 1).astype(low)
    for block in range(blocks):
        result = everything[block * query_block : (block + 1) * query_block]

        @pl.when(block % 2 == info_ref[1])
        def _():
            mine_ref[0, block // 2] = result

        @pl.when(block % 2 != info_ref[1])
        def _():
            send_ref[0, block // 2] = result

    @pl.when(step_id == pl.num_programs(0) - 1)
    def _():
        if final:
            skip = gw_acc.shape[1] - gw_ref.shape[3]
            spread(info_ref, gw_acc, scale, gw_ref, skip * info_ref[0])
            spread(info_ref, gw_acc, scale, gw_far_ref, skip * (1 - info_ref[0]))
        else:
            gw_ref[...] = gw_acc[...]
            gw_far_ref[...] = jnp.zeros_like(gw_far_ref)


def spread(info_ref, acc, scale, ref, begin):
    rows, count = ref.shape[2:]
    for index in range(8):
        place = pl.multiple_of(info_ref[2 + index] * rows, rows)
        ref[index % 2, index // 2] = (
            acc[pl.ds(place, rows), pl.ds(pl.multiple_of(begin, 128), count)] * scale
        ).astype(low)


def put_blocks(stage, acc, scale, owners, to_col, count):
    rows = stage.shape[1]
    for number, owner in enumerate(owners):
        for index in range(8):
            stage[2 * index + owner, :, to_col : to_col + count] = (
                acc[index * rows : (index + 1) * rows, number * count : (number + 1) * count]
                * scale
            ).astype(low)


def norm_back(values, grad, gain):
    centered = values - jnp.mean(values, axis=1, keepdims=True)
    rate = lax.rsqrt(jnp.mean(centered * centered, axis=1, keepdims=True) + norm_eps)
    normed = centered * rate
    weighted = grad * gain
    result = rate * (
        weighted
        - jnp.mean(weighted, axis=1, keepdims=True)
        - normed * jnp.mean(weighted * normed, axis=1, keepdims=True)
    )
    return result, normed


def gelu_parts(t):
    root = math.sqrt(2.0 / math.pi)
    square = t * t
    gate = 0.5 + 0.5 * jnp.tanh(t * (root + (root * 0.044715) * square))
    act = t * gate
    slope = gate + 2.0 * act * (1.0 - gate) * (root + (3.0 * root * 0.044715) * square)
    return act, slope


def middle_kernel(
    scale,
    chunks,
    info_ref,
    o_mine_ref,
    o_got_ref,
    mine_ref,
    got_ref,
    gy_ref,
    valid_ref,
    gain_ref,
    bias_ref,
    shards,
    keep_near_ref,
    keep_far_ref,
    send_near_ref,
    send_far_ref,
    gx_ref,
    go_mine_ref,
    go_send_ref,
    sums_ref,
    grads,
    x2_all,
    h_all,
    ht_all,
    gy_all,
    gyt_all,
    out_all,
    gh_all,
    up_both,
    down_both,
    up_acc,
    down_acc,
    act_all,
    grad_all,
    wo_ref,
    wo_acc,
    stage,
    stage_out,
    weight_sems,
    stage_sem,
):
    phase = pl.program_id(0)
    r = pl.program_id(1)
    last = pl.num_programs(1) - 1
    cols = o_mine_ref.shape[3]
    part = o_mine_ref.shape[2]
    chunk = up_both.shape[2] // 2
    c = info_ref[1]
    first_half = info_ref[0] == 0

    def weight_copies(f, slot):
        begin = pl.multiple_of(cols + f * 2 * chunk, 128)
        sems = weight_sems.at[slot]
        return load_shards(
            [(shards, m, begin, chunk, m * chunk) for m in range(2)], up_both.at[slot], sems
        ) + load_shards(
            [(shards, m, begin + chunk, chunk, m * chunk) for m in range(2)],
            down_both.at[slot],
            sems.at[pl.ds(2, 2)],
        )

    def stage_copy(f):
        return pltpu.make_async_copy(
            stage,
            grads.at[:, :, pl.ds(pl.multiple_of(f * 2 * chunk, 128), 2 * chunk)],
            stage_sem.at[0],
        )

    def both_heads():
        return jnp.concatenate(
            [o_mine_ref[0].reshape(2 * part, cols), o_got_ref[0].reshape(2 * part, cols)], axis=1
        )

    @pl.when((phase == 0) & (r == 0))
    def _():
        copies = load_shards(
            [(shards, c, 0, cols, 0), (shards, 1 - c, 0, cols, cols)], wo_ref, weight_sems.at[1]
        )
        run_all(copies)
        for copy in weight_copies(0, 0):
            copy.start()
        sums_ref[...] = jnp.zeros_like(sums_ref)
        wo_acc[...] = jnp.zeros_like(wo_acc)

    @pl.when(phase == 0)
    def _():
        x = jnp.concatenate(
            [
                jnp.where(first_half, mine_ref[0], got_ref[0]),
                jnp.where(first_half, got_ref[0], mine_ref[0]),
            ],
            axis=0,
        ).astype(wide)
        x2 = x + dot(both_heads(), wo_ref[...], 1, 1)
        x2_all[r] = x2
        out_all[r] = x2
        gh_all[r] = jnp.zeros_like(x2)
        centered = x2 - jnp.mean(x2, axis=1, keepdims=True)
        variance = jnp.mean(centered * centered, axis=1, keepdims=True)
        h = (centered * lax.rsqrt(variance + norm_eps) * gain_ref[...] + bias_ref[...]).astype(low)
        h_all[r] = h
        ht_all[r] = jnp.transpose(h)
        gy = gy_ref[...]
        gy_all[r] = gy
        gyt_all[r] = jnp.transpose(gy)

    @pl.when((phase > 0) & (phase <= chunks))
    def _():
        f = phase - 1
        slot = f % 2

        @pl.when(r == 0)
        def _():
            for copy in weight_copies(f, slot):
                copy.wait()

        @pl.when((r == 0) & (f + 1 < chunks))
        def _():
            for copy in weight_copies(f + 1, 1 - slot):
                copy.start()

        up_ref = up_both.at[slot]
        down_ref = down_both.at[slot]
        h = h_all[r]
        gy = gy_all[r]
        size = 512
        for at in range(0, 2 * chunk, size):
            act, slope = gelu_parts(dot(h, up_ref[:, at : at + size]))
            act_all[:, at : at + size] = act.astype(low)
            grad_all[:, at : at + size] = (dot(gy, down_ref[:, at : at + size]) * slope).astype(low)
        out_all[r] += dot(act_all[...], down_ref[...], 1, 1)
        gh_all[r] += dot(grad_all[...], up_ref[...], 1, 1)

        @pl.when(r == 0)
        def _():
            up_acc[...] = jnp.zeros_like(up_acc)
            down_acc[...] = jnp.zeros_like(down_acc)

        up_acc[...] += dot(ht_all[r], grad_all[...])
        down_acc[...] += dot(gyt_all[r], act_all[...])

        @pl.when((r == last) & (f > 0))
        def _():
            stage_copy(f - 1).wait()

        @pl.when(r == last)
        def _():
            put_blocks(stage, up_acc, scale, (0, 1), 0, chunk)
            put_blocks(stage, down_acc, scale, (0, 1), chunk, chunk)
            stage_copy(f).start()

    @pl.when(phase == chunks + 1)
    def _():
        out = (out_all[r] * valid_ref[...][:, :1]).astype(low)
        keep = jnp.where(first_half, out[:part], out[part:])
        send = jnp.where(first_half, out[part:], out[:part])
        keep_near_ref[0] = jnp.where(c == 0, keep[:, :cols], keep[:, cols:])
        keep_far_ref[0] = jnp.where(c == 0, keep[:, cols:], keep[:, :cols])
        send_near_ref[0] = jnp.where(c == 0, send[:, :cols], send[:, cols:])
        send_far_ref[0] = jnp.where(c == 0, send[:, cols:], send[:, :cols])
        gh = gh_all[r]
        back, normed = norm_back(x2_all[r], gh, gain_ref[...])
        gx = gy_all[r].astype(wide) + back
        gx_ref[...] = gx
        gx_low = gx.astype(low)
        go = dot(gx_low, wo_ref[...]).astype(low)
        go_mine_ref[0] = go[:, :cols].reshape(2, part, cols)
        go_send_ref[0] = go[:, cols:].reshape(2, part, cols)
        turned = jnp.transpose(gx_low)
        sums_ref[0:1, :] += jnp.sum(gh * normed, axis=0, keepdims=True)
        sums_ref[1:2, :] += jnp.sum(gh, axis=0, keepdims=True)
        wo_acc[...] += dot(turned, both_heads())

        @pl.when(r == last)
        def _():
            stage_copy(chunks - 1).wait()
            put_blocks(stage_out, wo_acc, scale, (c, 1 - c), 0, cols)
            copy = pltpu.make_async_copy(
                stage_out, grads.at[:, :, pl.ds(chunks * 2 * chunk, cols)], stage_sem.at[1]
            )
            copy.start()
            copy.wait()


def first_norm_kernel(
    info_ref, mine_ref, got_ref, a_ref, b_ref, gx2_ref, gain_ref, keep_ref, send_ref, sums_ref
):
    half = pl.program_id(1)
    x = jnp.where(half == info_ref[0], mine_ref[0], got_ref[0]).astype(wide)
    gh = a_ref[0, 0].astype(wide) + b_ref[0, 0].astype(wide)
    back, normed = norm_back(x, gh, gain_ref[...])
    out = (gx2_ref[...] + back).astype(low)

    @pl.when(half == info_ref[0])
    def _():
        keep_ref[0] = out

    @pl.when(half != info_ref[0])
    def _():
        send_ref[0] = out

    @pl.when((pl.program_id(0) == 0) & (half == 0))
    def _():
        sums_ref[...] = jnp.zeros_like(sums_ref)

    sums_ref[0:1, :] += jnp.sum(gh * normed, axis=0, keepdims=True)
    sums_ref[1:2, :] += jnp.sum(gh, axis=0, keepdims=True)


def place_kernel(plan, seqs, info_ref, *refs):
    sources, (out_ref, sems) = refs[: len(plan)], refs[len(plan) :]
    y, c = info_ref[0], info_ref[1]
    copies = []
    for number, (source, (own_y, own_c, begin)) in enumerate(zip(sources, plan)):
        at = seqs * (y if own_y else 1 - y) + begin
        copies.append(
            pltpu.make_async_copy(
                source,
                out_ref.at[pl.ds(at, source.shape[0]), c if own_c else 1 - c],
                sems.at[number],
            )
        )
    run_all(copies)


def shape_of(dims, kind=low):
    return jax.ShapeDtypeStruct(dims, kind)


def window_table(segs, blocks):
    length = segs.shape[1]
    pad_begin = jnp.sum((segs >= 0).astype(jnp.int32), axis=1, keepdims=True)
    begins = jnp.where(segs >= 0, segs, pad_begin)
    size = length // blocks
    firsts = begins[:, ::size]
    lasts = begins[:, size - 1 :: size]
    ends = jnp.sum((begins[:, None, :] <= lasts[:, :, None]).astype(jnp.int32), axis=2)
    reach = ends - firsts
    kinds = jnp.zeros_like(reach)
    spans = jnp.full_like(reach, windows[0])
    for index in range(1, len(windows)):
        larger = reach > windows[index - 1]
        kinds = jnp.where(larger, index, kinds)
        spans = jnp.where(larger, windows[index], spans)
    starts = jnp.minimum(firsts, length - spans)
    return starts.reshape(-1), kinds.reshape(-1)


def mask_columns(segs):
    codes = (segs + 16) // 16
    lane = jnp.arange(128, dtype=jnp.int32)
    bits = (codes[:, :, None] >> jnp.minimum(lane, 5)) & 1
    signs = (2 * bits - 1).astype(wide)
    return jnp.where(lane < 6, signs, jnp.where(lane < 9, 1.0, 0.0)).astype(low)


def swap(values, axis):
    return lax.ppermute(values, axis, [(0, 1), (1, 0)])


def in_order(index, mine, other, axis):
    return jnp.where(
        index == 0,
        jnp.concatenate([mine, other], axis=axis),
        jnp.concatenate([other, mine], axis=axis),
    )


def pick(values, index, axis):
    return lax.dynamic_index_in_dim(values, index, axis, keepdims=False)


def shift_far(values, step):
    return lax.ppermute(
        values,
        "dp",
        [(2 * ((z + step) % 4) + x, 2 * z + x) for z in range(4) for x in range(2)],
    )


def swap_x(values):
    return lax.ppermute(values, "dp", [(d, d ^ 1) for d in range(8)])


def gather_pieces(shard):
    pieces = []
    for step in range(4):
        piece = shard if step == 0 else shift_far(shard, step)
        pieces += [piece, swap_x(piece)]
    return pieces


def on_device_small(
    patches, segments, w_qkv, w_out, w_up, w_down, ln_gain, ln_bias, head_gain, cotangent
):
    half, seqs_all, width = patches.shape
    length = 2 * half
    seqs = seqs_all // 2
    cols = w_qkv.shape[2]
    part = half // 2
    y = lax.axis_index("seq")
    c = lax.axis_index("mlp")
    d = lax.axis_index("dp")
    dp_size = lax.axis_size("dp")
    scale = 1.0 / math.sqrt(dp_size * seqs_all * length)
    own_rows = seqs * half
    hidden = w_up.shape[1]
    shard_rows = width // dp_size
    places = jnp.stack(
        [2 * ((d // 2 + index // 2) % 4) + ((d % 2) ^ (index % 2)) for index in range(8)]
    )
    info = jnp.concatenate([jnp.stack([y, c]), places]).astype(jnp.int32)

    turned = jnp.transpose(patches, (1, 0, 2)).reshape(2, seqs, 2, part, width)
    got = swap(pick(pick(turned, 1 - y, 0), c, 1), "seq")
    far = swap(got, "mlp")
    turned = turned.reshape(seqs_all, half, width)
    small = jnp.concatenate(
        [
            ln_gain.astype(low),
            ln_bias.astype(low),
            head_gain.astype(low).reshape(1, -1),
            jnp.zeros((3, shard_rows), low),
        ]
    )
    small = jnp.pad(small, ((0, 8), (0, 3 * cols - shard_rows)))
    pairs = cols // 128
    w_in = jnp.transpose(w_qkv.astype(low).reshape(3, shard_rows, pairs, 128), (1, 2, 0, 3))
    w_in = w_in.reshape(shard_rows, 3 * cols)
    in_pieces = gather_pieces(
        jnp.concatenate(
            [w_in, small]
        )
    )
    small = [piece[shard_rows : shard_rows + 8, :shard_rows] for piece in in_pieces]
    chunk = hidden_chunk
    chunks = hidden // chunk
    up_low = w_up.astype(low)
    down_low = jnp.transpose(w_down.astype(low))
    parts = [jnp.transpose(w_out.astype(low))]
    for f in range(chunks):
        at = slice(f * chunk, (f + 1) * chunk)
        parts += [up_low[:, at], down_low[:, at]]

    def gather_shards(parts):
        return lax.all_gather(jnp.concatenate(parts, axis=1), ("dp", "mlp"), axis=0)

    shards = gather_shards(parts)

    order = (places[None, :] == jnp.arange(8)[:, None]).astype(low)
    small = jnp.einsum("nr,rkw->knw", order, jnp.stack(small), preferred_element_type=wide)
    gains = small[0:2].reshape(2, width)
    biases = small[2:4].reshape(2, width)
    head_gains = jnp.transpose(small[4].reshape(dp_size, 2, cols // 64, 64 // dp_size), (1, 2, 0, 3))
    head_gains = jnp.transpose(head_gains.reshape(2, pairs, 128), (1, 0, 2))
    key_scale = jnp.array([[[log2e / 8.0], [1.0]]], wide)
    head_scaled = (head_gains * key_scale).reshape(1, 2 * cols)
    head_gains = head_gains.reshape(1, 2 * cols)

    segs = lax.dynamic_slice_in_dim(jnp.transpose(segments), y * seqs, seqs, 0)
    cot = cotangent.reshape(2, part, seqs_all, cols)
    cot_other = swap(pick(cot, 1 - c, 0), "mlp")
    cot = jnp.transpose(in_order(c, pick(cot, c, 0), cot_other, 2), (1, 0, 2))
    cot = cot.reshape(2, seqs, part, width)
    cot_got = swap(pick(cot, 1 - y, 0), "seq")
    cot = in_order(y, pick(cot, y, 0)[:, None], cot_got[:, None], 1)
    valid = pick((segs >= 0).reshape(seqs, 2, 2, part), c, 2)
    gy = jnp.where(valid[..., None], cot, jnp.zeros_like(cot)).reshape(own_rows, width)
    valid = jnp.broadcast_to(valid.reshape(own_rows, 1).astype(wide), (own_rows, 128))

    starts, kinds = window_table(segs, length // query_block)
    aug = mask_columns(segs)
    lanes = jnp.arange(128)
    side = jnp.where(lanes < 6, mask_weight, jnp.where(lanes == 6, -6.0 * mask_weight, 0.0))
    side = side.astype(low)[None]
    means = jnp.where(lanes[:, None] // 64 == lanes[None] // 64, 1.0 / 64, 0.0).astype(low)
    means = jnp.concatenate([means, means])
    anywhere = pl.BlockSpec(memory_space=pl.ANY)

    def whole(dims):
        return pl.BlockSpec(dims, lambda *ids: (0,) * len(dims))

    def call(kernel, grid, in_specs, out_specs, out_shape, scratch, name, scalars, pins=(), share=1, vmem=vmem_bytes, alias=None):
        work = int(micros[name] * 1150000000 / share)
        ends = scalars + len(in_specs)

        def unpinned(*refs):
            kernel(*refs[:ends], *refs[ends + len(pins) :])

        run = pl.pallas_call(
            unpinned,
            grid_spec=pltpu.PrefetchScalarGridSpec(
                num_scalar_prefetch=scalars,
                grid=grid,
                in_specs=in_specs + [anywhere] * len(pins),
                out_specs=out_specs,
                scratch_shapes=scratch,
            ),
            out_shape=out_shape,
            compiler_params=params(len(grid), vmem),
            input_output_aliases=alias or {},
            cost_estimate=pl.CostEstimate(flops=work, bytes_accessed=1000000, transcendentals=0),
            name=name,
        )
        return lambda *operands: run(*operands, *pins)

    piece_sems = pltpu.SemaphoreType.DMA((4, 8))
    one_seq = pl.BlockSpec((1, part, width), lambda s, j, *_: (s, 0, 0))
    projected, rates, h1t = call(
        qkv_kernel,
        (seqs, 2),
        [
            pl.BlockSpec((1, half, width), lambda s, j, info: (seqs * info[0] + s, 0, 0)),
            one_seq,
            one_seq,
            whole((1, width)),
            whole((1, width)),
            whole((1, 2 * cols)),
            whole((256, 128)),
        ]
        + [anywhere] * 8,
        [
            pl.BlockSpec((1, half, 3 * cols), lambda s, j, *_: (s, j, 0)),
            pl.BlockSpec((1, half, 2 * cols), lambda s, j, *_: (s, j, 0)),
            pl.BlockSpec((width, half), lambda s, j, *_: (0, 2 * s + j)),
        ],
        [
            shape_of((seqs, length, 3 * cols)),
            shape_of((seqs, length, 2 * cols), wide),
            shape_of((width, seqs * length)),
        ],
        [pltpu.VMEM((width, 3 * cols), low), piece_sems],
        "qkv",
        1,
    )(info, turned, got, far, gains[:1], biases[:1], head_scaled, means, *in_pieces)
    def per_seq(*dims, base=0):
        return pl.BlockSpec((1,) + dims, lambda s, *_: (s + base,) + (0,) * len(dims))

    o_mine, o_send, inverse = call(
        attn_fwd_kernel,
        (seqs,),
        [per_seq(length, 3 * cols), per_seq(length, 128), whole((1, 128))],
        [per_seq(2, part, cols), per_seq(2, part, cols), per_seq(length, cols)],
        [shape_of((seqs, 2, part, cols))] * 2 + [shape_of((seqs, length, cols), wide)],
        [],
        "attn_fwd",
        3,
    )(info, starts, kinds, projected, aug, side)

    o_got = swap(o_send, "mlp")
    seq_of = seqs - 1
    final = chunks + 1

    def at_ends(p, r):
        return jnp.where((p == 0) | (p == final), r, seq_of)

    def at_start(p, r):
        return jnp.where(p == 0, r, seq_of)

    def at_final(p, r):
        return jnp.where(p == final, r, 0)

    heads_spec = pl.BlockSpec((1, 2, part, cols), lambda p, r, *_: (at_ends(p, r), 0, 0, 0))
    moved_spec = pl.BlockSpec((1, part, cols), lambda p, r, *_: (at_final(p, r), 0, 0))
    heads_out = pl.BlockSpec((1, 2, part, cols), lambda p, r, *_: (at_final(p, r), 0, 0, 0))
    by_seq_bf = pltpu.VMEM((seqs, half, width), low)
    by_seq_turned = pltpu.VMEM((seqs, width, half), low)
    by_seq_wide = pltpu.VMEM((seqs, half, width), wide)
    grad_shape = (16, shard_rows, 2 * hidden + cols)
    keep_near, keep_far, send_near, send_far, gx2, go_mine, go_send, second_sums, grads = call(
        partial(middle_kernel, scale, chunks),
        (chunks + 2, seqs),
        [
            heads_spec,
            heads_spec,
            pl.BlockSpec(
                (1, part, width), lambda p, r, info: (seqs * info[0] + at_start(p, r), info[1], 0)
            ),
            pl.BlockSpec((1, part, width), lambda p, r, *_: (at_start(p, r), 0, 0)),
            pl.BlockSpec((half, width), lambda p, r, *_: (at_start(p, r), 0)),
            pl.BlockSpec((half, 128), lambda p, r, *_: (at_final(p, r), 0)),
            whole((1, width)),
            whole((1, width)),
            anywhere,
        ],
        [
            moved_spec,
            moved_spec,
            moved_spec,
            moved_spec,
            pl.BlockSpec((half, width), lambda p, r, *_: (at_final(p, r), 0)),
            heads_out,
            heads_out,
            whole((8, width)),
            anywhere,
        ],
        [
            shape_of((seqs, part, cols)),
            shape_of((seqs, part, cols)),
            shape_of((seqs, part, cols)),
            shape_of((seqs, part, cols)),
            shape_of((own_rows, width), wide),
            shape_of((seqs, 2, part, cols)),
            shape_of((seqs, 2, part, cols)),
            shape_of((8, width), wide),
            shape_of(grad_shape),
        ],
        [by_seq_wide, by_seq_bf, by_seq_turned, by_seq_bf, by_seq_turned, by_seq_wide, by_seq_wide]
        + [pltpu.VMEM((2, width, 2 * chunk), low)] * 2
        + [pltpu.VMEM((width, 2 * chunk), wide)] * 2
        + [pltpu.VMEM((half, 2 * chunk), low)] * 2
        + [
            pltpu.VMEM((width, width), low),
            pltpu.VMEM((width, width), wide),
            pltpu.VMEM((16, shard_rows, 2 * chunk), low),
            pltpu.VMEM((16, shard_rows, cols), low),
            pltpu.SemaphoreType.DMA((2, 4, 8)),
            pltpu.SemaphoreType.DMA((2,)),
        ],
        "middle",
        1,
        vmem=62 * 1024 * 1024,
    )(info, o_mine, o_got, turned, got, gy, valid, gains[1:], biases[1:], shards)
    go_got = swap(go_send, "mlp")
    got_near = swap(send_near, "seq")
    got_far = swap(send_far, "seq")
    scattered = lax.psum_scatter(grads, ("dp", "mlp"), scatter_dimension=0, tiled=True)[0]

    share_cols = (3 * cols // 128 + 1) // 2 * 128

    def attention_back(base, count, partial_sum, pins):
        first = partial_sum is None
        final = base + count == seqs
        shares = (2, 4, shard_rows, share_cols)
        carried = [] if first else list(partial_sum)
        return call(
            partial(attn_bwd_kernel, base, scale, first, final),
            (count,),
            [per_seq(length, 3 * cols, base=base)]
            + [per_seq(2, part, cols, base=base)] * 4
            + [
                per_seq(length, cols, base=base),
                per_seq(length, 2 * cols, base=base),
                per_seq(length, 128, base=base),
                whole((1, 128)),
                whole((1, 2 * cols)),
                whole((256, 128)),
                pl.BlockSpec((width, length), lambda s, *_: (0, s + base)),
            ]
            + [anywhere] * 8
            + ([] if first else [whole((width, 3 * cols)), anywhere, anywhere]),
            [per_seq(2, part, width, base=base)] * 2
            + [whole(shares if final else (width, 3 * cols))]
            + [whole(shares if final else (8, 128)), whole((8, 2 * cols))],
            [shape_of((seqs, 2, part, width))] * 2
            + [shape_of(shares) if final else shape_of((width, 3 * cols), wide)]
            + [shape_of(shares if final else (8, 128))]
            + [shape_of((8, 2 * cols), wide)],
            [pltpu.VMEM((length, cols), wide)] * 3
            + [
                pltpu.VMEM((length, 3 * cols), low),
                pltpu.VMEM((width, 3 * cols), wide),
                pltpu.VMEM((width, 3 * cols), low),
                piece_sems,
            ],
            "attn_bwd",
            3,
            pins,
            seqs / count,
            alias={} if first else {24: 0, 25: 1},
        )(
            info, starts, kinds, projected, go_mine, go_got, o_mine, o_send, inverse, rates,
            aug, side, head_gains, means, h1t, *in_pieces, *carried,
        )

    def first_back(base, count, mine, got_part, pins):
        here = pl.BlockSpec((1, 1, part, width), lambda s, h, *_: (s, h, 0, 0))
        moved = pl.BlockSpec((1, part, width), lambda s, h, *_: (s, 0, 0))
        return call(
            first_norm_kernel,
            (count, 2),
            [
                pl.BlockSpec(
                    (1, part, width), lambda s, h, info: (seqs * info[0] + s + base, info[1], 0)
                ),
                pl.BlockSpec((1, part, width), lambda s, h, *_: (s + base, 0, 0)),
                here,
                here,
                pl.BlockSpec((part, width), lambda s, h, *_: (2 * (s + base) + h, 0)),
                whole((1, width)),
            ],
            [moved, moved, whole((8, width))],
            [shape_of((count, part, width))] * 2 + [shape_of((8, width), wide)],
            [],
            "first_norm",
            1,
            pins,
            seqs / count,
        )(info, turned, got, mine, got_part, gx2, gains[:1])

    def place(sources, plan, feature_count, pins=()):
        return call(
            partial(place_kernel, plan, seqs),
            (1,),
            [anywhere] * len(plan),
            whole((seqs_all, 2, part, feature_count)),
            shape_of((seqs_all, 2, part, feature_count)),
            [pltpu.SemaphoreType.DMA((len(plan),))],
            "place",
            1,
            pins,
        )(info, *sources)

    mine, send, partial_sum, _, head_sums = attention_back(0, 1, None, ())
    keep_core = swap(keep_far, "mlp")
    mine, send, gw_near, gw_far, head_sums_b = attention_back(
        1, seqs - 1, (partial_sum, mine, send), [got_near, got_far, keep_core]
    )
    head_sums = head_sums + head_sums_b
    gw_got = swap(gw_far, "seq")
    moved = swap(send, "mlp")
    keep, give, first_sums = first_back(0, seqs, mine, moved, ())
    got_core = swap(got_far, "mlp")
    far_x = swap_x((gw_near[1].astype(wide) + gw_got[1].astype(wide)).astype(low))
    keep_moved = swap(keep, "mlp")
    got_grad = swap(give, "seq")

    norms = jnp.concatenate([first_sums[:2], second_sums[:2]]) * scale
    heads = jnp.transpose(head_sums[0].reshape(pairs, 2, 128), (1, 0, 2)) * scale
    heads = heads.reshape(2, cols // 64, dp_size, 64 // dp_size)
    heads = jnp.transpose(heads, (2, 0, 1, 3)).reshape(1, width)
    small = jnp.concatenate([norms + swap(norms, "mlp"), heads])
    small = small + swap(small, "seq")
    small = small + swap_x(small)
    small = small.reshape(5, 4, 2, shard_rows)
    small = lax.dynamic_index_in_dim(small, d % 2, 2, keepdims=False)
    small = jnp.concatenate([small, small], axis=1)
    small = lax.dynamic_slice_in_dim(small, d // 2, 4, 1)
    small = jnp.pad(jnp.transpose(small, (1, 2, 0)), ((0, 0), (0, 0), (0, 123)))
    total = gw_near[0].astype(wide) + gw_got[0].astype(wide) + far_x.astype(wide)
    total = jnp.concatenate([total, small], axis=2)
    low_total = total.astype(low)
    moved = [shift_far(low_total[step], 4 - step) for step in range(1, 4)]

    total = total[0] + sum(part.astype(wide) for part in moved)
    both = jnp.concatenate([scattered, total[:, :share_cols].astype(low)], axis=1)
    both_got = swap(both, "seq").astype(wide)
    scattered = scattered.astype(wide) + both_got[:, : scattered.shape[1]]
    total_got = both_got[:, scattered.shape[1] :]
    small = total[:, share_cols:]
    overlap = 2 * share_cols - 3 * cols
    gw_in = jnp.where(
        y == 0,
        jnp.concatenate([total[:, :share_cols], total_got[:, overlap:]], axis=1),
        jnp.concatenate([total_got[:, : 3 * cols - share_cols], total[:, :share_cols]], axis=1),
    )

    plan = [(True, True, 0), (True, False, 0), (False, True, 0), (False, False, 0)]
    out = place([keep_near, keep_core, got_near, got_core], plan, cols, [])
    out = jnp.transpose(out.reshape(seqs_all, half, cols), (1, 0, 2))
    grad_patches = place([keep, keep_moved, got_grad, swap(got_grad, "mlp")], plan, width, [])
    grad_patches = jnp.transpose(grad_patches.reshape(seqs_all, half, width), (1, 0, 2))

    gw_up = jnp.concatenate(
        [scattered[:, 2 * f * chunk : (2 * f + 1) * chunk] for f in range(chunks)], axis=1
    )
    gw_down = jnp.concatenate(
        [scattered[:, (2 * f + 1) * chunk : (2 * f + 2) * chunk] for f in range(chunks)], axis=1
    )
    gw_out = scattered[:, 2 * hidden :]
    gw_in = gw_in.reshape(shard_rows, pairs, 3, 128)
    gw_in = jnp.transpose(gw_in, (2, 0, 1, 3)).reshape(3, shard_rows, cols)
    norms = jnp.transpose(small[:, :4])
    heads = small[:, 4].reshape(2, cols // 64, 64 // dp_size)
    return (
        out,
        grad_patches,
        gw_in,
        jnp.transpose(gw_out),
        gw_up,
        jnp.transpose(gw_down),
        norms[0::2],
        norms[1::2],
        heads,
    )


def solution(mesh):
    shape = dict(mesh.shape)
    small = shape["seq"] == 2 and shape["mlp"] == 2 and shape["dp"] == 8
    return jax.shard_map(
        on_device_small if small else on_device,
        mesh=mesh,
        in_specs=(
            P("seq", "dp", None),
            P(None, "dp"),
            P(None, "dp", "mlp"),
            P("mlp", "dp"),
            P("dp", "mlp"),
            P("mlp", "dp"),
            P(None, "dp"),
            P(None, "dp"),
            P(None, "mlp", "dp"),
            P("seq", "dp", "mlp"),
        ),
        out_specs=(
            P("seq", "dp", "mlp"),
            P("seq", "dp", None),
            P(None, "dp", "mlp"),
            P("mlp", "dp"),
            P("dp", "mlp"),
            P("mlp", "dp"),
            P(None, "dp"),
            P(None, "dp"),
            P(None, "mlp", "dp"),
        ),
        check_vma=False,
    )
```

```python
from functools import partial
import math

import jax
import jax.numpy as jnp
from jax import lax
from jax.experimental import pallas as pl
from jax.experimental.pallas import tpu as pltpu
from jax.sharding import PartitionSpec as P

norm_eps = 1e-06
masked_value = -1e30


def layer_norm(values, gain_row, bias_row):
    average = jnp.mean(values, axis=-1, keepdims=True)
    centered = values - average
    variance = jnp.mean(centered * centered, axis=-1, keepdims=True)
    return centered * lax.rsqrt(variance + norm_eps) * gain_row + bias_row


def head_norm(values, gain_rows):
    average = jnp.mean(values, axis=-1, keepdims=True)
    centered = values - average
    variance = jnp.mean(centered * centered, axis=-1, keepdims=True)
    return centered * lax.rsqrt(variance + norm_eps) * gain_rows


def on_device(
    patches, segments, w_qkv, w_out, w_up, w_down, ln_gain, ln_bias, head_gain, cotangent
):
    (
        query_weight,
        out_weight,
        up_projection_weight,
        down_projection_weight,
        norm_gains,
        norm_biases,
        head_gains,
    ) = (
        lax.all_gather(w_qkv.astype(jnp.bfloat16), "dp", axis=1, tiled=True),
        lax.all_gather(w_out.astype(jnp.bfloat16), "dp", axis=1, tiled=True),
        lax.all_gather(w_up.astype(jnp.bfloat16), "dp", axis=0, tiled=True),
        lax.all_gather(w_down.astype(jnp.bfloat16), "dp", axis=1, tiled=True),
        lax.all_gather(ln_gain.astype(jnp.bfloat16), "dp", axis=1, tiled=True),
        lax.all_gather(ln_bias.astype(jnp.bfloat16), "dp", axis=1, tiled=True),
        lax.all_gather(head_gain.astype(jnp.bfloat16), "dp", axis=2, tiled=True),
    )
    local_rows = patches.shape[0]
    seq_here = patches.shape[1]
    width = patches.shape[2]
    head_cols = query_weight.shape[2]
    heads_here = head_gains.shape[1]
    head_size = head_gains.shape[2]
    seq_len = local_rows * lax.axis_size("seq")
    feature_cols = width // lax.axis_size("mlp")
    score_scale = head_size ** (-0.5)
    gain_float = norm_gains.astype(jnp.float32)
    bias_float = norm_biases.astype(jnp.float32)
    head_float = head_gains.astype(jnp.float32)
    seg_here = lax.dynamic_slice_in_dim(segments, lax.axis_index("seq") * local_rows, local_rows, 0)
    valid_mask = (seg_here >= 0).astype(jnp.float32)[:, :, None]
    query_segs = jnp.transpose(seg_here)
    key_segs = jnp.transpose(segments)
    patch_float = patches.astype(jnp.float32)
    normed = layer_norm(patch_float, gain_float[0], bias_float[0]).astype(jnp.bfloat16)
    projected = jnp.einsum(
        "lsd,cde->csle", normed, query_weight, preferred_element_type=jnp.float32
    )
    shape_heads = (seq_here, local_rows, heads_here, head_size)
    query_raw = projected[0].reshape(shape_heads)
    key_raw = projected[1].reshape(shape_heads)
    query_low = head_norm(query_raw, head_float[0]).astype(jnp.bfloat16)
    key_low = head_norm(key_raw, head_float[1]).astype(jnp.bfloat16)
    value_low = projected[2].astype(jnp.bfloat16)
    key_pairs = jnp.concatenate(
        [key_low.reshape(seq_here, local_rows, head_cols), value_low], axis=2
    )

    def split_pairs(gathered):
        key_heads = gathered[:, :head_cols].reshape(gathered.shape[0], heads_here, head_size)
        value_heads = gathered[:, head_cols:].reshape(gathered.shape[0], heads_here, head_size)
        return (key_heads, value_heads)

    def attend_forward(unused, inputs_seq):
        query_seq, pairs_seq, query_rows, key_rows = inputs_seq
        gathered = lax.all_gather(pairs_seq, "seq", axis=0, tiled=True)
        key_heads, value_heads = split_pairs(gathered)
        logits = (
            jnp.einsum("qhe,khe->hqk", query_seq, key_heads, preferred_element_type=jnp.float32)
            * score_scale
        )
        visible = (query_rows[:, None] == key_rows[None, :])[None]
        masked = jnp.where(visible, logits, masked_value)
        largest = jnp.max(masked, axis=2, keepdims=True)
        powered = jnp.exp(masked - largest)
        totals = jnp.sum(powered, axis=2, keepdims=True)
        attention = (powered / totals).astype(jnp.bfloat16)
        mixed = jnp.einsum(
            "hqk,khe->qhe", attention, value_heads, preferred_element_type=jnp.float32
        )
        log_total = (largest + jnp.log(totals))[:, :, 0]
        return (unused, (mixed.astype(jnp.bfloat16).reshape(local_rows, head_cols), log_total))

    _, (attn_heads, log_totals) = lax.scan(
        attend_forward, 0, (query_low, key_pairs, query_segs, key_segs)
    )
    attn_part = jnp.einsum(
        "slf,fd->lsd", attn_heads, out_weight, preferred_element_type=jnp.float32
    )
    attn_mine = lax.psum_scatter(
        attn_part.astype(jnp.bfloat16), "mlp", scatter_dimension=2, tiled=True
    ).astype(jnp.float32)
    patch_mine = lax.dynamic_slice_in_dim(
        patch_float, lax.axis_index("mlp") * feature_cols, feature_cols, 2
    )
    resid_mine = patch_mine + attn_mine
    residual = lax.all_gather(resid_mine.astype(jnp.bfloat16), "mlp", axis=2, tiled=True).astype(
        resid_mine.dtype
    )
    second_normalized = layer_norm(residual, gain_float[1], bias_float[1]).astype(jnp.bfloat16)
    hidden_pre = jnp.einsum(
        "own,nr->owr", second_normalized, up_projection_weight, preferred_element_type=jnp.float32
    )
    mlp_activation = jax.nn.gelu(hidden_pre, approximate=True).astype(jnp.bfloat16)
    branch_part = jnp.einsum(
        "ruo,oe->rue", mlp_activation, down_projection_weight, preferred_element_type=jnp.float32
    )
    branch_mine = lax.psum_scatter(
        branch_part.astype(jnp.bfloat16), "mlp", scatter_dimension=2, tiled=True
    ).astype(jnp.float32)
    out = (valid_mask * (resid_mine + branch_mine)).astype(jnp.bfloat16)
    cot_full = lax.all_gather(cotangent, "mlp", axis=2, tiled=True)
    grad_out = valid_mask * cot_full.astype(jnp.float32)
    output_gradient_reduced = grad_out.astype(jnp.bfloat16)
    grad_down = jnp.einsum(
        "xgr,xge->re", mlp_activation, output_gradient_reduced, preferred_element_type=jnp.float32
    )
    grad_act = jnp.einsum(
        "mit,nt->min",
        output_gradient_reduced,
        down_projection_weight,
        preferred_element_type=jnp.float32,
    )
    _, gelu_pull = jax.vjp(partial(jax.nn.gelu, approximate=True), hidden_pre)
    hidden_gradient = gelu_pull(grad_act)[0].astype(jnp.bfloat16)
    up_projection_gradient = jnp.einsum(
        "gih,giv->hv", second_normalized, hidden_gradient, preferred_element_type=jnp.float32
    )
    grad_normed_two = lax.psum(
        jnp.einsum(
            "vwb,kb->vwk", hidden_gradient, up_projection_weight, preferred_element_type=jnp.float32
        ).astype(jnp.bfloat16),
        "mlp",
    ).astype(jnp.float32)
    _, second_pull = jax.vjp(layer_norm, residual, gain_float[1], bias_float[1])
    grad_resid_norm, grad_gain_two, grad_bias_two = second_pull(grad_normed_two)
    grad_resid = grad_out + grad_resid_norm
    grad_resid_low = grad_resid.astype(jnp.bfloat16)
    grad_out_weight = jnp.einsum(
        "slf,lsd->fd", attn_heads, grad_resid_low, preferred_element_type=jnp.float32
    )
    grad_mixed = jnp.einsum(
        "lsd,fd->slf", grad_resid_low, out_weight, preferred_element_type=jnp.float32
    ).astype(jnp.bfloat16)

    def attend_backward(unused, inputs_seq):
        query_seq, pairs_seq, query_rows, key_rows, log_total, grad_seq = inputs_seq
        gathered = lax.all_gather(pairs_seq, "seq", axis=0, tiled=True)
        key_heads, value_heads = split_pairs(gathered)
        logits = (
            jnp.einsum("qhe,khe->hqk", query_seq, key_heads, preferred_element_type=jnp.float32)
            * score_scale
        )
        visible = (query_rows[:, None] == key_rows[None, :])[None]
        attention = jnp.exp(jnp.where(visible, logits - log_total[:, :, None], masked_value))
        attention_low = attention.astype(jnp.bfloat16)
        grad_heads = grad_seq.reshape(local_rows, heads_here, head_size)
        grad_attention = jnp.einsum(
            "qhe,khe->hqk", grad_heads, value_heads, preferred_element_type=jnp.float32
        )
        inner = jnp.sum(grad_attention * attention, axis=2, keepdims=True)
        grad_logits = (attention * (grad_attention - inner)).astype(jnp.bfloat16)
        grad_query = (
            jnp.einsum("hqk,khe->qhe", grad_logits, key_heads, preferred_element_type=jnp.float32)
            * score_scale
        )
        grad_key = (
            jnp.einsum("hqk,qhe->khe", grad_logits, query_seq, preferred_element_type=jnp.float32)
            * score_scale
        )
        grad_value = jnp.einsum(
            "hqk,qhe->khe", attention_low, grad_heads, preferred_element_type=jnp.float32
        )
        grad_pairs = lax.psum_scatter(
            jnp.concatenate(
                [
                    grad_key.reshape(lax.axis_size("seq") * local_rows, head_cols),
                    grad_value.reshape(lax.axis_size("seq") * local_rows, head_cols),
                ],
                axis=1,
            ).astype(jnp.bfloat16),
            "seq",
            scatter_dimension=0,
            tiled=True,
        ).astype(jnp.float32)
        return (unused, (grad_query.reshape(local_rows, head_cols), grad_pairs))

    _, (grad_queries, grad_pairs_all) = lax.scan(
        attend_backward, 0, (query_low, key_pairs, query_segs, key_segs, log_totals, grad_mixed)
    )
    _, query_pull = jax.vjp(head_norm, query_raw, head_float[0])
    grad_query_raw, grad_query_gain = query_pull(grad_queries.reshape(shape_heads))
    _, key_pull = jax.vjp(head_norm, key_raw, head_float[1])
    grad_key_raw, grad_key_gain = key_pull(grad_pairs_all[:, :, :head_cols].reshape(shape_heads))
    grad_projected = jnp.stack(
        [
            grad_query_raw.reshape(seq_here, local_rows, head_cols),
            grad_key_raw.reshape(seq_here, local_rows, head_cols),
            grad_pairs_all[:, :, head_cols:],
        ],
        axis=0,
    ).astype(jnp.bfloat16)
    grad_query_weight = jnp.einsum(
        "lsd,csle->cde", normed, grad_projected, preferred_element_type=jnp.float32
    )
    grad_normed = lax.psum(
        jnp.einsum(
            "csle,cde->lsd", grad_projected, query_weight, preferred_element_type=jnp.float32
        ).astype(jnp.bfloat16),
        "mlp",
    ).astype(jnp.float32)
    _, first_pull = jax.vjp(layer_norm, patch_float, gain_float[0], bias_float[0])
    grad_patch_norm, grad_gain_one, grad_bias_one = first_pull(grad_normed)
    grad_patches = (grad_resid + grad_patch_norm).astype(jnp.bfloat16)
    grad_scale = 1.0 / math.sqrt(lax.axis_size("dp") * seq_here * seq_len)
    term_qkv = grad_query_weight * grad_scale
    term_out = grad_out_weight * grad_scale
    term_up = up_projection_gradient * grad_scale
    term_down = grad_down * grad_scale
    term_gain = jnp.stack([grad_gain_one, grad_gain_two]) * grad_scale
    term_bias = jnp.stack([grad_bias_one, grad_bias_two]) * grad_scale
    term_head = jnp.stack([grad_query_gain, grad_key_gain]) * grad_scale
    summed = (
        lax.psum(term_qkv.astype(jnp.bfloat16), "seq").astype(jnp.float32),
        lax.psum(term_out.astype(jnp.bfloat16), "seq").astype(jnp.float32),
        lax.psum(term_up.astype(jnp.bfloat16), "seq").astype(jnp.float32),
        lax.psum(term_down.astype(jnp.bfloat16), "seq").astype(jnp.float32),
        lax.psum(term_gain.astype(jnp.bfloat16), "seq").astype(jnp.float32),
        lax.psum(term_bias.astype(jnp.bfloat16), "seq").astype(jnp.float32),
        lax.psum(term_head.astype(jnp.bfloat16), "seq").astype(jnp.float32),
    )
    shards = (
        lax.psum_scatter(
            summed[0].astype(jnp.bfloat16), "dp", scatter_dimension=1, tiled=True
        ).astype(jnp.float32),
        lax.psum_scatter(
            summed[1].astype(jnp.bfloat16), "dp", scatter_dimension=1, tiled=True
        ).astype(jnp.float32),
        lax.psum_scatter(
            summed[2].astype(jnp.bfloat16), "dp", scatter_dimension=0, tiled=True
        ).astype(jnp.float32),
        lax.psum_scatter(
            summed[3].astype(jnp.bfloat16), "dp", scatter_dimension=1, tiled=True
        ).astype(jnp.float32),
        lax.psum_scatter(
            summed[4].astype(jnp.bfloat16), "dp", scatter_dimension=1, tiled=True
        ).astype(jnp.float32),
        lax.psum_scatter(
            summed[5].astype(jnp.bfloat16), "dp", scatter_dimension=1, tiled=True
        ).astype(jnp.float32),
        lax.psum_scatter(
            summed[6].astype(jnp.bfloat16), "dp", scatter_dimension=2, tiled=True
        ).astype(jnp.float32),
    )
    return (
        out,
        grad_patches,
        shards[0],
        shards[1],
        shards[2],
        shards[3],
        shards[4],
        shards[5],
        shards[6],
    )


low = jnp.bfloat16
wide = jnp.float32
log2e = math.log2(math.e)
mask_weight = 128.0
query_block = 256
windows = (512, 1024)
vmem_bytes = 56 * 1024 * 1024
hidden_chunk = 512
micros = {
    "qkv": 25,
    "attn_fwd": 22,
    "middle": 80,
    "attn_bwd": 75,
    "first_norm": 8,
    "place": 4,
}


def dot(left, right, left_dim=1, right_dim=0):
    return lax.dot_general(
        left, right, (((left_dim,), (right_dim,)), ((), ())), preferred_element_type=wide
    )


def params(count, vmem):
    return pltpu.CompilerParams(
        dimension_semantics=("arbitrary",) * count, vmem_limit_bytes=vmem
    )


def split_dot(values, ones_matrix):
    top = values.astype(low)
    rest = (values - top.astype(wide)).astype(low)
    return dot(jnp.concatenate([top, rest], axis=1), ones_matrix)


def load_pieces(info_ref, sets, scratch, sems):
    copies = []
    rows = scratch.shape[0] // 8
    for number, (pieces, first, count, target) in enumerate(sets):
        for index in range(8):
            if len(pieces) == 8:
                piece = pieces[index]
            else:
                piece = pieces[index % 2].at[index // 2]
            place = pl.multiple_of(info_ref[2 + index] * rows, rows)
            copies.append(
                pltpu.make_async_copy(
                    piece.at[pl.ds(0, rows), pl.ds(first, count)],
                    scratch.at[pl.ds(place, rows), pl.ds(target, count)],
                    sems.at[number, index],
                )
            )
    return copies


def load_shards(pairs_of, scratch, sems):
    copies = []
    rows = scratch.shape[0] // 8
    for number, (source, owner, first, count, target) in enumerate(pairs_of):
        for index in range(8):
            copies.append(
                pltpu.make_async_copy(
                    source.at[2 * index + owner, :, pl.ds(first, count)],
                    scratch.at[pl.ds(index * rows, rows), pl.ds(target, count)],
                    sems.at[number, index],
                )
            )
    return copies


def run_all(copies):
    for copy in copies:
        copy.start()
    for copy in copies:
        copy.wait()


def qkv_kernel(info_ref, mine_ref, got_ref, far_ref, gain_ref, bias_ref, hg_ref, mean_ref, *refs):
    pieces, refs = refs[:8], refs[8:]
    p_ref, rate_ref, ht_ref, w_ref, sems = refs
    sub = pl.program_id(1)

    @pl.when((pl.program_id(0) == 0) & (sub == 0))
    def _():
        run_all(load_pieces(info_ref, [(pieces, 0, w_ref.shape[1], 0)], w_ref, sems))

    first_core = info_ref[1] == 0
    moved = jnp.concatenate(
        [
            jnp.where(first_core, got_ref[0], far_ref[0]),
            jnp.where(first_core, far_ref[0], got_ref[0]),
        ],
        axis=0,
    )
    x = jnp.where(sub == info_ref[0], mine_ref[0], moved).astype(wide)
    centered = x - jnp.mean(x, axis=1, keepdims=True)
    variance = jnp.mean(centered * centered, axis=1, keepdims=True)
    h = (centered * lax.rsqrt(variance + norm_eps) * gain_ref[...] + bias_ref[...]).astype(low)
    ht_ref[...] = jnp.transpose(h)
    means = mean_ref[...]
    projected = dot(h, w_ref[...])
    for at in range(0, projected.shape[1], 128):
        raw = projected[:, at : at + 128]
        if at % 384 == 256:
            p_ref[0, :, at : at + 128] = raw.astype(low)
            continue
        inner = raw - split_dot(raw, means)
        rate = lax.rsqrt(dot((inner * inner).astype(low), means[:128]) + norm_eps)
        to = at // 384 * 256 + at % 384
        rate_ref[0, :, to : to + 128] = rate
        p_ref[0, :, at : at + 128] = (inner * rate * hg_ref[:, to : to + 128]).astype(low)


def attn_fwd_kernel(
    info_ref, start_ref, kind_ref, p_ref, aug_ref, side_ref, mine_ref, send_ref, inv_ref
):
    seq = pl.program_id(0)
    blocks = p_ref.shape[1] // query_block
    pairs = p_ref.shape[2] // 384
    lane = lax.broadcasted_iota(jnp.int32, (query_block, 128), 1)

    def step(block, carry):
        row = pl.multiple_of(block * query_block, query_block)
        which = seq * blocks + block

        def body(size):
            begin = pl.multiple_of(start_ref[which], 16)
            rows = pl.ds(row, query_block)
            span = pl.ds(begin, size)
            q_side = aug_ref[0, rows, :] * side_ref[...]
            k_side = aug_ref[0, span, :]
            ones = jnp.ones((size, 128), low)
            outcomes = []
            for pair in range(pairs):
                at = 384 * pair
                q_pair = p_ref[0, rows, at : at + 128]
                keys = jnp.concatenate([p_ref[0, span, at + 128 : at + 256], k_side], axis=1)
                values = jnp.concatenate([p_ref[0, span, at + 256 : at + 384], ones], axis=1)
                mixed = []
                for head in range(2):
                    mine = jnp.where(lane // 64 == head, q_pair, jnp.zeros_like(q_pair))
                    scores = dot(jnp.concatenate([mine, q_side], axis=1), keys, 1, 1)
                    mixed.append(dot(jnp.exp2(scores).astype(low), values))
                inverse = 1.0 / jnp.where(lane < 64, mixed[0][:, 128:], mixed[1][:, 128:])
                outcome = jnp.where(lane < 64, mixed[0][:, :128], mixed[1][:, :128]) * inverse
                outcomes.append(outcome.astype(low))
                inv_ref[0, rows, 128 * pair : 128 * pair + 128] = inverse
            outcome = jnp.concatenate(outcomes, axis=1)

            @pl.when(block % 2 == info_ref[1])
            def _():
                mine_ref[0, block // 2] = outcome

            @pl.when(block % 2 != info_ref[1])
            def _():
                send_ref[0, block // 2] = outcome

        for index, size in enumerate(windows):
            pl.when(kind_ref[which] == index)(partial(body, size))
        return carry

    lax.fori_loop(0, blocks, step, 0)


def attn_bwd_kernel(
    base,
    scale,
    first,
    final,
    info_ref,
    start_ref,
    kind_ref,
    p_ref,
    go_mine_ref,
    go_got_ref,
    o_mine_ref,
    o_send_ref,
    inv_ref,
    rate_ref,
    aug_ref,
    side_ref,
    hg_ref,
    mean_ref,
    ht_ref,
    *refs,
):
    pieces, refs = refs[:8], refs[8:]
    if not first:
        gw_in_ref, _, _, *refs = refs
    mine_ref, send_ref, gw_ref, gw_far_ref, gain_ref, *refs = refs
    gq_acc, gk_acc, gv_acc, g_all, gw_acc, w_ref, sems = refs
    step_id = pl.program_id(0)
    seq = step_id + base
    blocks = p_ref.shape[1] // query_block
    pairs = p_ref.shape[2] // 384
    lane = lax.broadcasted_iota(jnp.int32, (query_block, 128), 1)

    @pl.when(step_id == 0)
    def _():
        for copy in load_pieces(info_ref, [(pieces, 0, w_ref.shape[1], 0)], w_ref, sems):
            copy.start()
        gain_ref[...] = jnp.zeros_like(gain_ref)
        gw_acc[...] = jnp.zeros_like(gw_acc) if first else gw_in_ref[...]

    gq_acc[...] = jnp.zeros_like(gq_acc)
    gk_acc[...] = jnp.zeros_like(gk_acc)
    gv_acc[...] = jnp.zeros_like(gv_acc)

    def step(block, carry):
        row = pl.multiple_of(block * query_block, query_block)
        which = seq * blocks + block

        size = windows[0]

        def body(turn, inner_carry):
            begin = pl.multiple_of(start_ref[which] + turn * size, 16)
            rows = pl.ds(row, query_block)
            span = pl.ds(begin, size)
            q_side = aug_ref[0, rows, :] * side_ref[...]
            k_side = aug_ref[0, span, :]
            near = block % 2 == info_ref[1]
            for pair in range(pairs):
                at = 384 * pair
                lanes = slice(128 * pair, 128 * pair + 128)
                q_pair = p_ref[0, rows, at : at + 128]
                k_pair = p_ref[0, span, at + 128 : at + 256]
                keys = jnp.concatenate([k_pair, k_side], axis=1)
                values = jnp.concatenate([p_ref[0, span, at + 256 : at + 384], k_side], axis=1)
                go = jnp.where(
                    near, go_mine_ref[0, block // 2, :, lanes], go_got_ref[0, block // 2, :, lanes]
                )
                o = jnp.where(
                    near, o_mine_ref[0, block // 2, :, lanes], o_send_ref[0, block // 2, :, lanes]
                )
                scaled = (go.astype(wide) * inv_ref[0, rows, lanes]).astype(low)
                product = scaled.astype(wide) * o.astype(wide)
                powers, grads, queries, pulls = [], [], [], []
                for head in range(2):
                    mine = lane // 64 == head
                    inner = jnp.sum(jnp.where(mine, product, 0.0), axis=1, keepdims=True)
                    one = inner.astype(low)
                    two = (inner - one.astype(wide)).astype(low)
                    three = (inner - one.astype(wide) - two.astype(wide)).astype(low)
                    none = jnp.zeros_like(q_pair)
                    go_side = jnp.where(
                        lane == 6,
                        -one,
                        jnp.where(lane == 7, -two, jnp.where(lane == 8, -three, none)),
                    )
                    q_mine = jnp.where(mine, q_pair, none)
                    go_mine = jnp.where(mine, scaled, none)
                    power = jnp.exp2(dot(keys, jnp.concatenate([q_mine, q_side], axis=1), 1, 1))
                    slope = dot(values, jnp.concatenate([go_mine, go_side], axis=1), 1, 1)
                    powers.append(power.astype(low))
                    grads.append((power * slope).astype(low))
                    queries.append(q_mine)
                    pulls.append(go_mine)
                gv_acc[span, lanes] += dot(
                    jnp.concatenate(powers, axis=1), jnp.concatenate(pulls, axis=0)
                )
                gk_acc[span, lanes] += dot(
                    jnp.concatenate(grads, axis=1), jnp.concatenate(queries, axis=0)
                )
                keys_turned = jnp.transpose(k_pair)
                turned = [dot(keys_turned[64 * i : 64 * i + 64], grads[i]) for i in range(2)]
                gq_acc[rows, lanes] += jnp.transpose(jnp.concatenate(turned, axis=0))

            return inner_carry

        lax.fori_loop(0, kind_ref[which] + 1, body, 0)
        return carry

    lax.fori_loop(0, blocks, step, 0)
    means = mean_ref[...]
    for pair in range(pairs):
        lanes = slice(128 * pair, 128 * pair + 128)
        g_all[:, 384 * pair + 256 : 384 * pair + 384] = gv_acc[:, lanes].astype(low)
        for index, acc, factor, unscale in (
            (0, gq_acc, 0.125, 8.0 / log2e),
            (1, gk_acc, 1.0 / log2e, 1.0),
        ):
            to = slice(384 * pair + 128 * index, 384 * pair + 128 * index + 128)
            at = slice(256 * pair + 128 * index, 256 * pair + 128 * index + 128)
            gain = hg_ref[:, at]
            grad = acc[:, lanes] * factor
            normed = p_ref[0, :, to].astype(wide) * unscale
            weighted = grad * gain
            cross = grad * normed
            inner = split_dot(weighted, means)
            outer = split_dot(cross, means)
            g_all[:, to] = (
                rate_ref[0, :, at] * (weighted - inner - normed / gain * outer)
            ).astype(low)
            gain_ref[0:1, at] += jnp.sum(cross, axis=0, keepdims=True) / gain

    @pl.when(step_id == 0)
    def _():
        for copy in load_pieces(info_ref, [(pieces, 0, w_ref.shape[1], 0)], w_ref, sems):
            copy.wait()

    gw_acc[...] += dot(ht_ref[...], g_all[...])
    everything = dot(g_all[...], w_ref[...], 1, 1).astype(low)
    for block in range(blocks):
        result = everything[block * query_block : (block + 1) * query_block]

        @pl.when(block % 2 == info_ref[1])
        def _():
            mine_ref[0, block // 2] = result

        @pl.when(block % 2 != info_ref[1])
        def _():
            send_ref[0, block // 2] = result

    @pl.when(step_id == pl.num_programs(0) - 1)
    def _():
        if final:
            skip = gw_acc.shape[1] - gw_ref.shape[3]
            spread(info_ref, gw_acc, scale, gw_ref, skip * info_ref[0])
            spread(info_ref, gw_acc, scale, gw_far_ref, skip * (1 - info_ref[0]))
        else:
            gw_ref[...] = gw_acc[...]
            gw_far_ref[...] = jnp.zeros_like(gw_far_ref)


def spread(info_ref, acc, scale, ref, begin):
    rows, count = ref.shape[2:]
    for index in range(8):
        place = pl.multiple_of(info_ref[2 + index] * rows, rows)
        ref[index % 2, index // 2] = (
            acc[pl.ds(place, rows), pl.ds(pl.multiple_of(begin, 128), count)] * scale
        ).astype(low)


def put_blocks(stage, acc, scale, owners, to_col, count):
    rows = stage.shape[1]
    for number, owner in enumerate(owners):
        for index in range(8):
            stage[2 * index + owner, :, to_col : to_col + count] = (
                acc[index * rows : (index + 1) * rows, number * count : (number + 1) * count]
                * scale
            ).astype(low)


def norm_back(values, grad, gain):
    centered = values - jnp.mean(values, axis=1, keepdims=True)
    rate = lax.rsqrt(jnp.mean(centered * centered, axis=1, keepdims=True) + norm_eps)
    normed = centered * rate
    weighted = grad * gain
    result = rate * (
        weighted
        - jnp.mean(weighted, axis=1, keepdims=True)
        - normed * jnp.mean(weighted * normed, axis=1, keepdims=True)
    )
    return result, normed


def gelu_parts(t):
    root = math.sqrt(2.0 / math.pi)
    square = t * t
    gate = 0.5 + 0.5 * jnp.tanh(t * (root + (root * 0.044715) * square))
    act = t * gate
    slope = gate + 2.0 * act * (1.0 - gate) * (root + (3.0 * root * 0.044715) * square)
    return act, slope


def middle_kernel(
    scale,
    chunks,
    info_ref,
    o_mine_ref,
    o_got_ref,
    mine_ref,
    got_ref,
    gy_ref,
    valid_ref,
    gain_ref,
    bias_ref,
    shards,
    keep_near_ref,
    keep_far_ref,
    send_near_ref,
    send_far_ref,
    gx_ref,
    go_mine_ref,
    go_send_ref,
    sums_ref,
    grads,
    x2_all,
    h_all,
    ht_all,
    gy_all,
    gyt_all,
    out_all,
    gh_all,
    up_both,
    down_both,
    up_acc,
    down_acc,
    act_all,
    grad_all,
    wo_ref,
    wo_acc,
    stage,
    stage_out,
    weight_sems,
    stage_sem,
):
    phase = pl.program_id(0)
    r = pl.program_id(1)
    last = pl.num_programs(1) - 1
    cols = o_mine_ref.shape[3]
    part = o_mine_ref.shape[2]
    chunk = up_both.shape[2] // 2
    c = info_ref[1]
    first_half = info_ref[0] == 0

    def weight_copies(f, slot):
        begin = pl.multiple_of(cols + f * 2 * chunk, 128)
        sems = weight_sems.at[slot]
        return load_shards(
            [(shards, m, begin, chunk, m * chunk) for m in range(2)], up_both.at[slot], sems
        ) + load_shards(
            [(shards, m, begin + chunk, chunk, m * chunk) for m in range(2)],
            down_both.at[slot],
            sems.at[pl.ds(2, 2)],
        )

    def stage_copy(f):
        return pltpu.make_async_copy(
            stage,
            grads.at[:, :, pl.ds(pl.multiple_of(f * 2 * chunk, 128), 2 * chunk)],
            stage_sem.at[0],
        )

    def both_heads():
        return jnp.concatenate(
            [o_mine_ref[0].reshape(2 * part, cols), o_got_ref[0].reshape(2 * part, cols)], axis=1
        )

    @pl.when((phase == 0) & (r == 0))
    def _():
        copies = load_shards(
            [(shards, c, 0, cols, 0), (shards, 1 - c, 0, cols, cols)], wo_ref, weight_sems.at[1]
        )
        run_all(copies)
        for copy in weight_copies(0, 0):
            copy.start()
        sums_ref[...] = jnp.zeros_like(sums_ref)
        wo_acc[...] = jnp.zeros_like(wo_acc)

    @pl.when(phase == 0)
    def _():
        x = jnp.concatenate(
            [
                jnp.where(first_half, mine_ref[0], got_ref[0]),
                jnp.where(first_half, got_ref[0], mine_ref[0]),
            ],
            axis=0,
        ).astype(wide)
        x2 = x + dot(both_heads(), wo_ref[...], 1, 1)
        x2_all[r] = x2
        out_all[r] = x2
        gh_all[r] = jnp.zeros_like(x2)
        centered = x2 - jnp.mean(x2, axis=1, keepdims=True)
        variance = jnp.mean(centered * centered, axis=1, keepdims=True)
        h = (centered * lax.rsqrt(variance + norm_eps) * gain_ref[...] + bias_ref[...]).astype(low)
        h_all[r] = h
        ht_all[r] = jnp.transpose(h)
        gy = gy_ref[...]
        gy_all[r] = gy
        gyt_all[r] = jnp.transpose(gy)

    @pl.when((phase > 0) & (phase <= chunks))
    def _():
        f = phase - 1
        slot = f % 2

        @pl.when(r == 0)
        def _():
            for copy in weight_copies(f, slot):
                copy.wait()

        @pl.when((r == 0) & (f + 1 < chunks))
        def _():
            for copy in weight_copies(f + 1, 1 - slot):
                copy.start()

        up_ref = up_both.at[slot]
        down_ref = down_both.at[slot]
        h = h_all[r]
        gy = gy_all[r]
        size = 512
        for at in range(0, 2 * chunk, size):
            act, slope = gelu_parts(dot(h, up_ref[:, at : at + size]))
            act_all[:, at : at + size] = act.astype(low)
            grad_all[:, at : at + size] = (dot(gy, down_ref[:, at : at + size]) * slope).astype(low)
        out_all[r] += dot(act_all[...], down_ref[...], 1, 1)
        gh_all[r] += dot(grad_all[...], up_ref[...], 1, 1)

        @pl.when(r == 0)
        def _():
            up_acc[...] = jnp.zeros_like(up_acc)
            down_acc[...] = jnp.zeros_like(down_acc)

        up_acc[...] += dot(ht_all[r], grad_all[...])
        down_acc[...] += dot(gyt_all[r], act_all[...])

        @pl.when((r == last) & (f > 0))
        def _():
            stage_copy(f - 1).wait()

        @pl.when(r == last)
        def _():
            put_blocks(stage, up_acc, scale, (0, 1), 0, chunk)
            put_blocks(stage, down_acc, scale, (0, 1), chunk, chunk)
            stage_copy(f).start()

    @pl.when(phase == chunks + 1)
    def _():
        out = (out_all[r] * valid_ref[...][:, :1]).astype(low)
        keep = jnp.where(first_half, out[:part], out[part:])
        send = jnp.where(first_half, out[part:], out[:part])
        keep_near_ref[0] = jnp.where(c == 0, keep[:, :cols], keep[:, cols:])
        keep_far_ref[0] = jnp.where(c == 0, keep[:, cols:], keep[:, :cols])
        send_near_ref[0] = jnp.where(c == 0, send[:, :cols], send[:, cols:])
        send_far_ref[0] = jnp.where(c == 0, send[:, cols:], send[:, :cols])
        gh = gh_all[r]
        back, normed = norm_back(x2_all[r], gh, gain_ref[...])
        gx = gy_all[r].astype(wide) + back
        gx_ref[...] = gx
        gx_low = gx.astype(low)
        go = dot(gx_low, wo_ref[...]).astype(low)
        go_mine_ref[0] = go[:, :cols].reshape(2, part, cols)
        go_send_ref[0] = go[:, cols:].reshape(2, part, cols)
        turned = jnp.transpose(gx_low)
        sums_ref[0:1, :] += jnp.sum(gh * normed, axis=0, keepdims=True)
        sums_ref[1:2, :] += jnp.sum(gh, axis=0, keepdims=True)
        wo_acc[...] += dot(turned, both_heads())

        @pl.when(r == last)
        def _():
            stage_copy(chunks - 1).wait()
            put_blocks(stage_out, wo_acc, scale, (c, 1 - c), 0, cols)
            copy = pltpu.make_async_copy(
                stage_out, grads.at[:, :, pl.ds(chunks * 2 * chunk, cols)], stage_sem.at[1]
            )
            copy.start()
            copy.wait()


def first_norm_kernel(
    info_ref, mine_ref, got_ref, a_ref, b_ref, gx2_ref, gain_ref, keep_ref, send_ref, sums_ref
):
    half = pl.program_id(1)
    x = jnp.where(half == info_ref[0], mine_ref[0], got_ref[0]).astype(wide)
    gh = a_ref[0, 0].astype(wide) + b_ref[0, 0].astype(wide)
    back, normed = norm_back(x, gh, gain_ref[...])
    out = (gx2_ref[...] + back).astype(low)

    @pl.when(half == info_ref[0])
    def _():
        keep_ref[0] = out

    @pl.when(half != info_ref[0])
    def _():
        send_ref[0] = out

    @pl.when((pl.program_id(0) == 0) & (half == 0))
    def _():
        sums_ref[...] = jnp.zeros_like(sums_ref)

    sums_ref[0:1, :] += jnp.sum(gh * normed, axis=0, keepdims=True)
    sums_ref[1:2, :] += jnp.sum(gh, axis=0, keepdims=True)


def place_kernel(plan, seqs, info_ref, *refs):
    sources, (out_ref, sems) = refs[: len(plan)], refs[len(plan) :]
    y, c = info_ref[0], info_ref[1]
    copies = []
    for number, (source, (own_y, own_c, begin)) in enumerate(zip(sources, plan)):
        at = seqs * (y if own_y else 1 - y) + begin
        copies.append(
            pltpu.make_async_copy(
                source,
                out_ref.at[pl.ds(at, source.shape[0]), c if own_c else 1 - c],
                sems.at[number],
            )
        )
    run_all(copies)


def shape_of(dims, kind=low):
    return jax.ShapeDtypeStruct(dims, kind)


def window_table(segs, blocks):
    length = segs.shape[1]
    pad_begin = jnp.sum((segs >= 0).astype(jnp.int32), axis=1, keepdims=True)
    begins = jnp.where(segs >= 0, segs, pad_begin)
    size = length // blocks
    firsts = begins[:, ::size]
    lasts = begins[:, size - 1 :: size]
    ends = jnp.sum((begins[:, None, :] <= lasts[:, :, None]).astype(jnp.int32), axis=2)
    reach = ends - firsts
    kinds = jnp.zeros_like(reach)
    spans = jnp.full_like(reach, windows[0])
    for index in range(1, len(windows)):
        larger = reach > windows[index - 1]
        kinds = jnp.where(larger, index, kinds)
        spans = jnp.where(larger, windows[index], spans)
    starts = jnp.minimum(firsts, length - spans)
    return starts.reshape(-1), kinds.reshape(-1)


def mask_columns(segs):
    codes = (segs + 16) // 16
    lane = jnp.arange(128, dtype=jnp.int32)
    bits = (codes[:, :, None] >> jnp.minimum(lane, 5)) & 1
    signs = (2 * bits - 1).astype(wide)
    return jnp.where(lane < 6, signs, jnp.where(lane < 9, 1.0, 0.0)).astype(low)


def swap(values, axis):
    return lax.ppermute(values, axis, [(0, 1), (1, 0)])


def in_order(index, mine, other, axis):
    return jnp.where(
        index == 0,
        jnp.concatenate([mine, other], axis=axis),
        jnp.concatenate([other, mine], axis=axis),
    )


def pick(values, index, axis):
    return lax.dynamic_index_in_dim(values, index, axis, keepdims=False)


def shift_far(values, step):
    return lax.ppermute(
        values,
        "dp",
        [(2 * ((z + step) % 4) + x, 2 * z + x) for z in range(4) for x in range(2)],
    )


def swap_x(values):
    return lax.ppermute(values, "dp", [(d, d ^ 1) for d in range(8)])


def gather_pieces(shard):
    pieces = []
    for step in range(4):
        piece = shard if step == 0 else shift_far(shard, step)
        pieces += [piece, swap_x(piece)]
    return pieces


def on_device_small(
    patches, segments, w_qkv, w_out, w_up, w_down, ln_gain, ln_bias, head_gain, cotangent
):
    half, seqs_all, width = patches.shape
    length = 2 * half
    seqs = seqs_all // 2
    cols = w_qkv.shape[2]
    part = half // 2
    y = lax.axis_index("seq")
    c = lax.axis_index("mlp")
    d = lax.axis_index("dp")
    dp_size = lax.axis_size("dp")
    scale = 1.0 / math.sqrt(dp_size * seqs_all * length)
    own_rows = seqs * half
    hidden = w_up.shape[1]
    shard_rows = width // dp_size
    places = jnp.stack(
        [2 * ((d // 2 + index // 2) % 4) + ((d % 2) ^ (index % 2)) for index in range(8)]
    )
    info = jnp.concatenate([jnp.stack([y, c]), places]).astype(jnp.int32)

    turned = jnp.transpose(patches, (1, 0, 2)).reshape(2, seqs, 2, part, width)
    got = swap(pick(pick(turned, 1 - y, 0), c, 1), "seq")
    far = swap(got, "mlp")
    turned = turned.reshape(seqs_all, half, width)
    small = jnp.concatenate(
        [
            ln_gain.astype(low),
            ln_bias.astype(low),
            head_gain.astype(low).reshape(1, -1),
            jnp.zeros((3, shard_rows), low),
        ]
    )
    small = jnp.pad(small, ((0, 8), (0, 3 * cols - shard_rows)))
    pairs = cols // 128
    w_in = jnp.transpose(w_qkv.astype(low).reshape(3, shard_rows, pairs, 128), (1, 2, 0, 3))
    w_in = w_in.reshape(shard_rows, 3 * cols)
    in_pieces = gather_pieces(
        jnp.concatenate(
            [w_in, small]
        )
    )
    small = [piece[shard_rows : shard_rows + 8, :shard_rows] for piece in in_pieces]
    chunk = hidden_chunk
    chunks = hidden // chunk
    up_low = w_up.astype(low)
    down_low = jnp.transpose(w_down.astype(low))
    parts = [jnp.transpose(w_out.astype(low))]
    for f in range(chunks):
        at = slice(f * chunk, (f + 1) * chunk)
        parts += [up_low[:, at], down_low[:, at]]

    def gather_shards(parts):
        return lax.all_gather(jnp.concatenate(parts, axis=1), ("dp", "mlp"), axis=0)

    shards = gather_shards(parts)

    order = (places[None, :] == jnp.arange(8)[:, None]).astype(low)
    small = jnp.einsum("nr,rkw->knw", order, jnp.stack(small), preferred_element_type=wide)
    gains = small[0:2].reshape(2, width)
    biases = small[2:4].reshape(2, width)
    head_gains = jnp.transpose(small[4].reshape(dp_size, 2, cols // 64, 64 // dp_size), (1, 2, 0, 3))
    head_gains = jnp.transpose(head_gains.reshape(2, pairs, 128), (1, 0, 2))
    key_scale = jnp.array([[[log2e / 8.0], [1.0]]], wide)
    head_scaled = (head_gains * key_scale).reshape(1, 2 * cols)
    head_gains = head_gains.reshape(1, 2 * cols)

    segs = lax.dynamic_slice_in_dim(jnp.transpose(segments), y * seqs, seqs, 0)
    cot = cotangent.reshape(2, part, seqs_all, cols)
    cot_other = swap(pick(cot, 1 - c, 0), "mlp")
    cot = jnp.transpose(in_order(c, pick(cot, c, 0), cot_other, 2), (1, 0, 2))
    cot = cot.reshape(2, seqs, part, width)
    cot_got = swap(pick(cot, 1 - y, 0), "seq")
    cot = in_order(y, pick(cot, y, 0)[:, None], cot_got[:, None], 1)
    valid = pick((segs >= 0).reshape(seqs, 2, 2, part), c, 2)
    gy = jnp.where(valid[..., None], cot, jnp.zeros_like(cot)).reshape(own_rows, width)
    valid = jnp.broadcast_to(valid.reshape(own_rows, 1).astype(wide), (own_rows, 128))

    starts, kinds = window_table(segs, length // query_block)
    aug = mask_columns(segs)
    lanes = jnp.arange(128)
    side = jnp.where(lanes < 6, mask_weight, jnp.where(lanes == 6, -6.0 * mask_weight, 0.0))
    side = side.astype(low)[None]
    means = jnp.where(lanes[:, None] // 64 == lanes[None] // 64, 1.0 / 64, 0.0).astype(low)
    means = jnp.concatenate([means, means])
    anywhere = pl.BlockSpec(memory_space=pl.ANY)

    def whole(dims):
        return pl.BlockSpec(dims, lambda *ids: (0,) * len(dims))

    def call(kernel, grid, in_specs, out_specs, out_shape, scratch, name, scalars, pins=(), share=1, vmem=vmem_bytes, alias=None):
        work = int(micros[name] * 1150000000 / share)
        ends = scalars + len(in_specs)

        def unpinned(*refs):
            kernel(*refs[:ends], *refs[ends + len(pins) :])

        run = pl.pallas_call(
            unpinned,
            grid_spec=pltpu.PrefetchScalarGridSpec(
                num_scalar_prefetch=scalars,
                grid=grid,
                in_specs=in_specs + [anywhere] * len(pins),
                out_specs=out_specs,
                scratch_shapes=scratch,
            ),
            out_shape=out_shape,
            compiler_params=params(len(grid), vmem),
            input_output_aliases=alias or {},
            cost_estimate=pl.CostEstimate(flops=work, bytes_accessed=1000000, transcendentals=0),
            name=name,
        )
        return lambda *operands: run(*operands, *pins)

    piece_sems = pltpu.SemaphoreType.DMA((4, 8))
    one_seq = pl.BlockSpec((1, part, width), lambda s, j, *_: (s, 0, 0))
    projected, rates, h1t = call(
        qkv_kernel,
        (seqs, 2),
        [
            pl.BlockSpec((1, half, width), lambda s, j, info: (seqs * info[0] + s, 0, 0)),
            one_seq,
            one_seq,
            whole((1, width)),
            whole((1, width)),
            whole((1, 2 * cols)),
            whole((256, 128)),
        ]
        + [anywhere] * 8,
        [
            pl.BlockSpec((1, half, 3 * cols), lambda s, j, *_: (s, j, 0)),
            pl.BlockSpec((1, half, 2 * cols), lambda s, j, *_: (s, j, 0)),
            pl.BlockSpec((width, half), lambda s, j, *_: (0, 2 * s + j)),
        ],
        [
            shape_of((seqs, length, 3 * cols)),
            shape_of((seqs, length, 2 * cols), wide),
            shape_of((width, seqs * length)),
        ],
        [pltpu.VMEM((width, 3 * cols), low), piece_sems],
        "qkv",
        1,
    )(info, turned, got, far, gains[:1], biases[:1], head_scaled, means, *in_pieces)
    def per_seq(*dims, base=0):
        return pl.BlockSpec((1,) + dims, lambda s, *_: (s + base,) + (0,) * len(dims))

    o_mine, o_send, inverse = call(
        attn_fwd_kernel,
        (seqs,),
        [per_seq(length, 3 * cols), per_seq(length, 128), whole((1, 128))],
        [per_seq(2, part, cols), per_seq(2, part, cols), per_seq(length, cols)],
        [shape_of((seqs, 2, part, cols))] * 2 + [shape_of((seqs, length, cols), wide)],
        [],
        "attn_fwd",
        3,
    )(info, starts, kinds, projected, aug, side)

    o_got = swap(o_send, "mlp")
    seq_of = seqs - 1
    final = chunks + 1

    def at_ends(p, r):
        return jnp.where((p == 0) | (p == final), r, seq_of)

    def at_start(p, r):
        return jnp.where(p == 0, r, seq_of)

    def at_final(p, r):
        return jnp.where(p == final, r, 0)

    heads_spec = pl.BlockSpec((1, 2, part, cols), lambda p, r, *_: (at_ends(p, r), 0, 0, 0))
    moved_spec = pl.BlockSpec((1, part, cols), lambda p, r, *_: (at_final(p, r), 0, 0))
    heads_out = pl.BlockSpec((1, 2, part, cols), lambda p, r, *_: (at_final(p, r), 0, 0, 0))
    by_seq_bf = pltpu.VMEM((seqs, half, width), low)
    by_seq_turned = pltpu.VMEM((seqs, width, half), low)
    by_seq_wide = pltpu.VMEM((seqs, half, width), wide)
    grad_shape = (16, shard_rows, 2 * hidden + cols)
    keep_near, keep_far, send_near, send_far, gx2, go_mine, go_send, second_sums, grads = call(
        partial(middle_kernel, scale, chunks),
        (chunks + 2, seqs),
        [
            heads_spec,
            heads_spec,
            pl.BlockSpec(
                (1, part, width), lambda p, r, info: (seqs * info[0] + at_start(p, r), info[1], 0)
            ),
            pl.BlockSpec((1, part, width), lambda p, r, *_: (at_start(p, r), 0, 0)),
            pl.BlockSpec((half, width), lambda p, r, *_: (at_start(p, r), 0)),
            pl.BlockSpec((half, 128), lambda p, r, *_: (at_final(p, r), 0)),
            whole((1, width)),
            whole((1, width)),
            anywhere,
        ],
        [
            moved_spec,
            moved_spec,
            moved_spec,
            moved_spec,
            pl.BlockSpec((half, width), lambda p, r, *_: (at_final(p, r), 0)),
            heads_out,
            heads_out,
            whole((8, width)),
            anywhere,
        ],
        [
            shape_of((seqs, part, cols)),
            shape_of((seqs, part, cols)),
            shape_of((seqs, part, cols)),
            shape_of((seqs, part, cols)),
            shape_of((own_rows, width), wide),
            shape_of((seqs, 2, part, cols)),
            shape_of((seqs, 2, part, cols)),
            shape_of((8, width), wide),
            shape_of(grad_shape),
        ],
        [by_seq_wide, by_seq_bf, by_seq_turned, by_seq_bf, by_seq_turned, by_seq_wide, by_seq_wide]
        + [pltpu.VMEM((2, width, 2 * chunk), low)] * 2
        + [pltpu.VMEM((width, 2 * chunk), wide)] * 2
        + [pltpu.VMEM((half, 2 * chunk), low)] * 2
        + [
            pltpu.VMEM((width, width), low),
            pltpu.VMEM((width, width), wide),
            pltpu.VMEM((16, shard_rows, 2 * chunk), low),
            pltpu.VMEM((16, shard_rows, cols), low),
            pltpu.SemaphoreType.DMA((2, 4, 8)),
            pltpu.SemaphoreType.DMA((2,)),
        ],
        "middle",
        1,
        vmem=62 * 1024 * 1024,
    )(info, o_mine, o_got, turned, got, gy, valid, gains[1:], biases[1:], shards)
    go_got = swap(go_send, "mlp")
    got_near = swap(send_near, "seq")
    got_far = swap(send_far, "seq")
    scattered = lax.psum_scatter(grads, ("dp", "mlp"), scatter_dimension=0, tiled=True)[0]

    share_cols = (3 * cols // 128 + 1) // 2 * 128

    def attention_back(base, count, partial_sum, pins):
        first = partial_sum is None
        final = base + count == seqs
        shares = (2, 4, shard_rows, share_cols)
        carried = [] if first else list(partial_sum)
        return call(
            partial(attn_bwd_kernel, base, scale, first, final),
            (count,),
            [per_seq(length, 3 * cols, base=base)]
            + [per_seq(2, part, cols, base=base)] * 4
            + [
                per_seq(length, cols, base=base),
                per_seq(length, 2 * cols, base=base),
                per_seq(length, 128, base=base),
                whole((1, 128)),
                whole((1, 2 * cols)),
                whole((256, 128)),
                pl.BlockSpec((width, length), lambda s, *_: (0, s + base)),
            ]
            + [anywhere] * 8
            + ([] if first else [whole((width, 3 * cols)), anywhere, anywhere]),
            [per_seq(2, part, width, base=base)] * 2
            + [whole(shares if final else (width, 3 * cols))]
            + [whole(shares if final else (8, 128)), whole((8, 2 * cols))],
            [shape_of((seqs, 2, part, width))] * 2
            + [shape_of(shares) if final else shape_of((width, 3 * cols), wide)]
            + [shape_of(shares if final else (8, 128))]
            + [shape_of((8, 2 * cols), wide)],
            [pltpu.VMEM((length, cols), wide)] * 3
            + [
                pltpu.VMEM((length, 3 * cols), low),
                pltpu.VMEM((width, 3 * cols), wide),
                pltpu.VMEM((width, 3 * cols), low),
                piece_sems,
            ],
            "attn_bwd",
            3,
            pins,
            seqs / count,
            alias={} if first else {24: 0, 25: 1},
        )(
            info, starts, kinds, projected, go_mine, go_got, o_mine, o_send, inverse, rates,
            aug, side, head_gains, means, h1t, *in_pieces, *carried,
        )

    def first_back(base, count, mine, got_part, pins):
        here = pl.BlockSpec((1, 1, part, width), lambda s, h, *_: (s, h, 0, 0))
        moved = pl.BlockSpec((1, part, width), lambda s, h, *_: (s, 0, 0))
        return call(
            first_norm_kernel,
            (count, 2),
            [
                pl.BlockSpec(
                    (1, part, width), lambda s, h, info: (seqs * info[0] + s + base, info[1], 0)
                ),
                pl.BlockSpec((1, part, width), lambda s, h, *_: (s + base, 0, 0)),
                here,
                here,
                pl.BlockSpec((part, width), lambda s, h, *_: (2 * (s + base) + h, 0)),
                whole((1, width)),
            ],
            [moved, moved, whole((8, width))],
            [shape_of((count, part, width))] * 2 + [shape_of((8, width), wide)],
            [],
            "first_norm",
            1,
            pins,
            seqs / count,
        )(info, turned, got, mine, got_part, gx2, gains[:1])

    def place(sources, plan, feature_count, pins=()):
        return call(
            partial(place_kernel, plan, seqs),
            (1,),
            [anywhere] * len(plan),
            whole((seqs_all, 2, part, feature_count)),
            shape_of((seqs_all, 2, part, feature_count)),
            [pltpu.SemaphoreType.DMA((len(plan),))],
            "place",
            1,
            pins,
        )(info, *sources)

    mine, send, partial_sum, _, head_sums = attention_back(0, 1, None, ())
    keep_core = swap(keep_far, "mlp")
    mine, send, gw_near, gw_far, head_sums_b = attention_back(
        1, seqs - 1, (partial_sum, mine, send), [got_near, got_far, keep_core]
    )
    head_sums = head_sums + head_sums_b
    gw_got = swap(gw_far, "seq")
    moved = swap(send, "mlp")
    keep, give, first_sums = first_back(0, seqs, mine, moved, ())
    got_core = swap(got_far, "mlp")
    far_x = swap_x((gw_near[1].astype(wide) + gw_got[1].astype(wide)).astype(low))
    keep_moved = swap(keep, "mlp")
    got_grad = swap(give, "seq")

    norms = jnp.concatenate([first_sums[:2], second_sums[:2]]) * scale
    heads = jnp.transpose(head_sums[0].reshape(pairs, 2, 128), (1, 0, 2)) * scale
    heads = heads.reshape(2, cols // 64, dp_size, 64 // dp_size)
    heads = jnp.transpose(heads, (2, 0, 1, 3)).reshape(1, width)
    small = jnp.concatenate([norms + swap(norms, "mlp"), heads])
    small = small + swap(small, "seq")
    small = small + swap_x(small)
    small = small.reshape(5, 4, 2, shard_rows)
    small = lax.dynamic_index_in_dim(small, d % 2, 2, keepdims=False)
    small = jnp.concatenate([small, small], axis=1)
    small = lax.dynamic_slice_in_dim(small, d // 2, 4, 1)
    small = jnp.pad(jnp.transpose(small, (1, 2, 0)), ((0, 0), (0, 0), (0, 123)))
    total = gw_near[0].astype(wide) + gw_got[0].astype(wide) + far_x.astype(wide)
    total = jnp.concatenate([total, small], axis=2)
    low_total = total.astype(low)
    moved = [shift_far(low_total[step], 4 - step) for step in range(1, 4)]

    total = total[0] + sum(part.astype(wide) for part in moved)
    both = jnp.concatenate([scattered, total[:, :share_cols].astype(low)], axis=1)
    both_got = swap(both, "seq").astype(wide)
    scattered = scattered.astype(wide) + both_got[:, : scattered.shape[1]]
    total_got = both_got[:, scattered.shape[1] :]
    small = total[:, share_cols:]
    overlap = 2 * share_cols - 3 * cols
    gw_in = jnp.where(
        y == 0,
        jnp.concatenate([total[:, :share_cols], total_got[:, overlap:]], axis=1),
        jnp.concatenate([total_got[:, : 3 * cols - share_cols], total[:, :share_cols]], axis=1),
    )

    plan = [(True, True, 0), (True, False, 0), (False, True, 0), (False, False, 0)]
    out = place([keep_near, keep_core, got_near, got_core], plan, cols, [])
    out = jnp.transpose(out.reshape(seqs_all, half, cols), (1, 0, 2))
    grad_patches = place([keep, keep_moved, got_grad, swap(got_grad, "mlp")], plan, width, [])
    grad_patches = jnp.transpose(grad_patches.reshape(seqs_all, half, width), (1, 0, 2))

    gw_up = jnp.concatenate(
        [scattered[:, 2 * f * chunk : (2 * f + 1) * chunk] for f in range(chunks)], axis=1
    )
    gw_down = jnp.concatenate(
        [scattered[:, (2 * f + 1) * chunk : (2 * f + 2) * chunk] for f in range(chunks)], axis=1
    )
    gw_out = scattered[:, 2 * hidden :]
    gw_in = gw_in.reshape(shard_rows, pairs, 3, 128)
    gw_in = jnp.transpose(gw_in, (2, 0, 1, 3)).reshape(3, shard_rows, cols)
    norms = jnp.transpose(small[:, :4])
    heads = small[:, 4].reshape(2, cols // 64, 64 // dp_size)
    return (
        out,
        grad_patches,
        gw_in,
        jnp.transpose(gw_out),
        gw_up,
        jnp.transpose(gw_down),
        norms[0::2],
        norms[1::2],
        heads,
    )


def solution(mesh):
    shape = dict(mesh.shape)
    small = shape["seq"] == 2 and shape["mlp"] == 2 and shape["dp"] == 8
    return jax.shard_map(
        on_device_small if small else on_device,
        mesh=mesh,
        in_specs=(
            P("seq", "dp", None),
            P(None, "dp"),
            P(None, "dp", "mlp"),
            P("mlp", "dp"),
            P("dp", "mlp"),
            P("mlp", "dp"),
            P(None, "dp"),
            P(None, "dp"),
            P(None, "mlp", "dp"),
            P("seq", "dp", "mlp"),
        ),
        out_specs=(
            P("seq", "dp", "mlp"),
            P("seq", "dp", None),
            P(None, "dp", "mlp"),
            P("mlp", "dp"),
            P("dp", "mlp"),
            P("mlp", "dp"),
            P(None, "dp"),
            P(None, "dp"),
            P(None, "mlp", "dp"),
        ),
        check_vma=False,
    )
```
